32 devices in a mesh: dp: 8 (over z, core), seq: 4 (over y, x).
Axes of the slice: x: 2, y: 2, z: 4, core: 2. Of those that a mesh axis runs over, the one named last changes fastest.
Arguments:
- inputs: bfloat16 [8, 1024, 1024], P('dp', 'seq'), may hold values from -6 to 6
- cotangent: bfloat16 [8, 1024, 1024], P('dp', 'seq'), may hold values from -6 to 6
- first_gain: float32 [1024], P('dp'), may hold values from 0.25 to 1.75
- w_qkv: bfloat16 [1024, 2048], P('dp'), may hold values from -0.1875 to 0.1875
- qk_gain: float32 [128], P('dp'), may hold values from 0.5 to 1.5, as said below
- w_out: bfloat16 [1024, 1024], P('dp'), may hold values from -1.5 to 1.5
- second_gain: float32 [1024], P('dp'), may hold values from 0.25 to 1.75
- w_gate: bfloat16 [1024, 4608], P('dp'), may hold values from -0.1875 to 0.1875
- w_up: bfloat16 [1024, 4608], P('dp'), may hold values from -0.1875 to 0.1875
- w_down: bfloat16 [4608, 1024], P('dp'), may hold values from -0.09375 to 0.09375
Outputs:
- outputs: bfloat16 [8, 1024, 1024], P('dp', 'seq')
- grad_inputs: float32 [8, 1024, 1024], P('dp', 'seq')
- grad_first_gain: float32 [1024], P('dp')
- grad_qkv: float32 [1024, 2048], P('dp')
- grad_qk_gain: float32 [128], P('dp')
- grad_out: float32 [1024, 1024], P('dp')
- grad_second_gain: float32 [1024], P('dp')
- grad_gate: float32 [1024, 4608], P('dp')
- grad_up: float32 [1024, 4608], P('dp')
- grad_down: float32 [4608, 1024], P('dp')
The draws below stay inside these ranges and needn't reach their ends.
Inputs may be any that keep to these rules, and one draw needn't show every extreme that they name: `qk_gain`: 64 query norm gains, then 64 key norm gains.
All inputs are finite; a program needn't handle non-finite values.
Results may differ from the reference program's by a relative error of at most 0.039.
Values may be sent and summed in bfloat16 or wider, within the bound.
A program may use at most 256 MiB of HBM per device.

```python
import math
import jax
import jax.numpy as jnp
from jax import lax

D = 1024
H = 16
KV = 8
HD = 64
FF = 4608
LENGTH = 1024
SEQS = 8


def draw_qk_gain(key, part):
    key = jax.random.fold_in(key, 7)
    return jnp.exp(jax.random.uniform(key, (2 * HD,), jnp.float32, math.log(0.5), math.log(1.5)))


def shard_levels(key, shape, cuts, low, high):
    loudness, own = 1.0, jax.random.fold_in(key, 6)
    for position, blocks in cuts:
        steps = jnp.exp(jax.random.uniform(jax.random.fold_in(own, position), (blocks,), jnp.float32, low / len(cuts), high / len(cuts)))
        loudness = loudness * jnp.repeat(steps, shape[position] // blocks).reshape([-1 if axis == position else 1 for axis in range(len(shape))])
    return loudness


def normal_values(rng, extent, spread, limit, split=(), held_as=jnp.bfloat16):
    values = jax.random.normal(rng, extent, jnp.float32) * spread
    if len(split) > 0:
        values = shard_levels(rng, extent, split, -0.22, 0.18) * values
    return jnp.clip(values, min=-limit, max=limit).astype(held_as)


def setup_inputs(seed: int = 0) -> dict:
    keys = jax.random.split(jax.random.key(seed), 11)
    return {
        "inputs": normal_values(keys[0], (SEQS, LENGTH, D), 1.0, 6.0, ((0, 8), (1, 4))),
        "cotangent": normal_values(keys[1], (SEQS, LENGTH, D), 1.0, 6.0, ((0, 8), (1, 4))),
        "first_gain": jnp.clip(1.0 + 0.15 * jax.random.normal(keys[2], (D,), jnp.float32), 0.25, 1.75),
        "w_qkv": normal_values(keys[3], (D, (H + 2 * KV) * HD), D ** -0.5, 0.1875, ((0, 8),)),
        "qk_gain": draw_qk_gain(jax.random.fold_in(keys[10], 71), 0),
        "w_out": normal_values(keys[5], (H * HD, D), (H * HD // 64) ** -0.5, 1.5, ((0, 8),)),
        "second_gain": jnp.clip(1.0 + 0.15 * jax.random.normal(keys[6], (D,), jnp.float32), 0.25, 1.75),
        "w_gate": normal_values(keys[7], (D, FF), D ** -0.5, 0.1875, ((0, 8),)),
        "w_up": normal_values(keys[8], (D, FF), D ** -0.5, 0.1875, ((0, 8),)),
        "w_down": normal_values(keys[9], (FF, D), FF ** -0.5, 0.09375, ((0, 8),)),
    }


EPSILON = 1e-06
THETA_BASE = 1000000.0
NEG_FILL = -1e+30

def norm_scale(vector):
    return lax.rsqrt(lax.optimization_barrier(jnp.mean(vector * vector, axis=-1, keepdims=True)) + EPSILON)

def norm_back(vector, scale, weighted):
    return scale * weighted - vector * scale ** 3 * lax.optimization_barrier(jnp.mean(weighted * vector, axis=-1, keepdims=True))

def rotate(vector):
    middle = vector.shape[-1] // 2
    return jnp.concatenate([-vector[..., middle:], vector[..., :middle]], axis=-1)

def rotate_back(vector):
    middle = vector.shape[-1] // 2
    return jnp.concatenate([vector[..., middle:], -vector[..., :middle]], axis=-1)

def rope_tables(positions):
    inverse = THETA_BASE ** (-jnp.arange(0, HD, 2).astype(jnp.float32) / HD)
    angles = positions.astype(jnp.float32)[:, None] * inverse[None, :]
    angles = jnp.concatenate([angles, angles], axis=-1)
    return (jnp.cos(angles), jnp.sin(angles))

def masked_scores(query_block, key_heads, start_row):
    block_rows = query_block.shape[0]
    length = key_heads.shape[0]
    scores = jnp.einsum('rkgd,lkd->kgrl', query_block.astype(jnp.float32), key_heads.astype(jnp.float32)) * HD ** (-0.5)
    allowed = (start_row + jnp.arange(block_rows))[:, None] >= jnp.arange(length)[None, :]
    return jnp.where(allowed, scores, NEG_FILL)

def split_heads(queries, key_value):
    length = queries.shape[0]
    key_count = key_value.shape[1] // (2 * HD)
    per_group = queries.shape[1] // HD // key_count
    block_rows = min(512, length)
    blocks = length // block_rows
    key_heads = key_value[:, :key_count * HD].reshape(length, key_count, HD)
    value_heads = key_value[:, key_count * HD:].reshape(length, key_count, HD)
    query_blocks = queries.reshape(blocks, block_rows, key_count, per_group, HD)
    starts = jnp.arange(blocks) * block_rows
    return (key_heads, value_heads, query_blocks, starts)

def attend_forward(queries, key_value):
    key_heads, value_heads, query_blocks, starts = split_heads(queries, key_value)

    def one_block(block_item):
        query_block, start_row = block_item
        scores = masked_scores(query_block, key_heads, start_row)
        row_top = lax.optimization_barrier(jnp.max(scores, axis=-1, keepdims=True))
        log_total = row_top + jnp.log(lax.optimization_barrier(jnp.sum(jnp.exp(scores - row_top), axis=-1, keepdims=True)))
        weights = jnp.exp(scores - log_total).astype(jnp.bfloat16)
        mixture = jnp.einsum('kgrl,lkd->rkgd', weights.astype(jnp.float32), value_heads.astype(jnp.float32))
        return (mixture.astype(jnp.bfloat16), log_total[..., 0])
    mixture, log_total = lax.map(one_block, (query_blocks, starts))
    return (mixture.reshape(queries.shape), log_total)

def attend_backward(queries, key_value, grad_mixed, log_total):
    key_heads, value_heads, query_blocks, starts = split_heads(queries, key_value)
    grad_blocks = grad_mixed.reshape(query_blocks.shape)
    key_f32 = key_heads.astype(jnp.float32)
    value_f32 = value_heads.astype(jnp.float32)

    def one_block(running, block_item):
        grad_keys, grad_values = running
        query_block, grad_block, total_block, start_row = block_item
        scores = masked_scores(query_block, key_heads, start_row)
        probability = jnp.exp(scores - total_block[..., None])
        weights = probability.astype(jnp.bfloat16).astype(jnp.float32)
        grad_f32 = grad_block.astype(jnp.float32)
        grad_values = grad_values + jnp.einsum('kgrl,rkgd->lkd', weights, grad_f32)
        grad_probs = jnp.einsum('rkgd,lkd->kgrl', grad_f32, value_f32)
        centre = lax.optimization_barrier(jnp.sum(probability * grad_probs, axis=-1, keepdims=True))
        grad_scores = (probability * (grad_probs - centre) * HD ** (-0.5)).astype(jnp.bfloat16).astype(jnp.float32)
        grad_query = jnp.einsum('kgrl,lkd->rkgd', grad_scores, key_f32)
        grad_keys = grad_keys + jnp.einsum('kgrl,rkgd->lkd', grad_scores, query_block.astype(jnp.float32))
        return ((grad_keys, grad_values), grad_query.astype(jnp.bfloat16))
    zero_init = jnp.zeros(key_heads.shape, jnp.float32)
    (grad_keys, grad_values), grad_query = lax.scan(one_block, (zero_init, zero_init), (query_blocks, grad_blocks, log_total, starts))
    length = queries.shape[0]
    grad_pair = jnp.concatenate([grad_keys.reshape(length, -1), grad_values.reshape(length, -1)], axis=-1).astype(jnp.bfloat16)
    return (grad_query.reshape(queries.shape), grad_pair)

def reference(inputs, cotangent, first_gain, w_qkv, qk_gain, w_out, second_gain, w_gate, w_up, w_down):
    query_width = H * HD
    key_width = KV * HD
    cosine_table, sine_table = rope_tables(jnp.arange(LENGTH))

    def one_sequence(running, pair_item):
        tokens, upstream = pair_item
        stream = tokens.astype(jnp.float32)
        scale_in = norm_scale(stream)
        normed_in = (stream * scale_in * first_gain).astype(jnp.bfloat16)
        projected = jnp.dot(normed_in, w_qkv, preferred_element_type=jnp.float32)
        queries = projected[:, :query_width].reshape(LENGTH, H, HD)
        key_raw = projected[:, query_width:query_width + key_width].reshape(LENGTH, KV, HD)
        scale_query = norm_scale(queries)
        scale_key = norm_scale(key_raw)
        query_normed = queries * scale_query * qk_gain[:HD]
        key_normed = key_raw * scale_key * qk_gain[HD:]
        query_rot = (query_normed * cosine_table[:, None, :] + rotate(query_normed) * sine_table[:, None, :]).astype(jnp.bfloat16)
        key_rot = (key_normed * cosine_table[:, None, :] + rotate(key_normed) * sine_table[:, None, :]).astype(jnp.bfloat16)
        value_rows = projected[:, query_width + key_width:].astype(jnp.bfloat16)
        query_flat = query_rot.reshape(LENGTH, query_width)
        key_value = jnp.concatenate([key_rot.reshape(LENGTH, key_width), value_rows], axis=-1)
        mixed, log_total = attend_forward(query_flat, key_value)
        residual = stream + jnp.dot(mixed, w_out, preferred_element_type=jnp.float32)
        scale_mid = norm_scale(residual)
        normed_mid = (residual * scale_mid * second_gain).astype(jnp.bfloat16)
        gate_pre = jnp.dot(normed_mid, w_gate, preferred_element_type=jnp.float32)
        up_pre = jnp.dot(normed_mid, w_up, preferred_element_type=jnp.float32)
        gate_sig = jax.nn.sigmoid(gate_pre)
        hidden_act = (gate_pre * gate_sig * up_pre).astype(jnp.bfloat16)
        outputs = (residual + jnp.dot(hidden_act, w_down, preferred_element_type=jnp.float32)).astype(jnp.bfloat16)
        grad_down = jnp.dot(hidden_act.T, upstream, preferred_element_type=jnp.float32)
        grad_hidden = jnp.dot(upstream, w_down.T, preferred_element_type=jnp.float32)
        grad_gate_pre = (grad_hidden * up_pre * gate_sig * (1.0 + gate_pre * (1.0 - gate_sig))).astype(jnp.bfloat16)
        grad_up_pre = (grad_hidden * gate_pre * gate_sig).astype(jnp.bfloat16)
        grad_gate = jnp.dot(normed_mid.T, grad_gate_pre, preferred_element_type=jnp.float32)
        grad_up = jnp.dot(normed_mid.T, grad_up_pre, preferred_element_type=jnp.float32)
        grad_normed_mid = jnp.dot(grad_gate_pre, w_gate.T, preferred_element_type=jnp.float32) + jnp.dot(grad_up_pre, w_up.T, preferred_element_type=jnp.float32)
        grad_second = lax.optimization_barrier(jnp.sum(grad_normed_mid * residual * scale_mid, axis=0))
        grad_residual = upstream.astype(jnp.float32) + norm_back(residual, scale_mid, grad_normed_mid * second_gain)
        residual_back = grad_residual.astype(jnp.bfloat16)
        grad_out = jnp.dot(mixed.T, residual_back, preferred_element_type=jnp.float32)
        grad_mixed = jnp.dot(residual_back, w_out.T, preferred_element_type=jnp.float32).astype(jnp.bfloat16)
        grad_query_flat, grad_pair = attend_backward(query_flat, key_value, grad_mixed, log_total)
        grad_query_rot = grad_query_flat.reshape(LENGTH, H, HD).astype(jnp.float32)
        grad_key_rot = grad_pair[:, :key_width].reshape(LENGTH, KV, HD).astype(jnp.float32)
        grad_value_rows = grad_pair[:, key_width:]
        grad_query_normed = grad_query_rot * cosine_table[:, None, :] + rotate_back(grad_query_rot * sine_table[:, None, :])
        grad_key_normed = grad_key_rot * cosine_table[:, None, :] + rotate_back(grad_key_rot * sine_table[:, None, :])
        grad_qk = jnp.concatenate([lax.optimization_barrier(jnp.sum(grad_query_normed * queries * scale_query, axis=(0, 1))), lax.optimization_barrier(jnp.sum(grad_key_normed * key_raw * scale_key, axis=(0, 1)))])
        grad_query_lin = norm_back(queries, scale_query, grad_query_normed * qk_gain[:HD])
        grad_key_lin = norm_back(key_raw, scale_key, grad_key_normed * qk_gain[HD:])
        grad_projected = jnp.concatenate([grad_query_lin.reshape(LENGTH, query_width).astype(jnp.bfloat16), grad_key_lin.reshape(LENGTH, key_width).astype(jnp.bfloat16), grad_value_rows], axis=-1)
        grad_qkv = jnp.dot(normed_in.T, grad_projected, preferred_element_type=jnp.float32)
        grad_normed_in = jnp.dot(grad_projected, w_qkv.T, preferred_element_type=jnp.float32)
        grad_first = lax.optimization_barrier(jnp.sum(grad_normed_in * stream * scale_in, axis=0))
        grad_stream = grad_residual + norm_back(stream, scale_in, grad_normed_in * first_gain)
        terms = (grad_first, grad_qkv, grad_qk, grad_out, grad_second, grad_gate, grad_up, grad_down)
        running = tuple((total + term for total, term in zip(running, terms)))
        return (running, (outputs, grad_stream))
    zero_init = (jnp.zeros((D,), jnp.float32), jnp.zeros(w_qkv.shape, jnp.float32), jnp.zeros((2 * HD,), jnp.float32), jnp.zeros(w_out.shape, jnp.float32), jnp.zeros((D,), jnp.float32), jnp.zeros(w_gate.shape, jnp.float32), jnp.zeros(w_up.shape, jnp.float32), jnp.zeros(w_down.shape, jnp.float32))
    totals, (outputs, grad_inputs) = lax.scan(one_sequence, zero_init, (inputs, cotangent))
    return (outputs, grad_inputs, totals[0], totals[1], totals[2], totals[3], totals[4], totals[5], totals[6], totals[7])
```

```python
import jax
import jax.numpy as jnp
from jax import lax
from jax.sharding import PartitionSpec as P

H = 16
KV = 8
HD = 64
EPSILON = 1e-06
THETA_BASE = 1000000.0
NEG_FILL = -1e30
F32 = jnp.float32
BF16 = jnp.bfloat16


def norm_scale(vector):
    return lax.rsqrt(jnp.mean(vector * vector, axis=-1, keepdims=True) + EPSILON)


def norm_back(vector, scale, weighted):
    return scale * weighted - vector * scale**3 * jnp.mean(weighted * vector, axis=-1, keepdims=True)


def rotate(vector):
    middle = vector.shape[-1] // 2
    return jnp.concatenate([-vector[..., middle:], vector[..., :middle]], axis=-1)


def rotate_back(vector):
    middle = vector.shape[-1] // 2
    return jnp.concatenate([vector[..., middle:], -vector[..., :middle]], axis=-1)


def rope_tables(positions):
    inverse = THETA_BASE ** (-jnp.arange(0, HD, 2).astype(F32) / HD)
    angles = positions.astype(F32)[:, None] * inverse[None, :]
    angles = jnp.concatenate([angles, angles], axis=-1)
    return (jnp.cos(angles), jnp.sin(angles))


def dot(a, b):
    return jnp.dot(a, b, preferred_element_type=F32)


def scores_of(q, k):
    length = q.shape[0]
    s = jnp.einsum("rkgd,lkd->kgrl", q, k, preferred_element_type=F32) * HD**-0.5
    allowed = jnp.arange(length)[:, None] >= jnp.arange(length)[None, :]
    return jnp.where(allowed, s, NEG_FILL)


def attend_forward(q, k, v):
    s = scores_of(q, k)
    top = jnp.max(s, axis=-1, keepdims=True)
    total = top + jnp.log(jnp.sum(jnp.exp(s - top), axis=-1, keepdims=True))
    w = jnp.exp(s - total).astype(BF16)
    mix = jnp.einsum("kgrl,lkd->rkgd", w, v, preferred_element_type=F32).astype(BF16)
    return mix, total


def attend_backward(q, k, v, g, total):
    s = scores_of(q, k)
    p = jnp.exp(s - total)
    w = p.astype(BF16)
    gv = jnp.einsum("kgrl,rkgd->lkd", w, g, preferred_element_type=F32)
    gp = jnp.einsum("rkgd,lkd->kgrl", g, v, preferred_element_type=F32)
    centre = jnp.sum(p * gp, axis=-1, keepdims=True)
    gs = (p * (gp - centre) * HD**-0.5).astype(BF16)
    gq = jnp.einsum("kgrl,lkd->rkgd", gs, k, preferred_element_type=F32)
    gk = jnp.einsum("kgrl,rkgd->lkd", gs, q, preferred_element_type=F32)
    return gq.astype(BF16), gk.astype(BF16), gv.astype(BF16)


def shards(inputs, cotangent, first_gain, w_qkv, qk_gain, w_out, second_gain, w_gate, w_up, w_down):
    _, tok, width = inputs.shape
    ns, nd = lax.axis_size("seq"), lax.axis_size("dp")
    s, d = lax.axis_index("seq"), lax.axis_index("dp")
    length = ns * tok
    hq, hk = H // ns, KV // ns
    qw, kw = hq * HD, hk * HD
    rows_d = w_down.shape[0]
    ff = rows_d * nd
    piece = rows_d // ns

    mine_qkv = jnp.concatenate(
        [
            lax.dynamic_slice_in_dim(w_qkv, s * qw, qw, 1),
            lax.dynamic_slice_in_dim(w_qkv, H * HD + s * kw, kw, 1),
            lax.dynamic_slice_in_dim(w_qkv, (H + KV) * HD + s * kw, kw, 1),
        ],
        axis=1,
    )
    gains = jnp.zeros((3, width), F32)
    gains = lax.dynamic_update_slice(gains, first_gain[None], (0, d * first_gain.shape[0]))
    gains = lax.dynamic_update_slice(gains, second_gain[None], (1, d * second_gain.shape[0]))
    gains = lax.dynamic_update_slice(gains, qk_gain[None], (2, d * qk_gain.shape[0]))
    gains = lax.psum(gains, "dp")
    gain_in, gain_mid, gain_qk = gains[0], gains[1], gains[2, : 2 * HD]
    weight_qkv = lax.all_gather(mine_qkv, "dp", axis=0, tiled=True)
    stream_all = lax.all_gather(inputs[0], "seq", axis=0, tiled=True)
    weight_out = lax.all_gather(w_out, "dp", axis=0, tiled=True)
    cot_all = lax.all_gather(cotangent[0], "seq", axis=0, tiled=True)

    def slice_ff(w):
        return w.reshape(w.shape[0], nd, ns, piece)[:, :, s, :].reshape(w.shape[0], nd * piece)

    ffn = jnp.concatenate([slice_ff(w_gate), slice_ff(w_up)], axis=1)
    ffn = lax.all_gather(ffn, "dp", axis=0, tiled=True)
    down = lax.all_gather(lax.dynamic_slice_in_dim(w_down, s * piece, piece, 0), "dp", axis=0, tiled=True)

    stream32 = stream_all.astype(F32)
    scale_in = norm_scale(stream32)
    normed_in = (stream32 * scale_in * gain_in).astype(BF16)
    projected = dot(normed_in, weight_qkv)
    cosine, sine = rope_tables(jnp.arange(length))
    cosine, sine = cosine[:, None, :], sine[:, None, :]
    queries = projected[:, :qw].reshape(length, hq, HD)
    key_raw = projected[:, qw : qw + kw].reshape(length, hk, HD)
    scale_query, scale_key = norm_scale(queries), norm_scale(key_raw)
    query_normed = queries * scale_query * gain_qk[:HD]
    key_normed = key_raw * scale_key * gain_qk[HD:]
    q = (query_normed * cosine + rotate(query_normed) * sine).astype(BF16).reshape(length, hk, hq // hk, HD)
    k = (key_normed * cosine + rotate(key_normed) * sine).astype(BF16)
    v = projected[:, qw + kw :].astype(BF16).reshape(length, hk, HD)
    mix, total = attend_forward(q, k, v)
    mix = mix.reshape(length, qw)
    mixed_rows = lax.all_to_all(mix, "seq", split_axis=0, concat_axis=1, tiled=True)
    stream = inputs[0].astype(F32)
    residual = stream + dot(mixed_rows, weight_out)

    scale_mid = norm_scale(residual)
    normed_own = (residual * scale_mid * gain_mid).astype(BF16)
    normed_mid = lax.all_gather(normed_own, "seq", axis=0, tiled=True)
    n = nd * piece
    both = dot(normed_mid, ffn)
    gate_pre, up_pre = both[:, :n], both[:, n:]
    gate_sig = jax.nn.sigmoid(gate_pre)
    hidden = (gate_pre * gate_sig * up_pre).astype(BF16)
    grad_hidden = jnp.einsum("ri,ji->rj", cot_all, down, preferred_element_type=F32)
    ggp = (grad_hidden * up_pre * gate_sig * (1.0 + gate_pre * (1.0 - gate_sig))).astype(BF16)
    gup = (grad_hidden * gate_pre * gate_sig).astype(BF16)
    gboth = jnp.concatenate([ggp, gup], axis=1)
    gnm = lax.psum_scatter(
        jnp.einsum("ri,ji->rj", gboth, ffn, preferred_element_type=F32).astype(BF16),
        "seq", scatter_dimension=0, tiled=True,
    ).astype(F32)
    out_part = lax.psum_scatter(dot(hidden, down).astype(BF16), "seq", scatter_dimension=0, tiled=True)
    outputs = (residual + out_part.astype(F32)).astype(BF16)
    upstream = cotangent[0]
    grad_second = jnp.sum(gnm * residual * scale_mid, axis=0)
    grad_residual = upstream.astype(F32) + norm_back(residual, scale_mid, gnm * gain_mid)
    residual_back = grad_residual.astype(BF16)
    grad_mixed = jnp.einsum("ri,ji->rj", residual_back, weight_out, preferred_element_type=F32).astype(BF16)
    g = lax.all_to_all(grad_mixed, "seq", split_axis=1, concat_axis=0, tiled=True)

    gg = jnp.einsum("ri,rj->ij", normed_mid, gboth, preferred_element_type=F32).astype(BF16)
    gd = jnp.einsum("ri,rj->ij", hidden, cot_all, preferred_element_type=F32).astype(BF16)
    gg = lax.psum_scatter(gg, "dp", scatter_dimension=0, tiled=True)
    gd = lax.psum_scatter(gd, "dp", scatter_dimension=0, tiled=True)
    gout = jnp.einsum("ri,rj->ij", mixed_rows, residual_back, preferred_element_type=F32).astype(BF16)
    gout = lax.psum_scatter(gout, "dp", scatter_dimension=0, tiled=True)
    gout = lax.psum_scatter(gout, "seq", scatter_dimension=1, tiled=True)

    gq, gk, gv = attend_backward(q, k, v, g.reshape(q.shape), total)
    gq = gq.reshape(length, hq, HD).astype(F32)
    gk = gk.astype(F32)
    gqn = gq * cosine + rotate_back(gq * sine)
    gkn = gk * cosine + rotate_back(gk * sine)
    grad_qk = jnp.concatenate(
        [jnp.sum(gqn * queries * scale_query, axis=(0, 1)), jnp.sum(gkn * key_raw * scale_key, axis=(0, 1))]
    )
    gql = norm_back(queries, scale_query, gqn * gain_qk[:HD]).reshape(length, qw).astype(BF16)
    gkl = norm_back(key_raw, scale_key, gkn * gain_qk[HD:]).reshape(length, kw).astype(BF16)
    gproj = jnp.concatenate([gql, gkl, gv.reshape(length, kw)], axis=1)
    gqkv = jnp.einsum("ri,rj->ij", normed_in, gproj, preferred_element_type=F32).astype(BF16)
    gqkv = lax.psum_scatter(gqkv, "dp", scatter_dimension=0, tiled=True)
    gni = jnp.einsum("ri,ji->rj", gproj, weight_qkv, preferred_element_type=F32).astype(BF16)
    gni = lax.psum_scatter(gni, "seq", scatter_dimension=0, tiled=True).astype(F32)
    scale_own = norm_scale(stream)
    grad_first = jnp.sum(gni * stream * scale_own, axis=0)
    grad_stream = grad_residual + norm_back(stream, scale_own, gni * gain_in)
    small = jnp.stack([grad_first, grad_second, jnp.pad(grad_qk, (0, width - 2 * HD))])
    small = lax.psum(small, ("dp", "seq"))

    gl = first_gain.shape[0]
    ql = qk_gain.shape[0]
    g_first = lax.dynamic_slice(small, (0, d * gl), (1, gl))[0]
    g_second = lax.dynamic_slice(small, (1, d * gl), (1, gl))[0]
    g_qk = lax.dynamic_slice(small, (2, d * ql), (1, ql))[0]

    flat = jnp.concatenate(
        [gg.reshape(-1, 128), gd.reshape(-1, 128), gout.reshape(-1, 128), gqkv.reshape(-1, 128)], axis=0
    )
    flat = lax.all_gather(flat, "seq", axis=0)
    rows = w_gate.shape[0]
    a = gg.size // 128
    b = a + gd.size // 128
    c = b + gout.size // 128
    gg = flat[:, :a].reshape(ns, rows, 2, nd, piece).astype(F32)
    gg = gg.transpose(2, 1, 3, 0, 4).reshape(2, rows, ff)
    gd = flat[:, a:b].reshape(rows_d, width).astype(F32)
    gout = flat[:, b:c].reshape(ns, rows, width // ns).astype(F32).transpose(1, 0, 2).reshape(rows, width)
    gqkv = flat[:, c:].reshape(ns, rows, qw + 2 * kw).astype(F32).transpose(1, 0, 2)
    gqkv = jnp.concatenate(
        [
            gqkv[:, :, :qw].reshape(rows, -1),
            gqkv[:, :, qw : qw + kw].reshape(rows, -1),
            gqkv[:, :, qw + kw :].reshape(rows, -1),
        ],
        axis=1,
    )
    return (outputs[None], grad_stream[None], g_first, gqkv, g_qk, gout, g_second, gg[0], gg[1], gd)


def solution(mesh):
    act = P("dp", "seq", None)
    vec, mat = P("dp"), P("dp", None)
    in_specs = (act, act, vec, mat, vec, mat, vec, mat, mat, mat)
    out_specs = (act, act, vec, mat, vec, mat, vec, mat, mat, mat)
    return jax.shard_map(shards, mesh=mesh, in_specs=in_specs, out_specs=out_specs, check_vma=False)
```

```python
import functools

import jax
import jax.numpy as jnp
import numpy as np
from jax import lax
from jax.experimental import pallas as pl
from jax.experimental.pallas import tpu as pltpu
from jax.sharding import PartitionSpec as P

H = 16
KV = 8
HD = 64
EPSILON = 1e-06
THETA_BASE = 1000000.0
NEG_FILL = -1e30
F32 = jnp.float32
BF16 = jnp.bfloat16


def norm_scale(vector):
    return lax.rsqrt(jnp.mean(vector * vector, axis=-1, keepdims=True) + EPSILON)


def norm_back(vector, scale, weighted):
    return scale * weighted - vector * scale**3 * jnp.mean(weighted * vector, axis=-1, keepdims=True)


def rotate(vector):
    middle = vector.shape[-1] // 2
    return jnp.concatenate([-vector[..., middle:], vector[..., :middle]], axis=-1)


def rotate_back(vector):
    middle = vector.shape[-1] // 2
    return jnp.concatenate([vector[..., middle:], -vector[..., :middle]], axis=-1)


def rope_tables(positions):
    inverse = THETA_BASE ** (-jnp.arange(0, HD, 2).astype(F32) / HD)
    angles = positions.astype(F32)[:, None] * inverse[None, :]
    angles = jnp.concatenate([angles, angles], axis=-1)
    return (jnp.cos(angles), jnp.sin(angles))


def rope_columns(length):
    inverse = np.float32(THETA_BASE) ** (-np.arange(0, HD, 2).astype(np.float32) / np.float32(HD))
    angles = (np.arange(length, dtype=np.float32)[None, :] * inverse.astype(np.float32)[:, None]).astype(np.float32)
    angles = angles.astype(np.float64)
    return jnp.asarray(np.cos(angles), F32), jnp.asarray(np.sin(angles), F32)


MESH = pl.DeviceIdType.MESH
DMA = pltpu.SemaphoreType.DMA


def mm(a, b):
    return jnp.dot(a, b, preferred_element_type=F32)


def mm_nt(a, b):
    return lax.dot_general(a, b, (((1,), (1,)), ((), ())), preferred_element_type=F32)


def remote(src, dst, send, recv, device):
    return pltpu.make_async_remote_copy(
        src_ref=src, dst_ref=dst, send_sem=send, recv_sem=recv, device_id=device, device_id_type=MESH
    )


def greet(ns, nd, s, d):
    bar = pltpu.get_barrier_semaphore()
    for j in range(1, nd):
        pl.semaphore_signal(bar, inc=1, device_id=(lax.rem(d + j, nd), s), device_id_type=MESH)
    for j in range(1, ns):
        pl.semaphore_signal(bar, inc=1, device_id=(d, lax.rem(s + j, ns)), device_id_type=MESH)
    pl.semaphore_wait(bar, nd + ns - 2)


def front_kernel(
    ns, nd, x, gains, wqkv_mine, wout_mine, cot, cos, sin,
    normed, projT, qT, kT, vT, krows, vrows, inv, mixT, mrowsT, resid, wout, wqkv, gsum, cotall,
    xall, gbuf, xs, xr, gs, gr, qs, qr, os_, or_, fs, fr, cs, cr, ms, mr,
):
    d, s = lax.axis_index("dp"), lax.axis_index("seq")
    nz = nd // 2
    zz, core = d // 2, lax.rem(d, 2)
    sib = d + 1 - 2 * core
    T = x.shape[0]
    L = ns * T
    R = wqkv_mine.shape[0]
    hq, hk = H // ns, KV // ns
    group = hq // hk
    qw, kw = hq * HD, hk * HD
    own = pl.ds(pl.multiple_of(s * T, T), T)
    mine = pl.ds(pl.multiple_of(d * R, R), R)
    greet(ns, nd, s, d)

    def to(j):
        return (d, lax.rem(s + j, ns))

    x_copies = [remote(x, xall.at[own], xs.at[j], xr.at[j], to(j)) for j in range(1, ns)]
    g_copies = [
        remote(gains, gbuf.at[d], gs.at[j], gr.at[j], (lax.rem(d + j, nd), s)) for j in range(1, nd)
    ]
    q_copies = [
        remote(wqkv_mine, wqkv.at[mine], qs.at[j], qr.at[j], (lax.rem(d + j, nd), s)) for j in range(1, nd)
    ]
    o_copies = [
        remote(wout_mine, wout.at[mine], os_.at[j], or_.at[j], (2 * lax.rem(zz + j, nz) + core, s))
        for j in range(1, nz)
    ]
    o_copies.append(remote(wout_mine, wout.at[mine], os_.at[0], or_.at[0], (sib, s)))
    for c in x_copies + g_copies + q_copies + o_copies:
        c.start()
    xall[own, :] = x[...]
    gbuf[d] = gains[...]
    wqkv[mine, :] = wqkv_mine[...]
    wout[mine, :] = wout_mine[...]
    cotall[own, :] = cot[...]
    for c in g_copies:
        c.wait_recv()
    total = gbuf[0]
    for k in range(1, nd):
        total = total + gbuf[k]
    gsum[...] = total
    gain_in = total[0:1, :]
    columns = jnp.transpose(total[:, : 2 * HD])
    gain_q, gain_k = columns[:HD, 2:3], columns[HD:, 2:3]

    c_copies = [remote(cot, cotall.at[own], cs.at[j], cr.at[j], to(j)) for j in range(1, ns)]
    for j in range(ns):
        rows = pl.ds(pl.multiple_of(lax.rem(s + ns - j, ns) * T, T), T)
        if j:
            x_copies[j - 1].wait_recv()
        xc = xall[rows, :].astype(F32)
        scale = lax.rsqrt(jnp.mean(xc * xc, axis=-1, keepdims=True) + EPSILON)
        normed[rows, :] = (xc * scale * gain_in).astype(BF16)
    for c in c_copies:
        c.start()
    for c in q_copies:
        c.wait_recv()
    for j in range(ns):
        rows = pl.ds(j * T, T)
        proj = mm(normed[rows, :], wqkv[...])
        projT[:, rows] = jnp.transpose(proj[:, : qw + kw])
        val = proj[:, qw + kw :]
        vT[:, rows] = jnp.transpose(val).astype(BF16)
        for i in range(hk):
            vrows[i, rows, :] = val[:, i * HD : (i + 1) * HD].astype(BF16)

    half = HD // 2

    def rope(row, gain, factor):
        u = projT[row, :]
        scale = lax.rsqrt(jnp.mean(u * u, axis=0, keepdims=True) + EPSILON)
        u = u * scale * gain
        a, b = u[:half], u[half:]
        return jnp.concatenate([a * cos[...] - b * sin[...], b * cos[...] + a * sin[...]], axis=0) * factor

    def rope_query(h, carry):
        row = pl.ds(pl.multiple_of(h * HD, HD), HD)
        qT[row, :] = rope(row, gain_q, HD**-0.5).astype(BF16)
        return carry

    lax.fori_loop(0, hq, rope_query, 0)
    for i in range(hk):
        r = rope(pl.ds(qw + i * HD, HD), gain_k, 1.0)
        kT[i * HD : (i + 1) * HD, :] = r.astype(BF16)
        krows[i, :, :] = jnp.transpose(r).astype(BF16)

    for c in o_copies:
        c.wait_recv()
    f_copies = []
    for j in range(1, nz):
        piece = pl.ds(pl.multiple_of((2 * lax.rem(zz + nz - j, nz) + core) * R, R), R)
        c = remote(wout.at[piece], wout.at[piece], fs.at[j], fr.at[j], (sib, s))
        c.start()
        f_copies.append(c)

    keep = lax.broadcasted_iota(jnp.int32, (T, T), 0) <= lax.broadcasted_iota(jnp.int32, (T, T), 1)
    for rb in range(ns):
        cols = pl.ds(rb * T, T)
        span = rb * T

        def head(h, carry):
            kv = h // group
            row = pl.ds(pl.multiple_of(h * HD, HD), HD)
            vrow = pl.ds(pl.multiple_of(kv * HD, HD), HD)
            q = qT[row, cols]
            p = jnp.where(keep, jnp.exp(mm(krows[kv, cols, :], q)), 0.0)
            tot = jnp.sum(p, axis=0, keepdims=True)
            m = mm(vT[vrow, cols], p.astype(BF16))
            if span:
                p = jnp.exp(mm(krows[kv, 0:span, :], q))
                tot = tot + jnp.sum(p, axis=0, keepdims=True)
                m = m + mm(vT[vrow, 0:span], p.astype(BF16))
            one = 1.0 / tot
            inv[h, :, cols] = one
            mixT[rb, row, :] = (m * one).astype(BF16)
            return carry

        lax.fori_loop(0, hq, head, 0)
        block = pl.ds(pl.multiple_of(s * qw, qw), qw)

        @pl.when(s != rb)
        def _():
            remote(mixT.at[rb], mrowsT.at[block], ms.at[rb], mr.at[s], (d, rb)).start()

    block = pl.ds(pl.multiple_of(s * qw, qw), qw)
    mrowsT[block, :] = mixT[s]
    for j in range(1, ns):
        src = lax.rem(s + ns - j, ns)
        part = pl.ds(pl.multiple_of(src * qw, qw), qw)
        remote(mixT.at[0], mrowsT.at[part], ms.at[0], mr.at[src], (d, src)).wait_recv()
    for c in f_copies:
        c.wait_recv()
    resid[...] = x[...].astype(F32) + mm(jnp.transpose(mrowsT[...]), wout[...])
    for rb in range(ns):

        @pl.when(s != rb)
        def _():
            remote(mixT.at[rb], mrowsT.at[block], ms.at[rb], mr.at[s], (d, rb)).wait_send()

    for c in c_copies:
        c.wait_recv()
    for c in x_copies + g_copies + q_copies + o_copies + f_copies + c_copies:
        c.wait_send()


def vmem(n):
    return [pl.BlockSpec(memory_space=pltpu.VMEM)] * n


def front(ns, nd, x, gains, wqkv_mine, wout_mine, cot):
    T, width = x.shape
    L = ns * T
    hq, hk = H // ns, KV // ns
    qw, kw = hq * HD, hk * HD
    cos, sin = rope_columns(L)
    sh = jax.ShapeDtypeStruct
    outs = (
        sh((L, width), BF16), sh((qw + kw, L), F32), sh((qw, L), BF16), sh((kw, L), BF16), sh((kw, L), BF16),
        sh((hk, L, HD), BF16), sh((hk, L, HD), BF16), sh((hq, 1, L), F32), sh((ns, qw, T), BF16),
        sh((H * HD, T), BF16), sh((T, width), F32), sh((H * HD, width), BF16), sh((width, qw + 2 * kw), BF16),
        sh((8, width), F32), sh((L, width), BF16),
    )
    return pl.pallas_call(
        functools.partial(front_kernel, ns, nd),
        out_shape=outs,
        in_specs=vmem(7),
        out_specs=vmem(len(outs)),
        scratch_shapes=[
            pltpu.VMEM((L, width), BF16), pltpu.VMEM((nd, 8, width), F32),
            DMA((ns,)), DMA((ns,)), DMA((nd,)), DMA((nd,)), DMA((nd,)), DMA((nd,)), DMA((nd,)), DMA((nd,)),
            DMA((nd,)), DMA((nd,)), DMA((ns,)), DMA((ns,)), DMA((ns,)), DMA((ns,)),
        ],
        compiler_params=pltpu.CompilerParams(
            collective_id=0, has_side_effects=True, vmem_limit_bytes=56 << 20
        ),
        cost_estimate=pl.CostEstimate(flops=6_000_000_000, bytes_accessed=20_000_000, transcendentals=3_000_000),
    )(x, gains, wqkv_mine, wout_mine, cot, cos, sin)


def dot(a, b):
    return jnp.dot(a, b, preferred_element_type=F32)


def scores_of(q, k):
    length = q.shape[0]
    s = jnp.einsum("rkgd,lkd->kgrl", q, k, preferred_element_type=F32) * HD**-0.5
    allowed = jnp.arange(length)[:, None] >= jnp.arange(length)[None, :]
    return jnp.where(allowed, s, NEG_FILL)


def attend_forward(q, k, v):
    s = scores_of(q, k)
    top = jnp.max(s, axis=-1, keepdims=True)
    total = top + jnp.log(jnp.sum(jnp.exp(s - top), axis=-1, keepdims=True))
    w = jnp.exp(s - total).astype(BF16)
    mix = jnp.einsum("kgrl,lkd->rkgd", w, v, preferred_element_type=F32).astype(BF16)
    return mix, total


def attend_backward(q, k, v, g, total):
    s = scores_of(q, k)
    p = jnp.exp(s - total)
    w = p.astype(BF16)
    gv = jnp.einsum("kgrl,rkgd->lkd", w, g, preferred_element_type=F32)
    gp = jnp.einsum("rkgd,lkd->kgrl", g, v, preferred_element_type=F32)
    centre = jnp.sum(p * gp, axis=-1, keepdims=True)
    gs = (p * (gp - centre) * HD**-0.5).astype(BF16)
    gq = jnp.einsum("kgrl,lkd->rkgd", gs, k, preferred_element_type=F32)
    gk = jnp.einsum("kgrl,rkgd->lkd", gs, q, preferred_element_type=F32)
    return gq.astype(BF16), gk.astype(BF16), gv.astype(BF16)


def shards(inputs, cotangent, first_gain, w_qkv, qk_gain, w_out, second_gain, w_gate, w_up, w_down):
    _, tok, width = inputs.shape
    ns, nd = lax.axis_size("seq"), lax.axis_size("dp")
    s, d = lax.axis_index("seq"), lax.axis_index("dp")
    length = ns * tok
    hq, hk = H // ns, KV // ns
    qw, kw = hq * HD, hk * HD
    rows_d = w_down.shape[0]
    ff = rows_d * nd
    piece = rows_d // ns

    mine_qkv = jnp.concatenate(
        [
            lax.dynamic_slice_in_dim(w_qkv, s * qw, qw, 1),
            lax.dynamic_slice_in_dim(w_qkv, H * HD + s * kw, kw, 1),
            lax.dynamic_slice_in_dim(w_qkv, (H + KV) * HD + s * kw, kw, 1),
        ],
        axis=1,
    )
    gains = jnp.zeros((8, width), F32)
    gains = lax.dynamic_update_slice(gains, first_gain[None], (0, d * first_gain.shape[0]))
    gains = lax.dynamic_update_slice(gains, second_gain[None], (1, d * second_gain.shape[0]))
    gains = lax.dynamic_update_slice(gains, qk_gain[None], (2, d * qk_gain.shape[0]))
    (normed_in, projT, qT, kT, vT, krows, vrows, inv, mixT, mrowsT, residual, weight_out, weight_qkv, gains,
     cot_all) = front(ns, nd, inputs[0], gains, mine_qkv, w_out, cotangent[0])
    gain_in, gain_mid, gain_qk = gains[0], gains[1], gains[2, : 2 * HD]

    def slice_ff(w):
        return w.reshape(w.shape[0], nd, ns, piece)[:, :, s, :].reshape(w.shape[0], nd * piece)

    ffn = jnp.concatenate([slice_ff(w_gate), slice_ff(w_up)], axis=1)
    ffn = lax.all_gather(ffn, "dp", axis=0, tiled=True)
    down = lax.all_gather(lax.dynamic_slice_in_dim(w_down, s * piece, piece, 0), "dp", axis=0, tiled=True)

    stream = inputs[0].astype(F32)
    cosine, sine = rope_tables(jnp.arange(length))
    cosine, sine = cosine[:, None, :], sine[:, None, :]
    queries = projT[:qw].T.reshape(length, hq, HD)
    key_raw = projT[qw:].T.reshape(length, hk, HD)
    scale_query, scale_key = norm_scale(queries), norm_scale(key_raw)
    q = (qT.T * 8.0).astype(BF16).reshape(length, hk, hq // hk, HD)
    k = krows.transpose(1, 0, 2)
    v = vrows.transpose(1, 0, 2)
    total = -jnp.log(inv.reshape(hk, hq // hk, length, 1))
    mixed_rows = mrowsT.T

    scale_mid = norm_scale(residual)
    normed_own = (residual * scale_mid * gain_mid).astype(BF16)
    normed_mid = lax.all_gather(normed_own, "seq", axis=0, tiled=True)
    n = nd * piece
    both = dot(normed_mid, ffn)
    gate_pre, up_pre = both[:, :n], both[:, n:]
    gate_sig = jax.nn.sigmoid(gate_pre)
    hidden = (gate_pre * gate_sig * up_pre).astype(BF16)
    grad_hidden = jnp.einsum("ri,ji->rj", cot_all, down, preferred_element_type=F32)
    ggp = (grad_hidden * up_pre * gate_sig * (1.0 + gate_pre * (1.0 - gate_sig))).astype(BF16)
    gup = (grad_hidden * gate_pre * gate_sig).astype(BF16)
    gboth = jnp.concatenate([ggp, gup], axis=1)
    gnm = lax.psum_scatter(
        jnp.einsum("ri,ji->rj", gboth, ffn, preferred_element_type=F32).astype(BF16),
        "seq", scatter_dimension=0, tiled=True,
    ).astype(F32)
    out_part = lax.psum_scatter(dot(hidden, down).astype(BF16), "seq", scatter_dimension=0, tiled=True)
    outputs = (residual + out_part.astype(F32)).astype(BF16)
    upstream = cotangent[0]
    grad_second = jnp.sum(gnm * residual * scale_mid, axis=0)
    grad_residual = upstream.astype(F32) + norm_back(residual, scale_mid, gnm * gain_mid)
    residual_back = grad_residual.astype(BF16)
    grad_mixed = jnp.einsum("ri,ji->rj", residual_back, weight_out, preferred_element_type=F32).astype(BF16)
    g = lax.all_to_all(grad_mixed, "seq", split_axis=1, concat_axis=0, tiled=True)

    gg = jnp.einsum("ri,rj->ij", normed_mid, gboth, preferred_element_type=F32).astype(BF16)
    gd = jnp.einsum("ri,rj->ij", hidden, cot_all, preferred_element_type=F32).astype(BF16)
    gg = lax.psum_scatter(gg, "dp", scatter_dimension=0, tiled=True)
    gd = lax.psum_scatter(gd, "dp", scatter_dimension=0, tiled=True)
    gout = jnp.einsum("ri,rj->ij", mixed_rows, residual_back, preferred_element_type=F32).astype(BF16)
    gout = lax.psum_scatter(gout, "dp", scatter_dimension=0, tiled=True)
    gout = lax.psum_scatter(gout, "seq", scatter_dimension=1, tiled=True)

    gq, gk, gv = attend_backward(q, k, v, g.reshape(q.shape), total)
    gq = gq.reshape(length, hq, HD).astype(F32)
    gk = gk.astype(F32)
    gqn = gq * cosine + rotate_back(gq * sine)
    gkn = gk * cosine + rotate_back(gk * sine)
    grad_qk = jnp.concatenate(
        [jnp.sum(gqn * queries * scale_query, axis=(0, 1)), jnp.sum(gkn * key_raw * scale_key, axis=(0, 1))]
    )
    gql = norm_back(queries, scale_query, gqn * gain_qk[:HD]).reshape(length, qw).astype(BF16)
    gkl = norm_back(key_raw, scale_key, gkn * gain_qk[HD:]).reshape(length, kw).astype(BF16)
    gproj = jnp.concatenate([gql, gkl, gv.reshape(length, kw)], axis=1)
    gqkv = jnp.einsum("ri,rj->ij", normed_in, gproj, preferred_element_type=F32).astype(BF16)
    gqkv = lax.psum_scatter(gqkv, "dp", scatter_dimension=0, tiled=True)
    gni = jnp.einsum("ri,ji->rj", gproj, weight_qkv, preferred_element_type=F32).astype(BF16)
    gni = lax.psum_scatter(gni, "seq", scatter_dimension=0, tiled=True).astype(F32)
    scale_own = norm_scale(stream)
    grad_first = jnp.sum(gni * stream * scale_own, axis=0)
    grad_stream = grad_residual + norm_back(stream, scale_own, gni * gain_in)
    small = jnp.stack([grad_first, grad_second, jnp.pad(grad_qk, (0, width - 2 * HD))])
    small = lax.psum(small, ("dp", "seq"))

    gl = first_gain.shape[0]
    ql = qk_gain.shape[0]
    g_first = lax.dynamic_slice(small, (0, d * gl), (1, gl))[0]
    g_second = lax.dynamic_slice(small, (1, d * gl), (1, gl))[0]
    g_qk = lax.dynamic_slice(small, (2, d * ql), (1, ql))[0]

    flat = jnp.concatenate(
        [gg.reshape(-1, 128), gd.reshape(-1, 128), gout.reshape(-1, 128), gqkv.reshape(-1, 128)], axis=0
    )
    flat = lax.all_gather(flat, "seq", axis=0)
    rows = w_gate.shape[0]
    a = gg.size // 128
    b = a + gd.size // 128
    c = b + gout.size // 128
    gg = flat[:, :a].reshape(ns, rows, 2, nd, piece).astype(F32)
    gg = gg.transpose(2, 1, 3, 0, 4).reshape(2, rows, ff)
    gd = flat[:, a:b].reshape(rows_d, width).astype(F32)
    gout = flat[:, b:c].reshape(ns, rows, width // ns).astype(F32).transpose(1, 0, 2).reshape(rows, width)
    gqkv = flat[:, c:].reshape(ns, rows, qw + 2 * kw).astype(F32).transpose(1, 0, 2)
    gqkv = jnp.concatenate(
        [
            gqkv[:, :, :qw].reshape(rows, -1),
            gqkv[:, :, qw : qw + kw].reshape(rows, -1),
            gqkv[:, :, qw + kw :].reshape(rows, -1),
        ],
        axis=1,
    )
    return (outputs[None], grad_stream[None], g_first, gqkv, g_qk, gout, g_second, gg[0], gg[1], gd)


def solution(mesh):
    act = P("dp", "seq", None)
    vec, mat = P("dp"), P("dp", None)
    in_specs = (act, act, vec, mat, vec, mat, vec, mat, mat, mat)
    out_specs = (act, act, vec, mat, vec, mat, vec, mat, mat, mat)
    return jax.shard_map(shards, mesh=mesh, in_specs=in_specs, out_specs=out_specs, check_vma=False)
```

```python
import functools

import jax
import jax.numpy as jnp
import numpy as np
from jax import lax
from jax.experimental import pallas as pl
from jax.experimental.pallas import tpu as pltpu
from jax.sharding import PartitionSpec as P

H = 16
KV = 8
HD = 64
EPSILON = 1e-06
THETA_BASE = 1000000.0
F32 = jnp.float32
BF16 = jnp.bfloat16


def rope_columns(length):
    inverse = np.float32(THETA_BASE) ** (-np.arange(0, HD, 2).astype(np.float32) / np.float32(HD))
    angles = (np.arange(length, dtype=np.float32)[None, :] * inverse.astype(np.float32)[:, None]).astype(np.float32)
    angles = angles.astype(np.float64)
    return jnp.asarray(np.cos(angles), F32), jnp.asarray(np.sin(angles), F32)


MESH = pl.DeviceIdType.MESH
DMA = pltpu.SemaphoreType.DMA


def mm(a, b):
    return jnp.dot(a, b, preferred_element_type=F32)


def mm_nt(a, b):
    return lax.dot_general(a, b, (((1,), (1,)), ((), ())), preferred_element_type=F32)


def remote(src, dst, send, recv, device):
    return pltpu.make_async_remote_copy(
        src_ref=src, dst_ref=dst, send_sem=send, recv_sem=recv, device_id=device, device_id_type=MESH
    )


def block_of(index, size):
    return pl.ds(pl.multiple_of(index * size, size), size)


class Place:
    def __init__(self, ns, nd):
        self.ns, self.nd, self.nz = ns, nd, nd // 2
        self.d, self.s = lax.axis_index("dp"), lax.axis_index("seq")
        self.zz, self.core = self.d // 2, lax.rem(self.d, 2)
        self.sib = (self.d + 1 - 2 * self.core, self.s)

    def seq_to(self, j):
        return (self.d, lax.rem(self.s + j, self.ns))

    def seq_from(self, j):
        return lax.rem(self.s + self.ns - j, self.ns)

    def dp_to(self, j):
        return (lax.rem(self.d + j, self.nd), self.s)

    def z_index(self, j):
        return lax.rem(self.zz + j, self.nz)

    def z_from(self, j):
        return lax.rem(self.zz + self.nz - j, self.nz)

    def z_device(self, z):
        return (2 * z + self.core, self.s)

    def greet(self):
        bar = pltpu.get_barrier_semaphore()
        for j in range(1, self.nd):
            pl.semaphore_signal(bar, inc=1, device_id=self.dp_to(j), device_id_type=MESH)
        for j in range(1, self.ns):
            pl.semaphore_signal(bar, inc=1, device_id=self.seq_to(j), device_id_type=MESH)
        pl.semaphore_wait(bar, self.nd + self.ns - 2)


class Gather:
    def __init__(self, at, src, dst, sems):
        self.at, self.src, self.dst = at, src, dst
        self.send, self.recv, self.fsend, self.frecv, self.rsend = sems
        self.rows = src.shape[0]

    def piece(self, z):
        return self.dst.at[block_of(2 * z + self.at.core, self.rows)]

    def direct(self, j):
        at = self.at
        return remote(self.src, self.piece(at.zz), self.send.at[j], self.recv.at[j], at.z_device(at.z_index(j)))

    def near(self, j):
        at = self.at
        away = at.z_index(j) - at.zz
        return (away < at.nz - 1) & (away > 1 - at.nz)

    def across(self, j):
        piece = self.src if j == 0 else self.piece(self.at.z_from(j))
        return remote(piece, self.piece(self.at.z_from(j)), self.fsend.at[j], self.frecv.at[j], self.at.sib)

    def relay(self, j):
        nz = self.at.nz
        legs = []
        if j == nz - 2:
            legs.append((nz - 2, 0, nz - 1, nz - 1, 0))
        if j == 2:
            legs.append((1, nz - 1, 0, 1, 1))
        out = []
        for here, origin, target, index, k in legs:
            piece = self.piece(origin)
            copy = remote(piece, piece, self.rsend.at[k], self.recv.at[index], self.at.z_device(target))
            out.append((self.at.zz == here, copy))
        return out

    def order(self):
        nz = self.at.nz
        return list(range(2, nz - 1)) + [1, nz - 1]

    def start(self):
        at = self.at
        for j in range(1, at.nz):

            @pl.when(self.near(j))
            def _():
                self.direct(j).start()

        self.across(0).start()
        self.dst[block_of(at.d, self.rows), :] = self.src[...]

    def arrive(self):
        for j in self.order():
            self.direct(j).wait_recv()
            for here, copy in self.relay(j):
                pl.when(here)(copy.start)
            self.across(j).start()

    def finish(self):
        for j in range(self.at.nz):
            self.across(j).wait_recv()

    def drain(self):
        for j in range(self.at.nz):
            self.across(j).wait_send()
            if j:
                pl.when(self.near(j))(self.direct(j).wait_send)
                for here, copy in self.relay(j):
                    pl.when(here)(copy.wait_send)


def gather_sems(nz):
    return [DMA((nz,)), DMA((nz,)), DMA((nz,)), DMA((nz,)), DMA((2,))]


def forward_kernel(
    ns, nd, x, gains, wqkv_mine, wout_mine, cot, gu_mine, dn_mine, cos, sin,
    normed, projT, qT, kT, krows, vrows, inv, mixT, mrowsT, wout, wqkv, gsum, gres, osend, oown, guown, dnown, gsecond,
    vT, resid, cotall, xall, gbuf, gu, dn, pre, hrow, hT, gb, gsend, grecv, gown, nmT, gus, gur, dns, dnr,
    xs, xr, gs, gr, cs, cr, ms, mr, ns_, nr, ps, pr, ss, sr, *gsems,
):
    at = Place(ns, nd)
    s, d, nz, core = at.s, at.d, at.nz, at.core
    T, width = x.shape
    L = ns * T
    R = wqkv_mine.shape[0]
    n = dn.shape[0]
    piece = dn_mine.shape[0]
    hq, hk = H // ns, KV // ns
    group = hq // hk
    qw, kw = hq * HD, hk * HD
    own = block_of(s, T)
    at.greet()

    x_copies = [remote(x, xall.at[own], xs.at[j], xr.at[j], at.seq_to(j)) for j in range(1, ns)]
    g_copies = [remote(gains, gbuf.at[d], gs.at[j], gr.at[j], at.dp_to(j)) for j in range(1, nd)]
    c_copies = [remote(cot, cotall.at[own], cs.at[j], cr.at[j], at.seq_to(j)) for j in range(1, ns)]
    take_qkv = Gather(at, wqkv_mine, wqkv, gsems[0:5])
    take_out = Gather(at, wout_mine, wout, gsems[5:10])
    take_gu = Gather(at, gu_mine, gu, gsems[10:15])
    take_dn = Gather(at, dn_mine, dn, gsems[15:20])
    for c in g_copies + x_copies:
        c.start()
    take_qkv.start()
    xall[own, :] = x[...]
    gbuf[d] = gains[...]
    cotall[own, :] = cot[...]
    for c in g_copies:
        c.wait_recv()
    total = gbuf[0]
    for k in range(1, nd):
        total = total + gbuf[k]
    gsum[...] = total
    gain_in, gain_mid = total[0:1, :], total[1:2, :]
    columns = jnp.transpose(total[:, : 2 * HD])
    gain_q, gain_k = columns[:HD, 2:3], columns[HD:, 2:3]
    take_qkv.arrive()
    take_out.start()
    take_gu.start()
    for j in range(ns):
        rows = block_of(at.seq_from(j), T)
        if j:
            x_copies[j - 1].wait_recv()
        xc = xall[rows, :].astype(F32)
        scale = lax.rsqrt(jnp.mean(xc * xc, axis=-1, keepdims=True) + EPSILON)
        normed[rows, :] = (xc * scale * gain_in).astype(BF16)
    for c in c_copies:
        c.start()
    take_qkv.finish()
    for j in range(ns):
        rows = pl.ds(j * T, T)
        proj = mm(normed[rows, :], wqkv[...])
        projT[:, rows] = jnp.transpose(proj[:, : qw + kw])
        val = proj[:, qw + kw :]
        vT[:, rows] = jnp.transpose(val).astype(BF16)
        for i in range(hk):
            vrows[i, rows, :] = val[:, i * HD : (i + 1) * HD].astype(BF16)

    half = HD // 2

    def rope(row, gain, factor):
        u = projT[row, :]
        scale = lax.rsqrt(jnp.mean(u * u, axis=0, keepdims=True) + EPSILON)
        u = u * scale * gain
        a, b = u[:half], u[half:]
        return jnp.concatenate([a * cos[...] - b * sin[...], b * cos[...] + a * sin[...]], axis=0) * factor

    def rope_query(h, carry):
        row = block_of(h, HD)
        qT[row, :] = rope(row, gain_q, HD**-0.5).astype(BF16)
        return carry

    lax.fori_loop(0, hq, rope_query, 0)
    for i in range(hk):
        r = rope(pl.ds(qw + i * HD, HD), gain_k, 1.0)
        kT[i * HD : (i + 1) * HD, :] = r.astype(BF16)
        krows[i, :, :] = jnp.transpose(r).astype(BF16)

    keep = lax.broadcasted_iota(jnp.int32, (T, T), 0) <= lax.broadcasted_iota(jnp.int32, (T, T), 1)
    block = block_of(s, qw)

    def mixed_out(rb):
        return remote(mixT.at[rb], mrowsT.at[block], ms.at[rb], mr.at[s], (d, rb))

    for rb in range(ns):
        cols = pl.ds(rb * T, T)
        span = rb * T

        def head(h, carry):
            kv = h // group
            row, vrow = block_of(h, HD), block_of(kv, HD)
            q = qT[row, cols]
            p = jnp.where(keep, jnp.exp(mm(krows[kv, cols, :], q)), 0.0)
            tot = jnp.sum(p, axis=0, keepdims=True)
            m = mm(vT[vrow, cols], p.astype(BF16))
            if span:
                p = jnp.exp(mm(krows[kv, 0:span, :], q))
                tot = tot + jnp.sum(p, axis=0, keepdims=True)
                m = m + mm(vT[vrow, 0:span], p.astype(BF16))
            one = 1.0 / tot
            inv[h, :, cols] = one
            mixT[rb, row, :] = (m * one).astype(BF16)
            return carry

        lax.fori_loop(0, hq, head, 0)
        pl.when(s != rb)(mixed_out(rb).start)

    take_out.arrive()
    mrowsT[block, :] = mixT[s]
    for j in range(1, ns):
        src = at.seq_from(j)
        remote(mixT.at[0], mrowsT.at[block_of(src, qw)], ms.at[0], mr.at[src], (d, src)).wait_recv()
    take_out.finish()
    residual = x[...].astype(F32) + mm(jnp.transpose(mrowsT[...]), wout[...])
    resid[...] = residual
    scale_mid = lax.rsqrt(jnp.mean(residual * residual, axis=-1, keepdims=True) + EPSILON)
    xall[own, :] = (residual * scale_mid * gain_mid).astype(BF16)
    n_copies = [
        remote(xall.at[own], xall.at[own], ns_.at[j], nr.at[j], at.seq_to(j)) for j in range(1, ns)
    ]
    for c in c_copies:
        c.wait_recv()
    for c in n_copies:
        c.start()
    take_gu.arrive()
    take_dn.start()
    take_gu.finish()

    ft = 384 if n % 384 == 0 else 128
    nt = n // ft
    p_copies = []
    for j in range(ns):
        rows = block_of(at.seq_from(j), T)
        if j:
            n_copies[j - 1].wait_recv()

        def pre_tile(i, carry):
            f = block_of(i, ft)
            pre[:, f] = mm(xall[rows, :], gu[:, f])
            return carry

        lax.fori_loop(0, 2 * nt, pre_tile, 0)
        if j == 0:
            take_dn.arrive()
            take_dn.finish()

        def hidden_tile(i, carry):
            f, f2 = block_of(i, ft), block_of(i + nt, ft)
            gate, up = pre[:, f], pre[:, f2]
            sig = 1.0 / (1.0 + jnp.exp(-gate))
            act = gate * sig
            back = mm_nt(cotall[rows, :], dn[f, :])
            hid = act * up
            hrow[:, f] = hid.astype(BF16)
            hT[f, rows] = jnp.transpose(hid).astype(BF16)
            gb[rows, f] = (back * up * sig * (1.0 + gate * (1.0 - sig))).astype(BF16)
            gb[rows, f2] = (back * act).astype(BF16)
            return carry

        lax.fori_loop(0, nt, hidden_tile, 0)
        wt = 256

        def back_tile(i, carry):
            w = block_of(i, wt)
            part = mm_nt(gb[rows, :], gu[w, :])
            if j:
                gsend[j - 1, :, w] = part.astype(BF16)
            else:
                gown[:, w] = part
            return carry

        lax.fori_loop(0, width // wt, back_tile, 0)
        if j:
            c = remote(gsend.at[j - 1], grecv.at[ns - j - 1], ps.at[j], pr.at[ns - j], at.seq_to(ns - j))
            c.start()
            p_copies.append(c)

        def out_tile(i, carry):
            w = block_of(i, wt)
            part = mm(hrow[...], dn[:, w])
            if j:
                osend[j - 1, :, w] = part.astype(BF16)
            else:
                oown[:, w] = part + resid[:, w]
            return carry

        lax.fori_loop(0, width // wt, out_tile, 0)

    for k in range(nd):
        nmT[k % 2, (k // 2) * R : (k // 2 + 1) * R, :] = jnp.transpose(xall[:, k * R : (k + 1) * R])

    def dn_rows(c, i):
        return hT[block_of(2 * i + c, piece), :]

    def dn_other(i, carry):
        dns[block_of(i, piece), :] = mm(dn_rows(1 - core, i), cotall[...]).astype(BF16)
        return carry

    lax.fori_loop(0, nz, dn_other, 0)
    dn_copy = remote(dns, dnr, ss.at[0], sr.at[0], at.sib)
    dn_copy.start()

    def gu_other(i, carry):
        f = block_of(i, 256)
        gus[:, f] = mm(nmT[1 - core], gb[:, f]).astype(BF16)
        return carry

    lax.fori_loop(0, 2 * n // 256, gu_other, 0)
    gu_copy = remote(gus, gur, ss.at[1], sr.at[1], at.sib)
    gu_copy.start()
    dn_copy.wait_recv()

    def dn_mine_sum(i, carry):
        r = block_of(i, piece)
        dnown[r, :] = (mm(dn_rows(core, i), cotall[...]) + dnr[r, :].astype(F32)).astype(BF16)
        return carry

    lax.fori_loop(0, nz, dn_mine_sum, 0)
    gu_copy.wait_recv()

    def gu_mine_sum(i, carry):
        f = block_of(i, 256)
        guown[:, f] = (mm(nmT[core], gb[:, f]) + gur[:, f].astype(F32)).astype(BF16)
        return carry

    lax.fori_loop(0, 2 * n // 256, gu_mine_sum, 0)

    for c in p_copies:
        c.wait_recv()
    gnm = gown[...]
    for j in range(1, ns):
        gnm = gnm + grecv[j - 1].astype(F32)
    residual = resid[...]
    scale_mid = lax.rsqrt(jnp.mean(residual * residual, axis=-1, keepdims=True) + EPSILON)
    gsecond[...] = jnp.broadcast_to(jnp.sum(gnm * residual * scale_mid, axis=0, keepdims=True), (8, width))
    weighted = gnm * gain_mid
    gres[...] = (
        cot[...].astype(F32)
        + scale_mid * weighted
        - residual * (scale_mid * scale_mid * scale_mid) * jnp.mean(weighted * residual, axis=-1, keepdims=True)
    )
    for rb in range(ns):
        pl.when(s != rb)(mixed_out(rb).wait_send)
    for c in x_copies + g_copies + c_copies + n_copies + p_copies + [dn_copy, gu_copy]:
        c.wait_send()
    for t in (take_qkv, take_out, take_gu, take_dn):
        t.drain()


def vmem(n):
    return [pl.BlockSpec(memory_space=pltpu.VMEM)] * n


def forward(ns, nd, x, gains, wqkv_mine, wout_mine, cot, gu_mine, dn_mine):
    T, width = x.shape
    L = ns * T
    R, n2 = gu_mine.shape
    n = n2 // 2
    piece = dn_mine.shape[0]
    nz = nd // 2
    hq, hk = H // ns, KV // ns
    qw, kw = hq * HD, hk * HD
    cos, sin = rope_columns(L)
    sh, vm = jax.ShapeDtypeStruct, pltpu.VMEM
    outs = (
        sh((L, width), BF16), sh((qw + kw, L), F32), sh((qw, L), BF16), sh((kw, L), BF16),
        sh((hk, L, HD), BF16), sh((hk, L, HD), BF16), sh((hq, 1, L), F32), sh((ns, qw, T), BF16),
        sh((H * HD, T), BF16), sh((H * HD, width), BF16), sh((width, qw + 2 * kw), BF16), sh((8, width), F32),
        sh((T, width), F32), sh((ns - 1, T, width), BF16), sh((T, width), F32),
        sh((nz * R, n2), BF16), sh((nz * piece, width), BF16), sh((8, width), F32),
    )
    scratch = [
        vm((kw, L), BF16), vm((T, width), F32), vm((L, width), BF16), vm((L, width), BF16), vm((nd, 8, width), F32),
        vm((nd * R, n2), BF16), vm((n, width), BF16), vm((T, n2), F32), vm((T, n), BF16), vm((n, L), BF16),
        vm((L, n2), BF16), vm((ns - 1, T, width), BF16), vm((ns - 1, T, width), BF16), vm((T, width), F32),
        vm((2, nz * R, L), BF16), vm((nz * R, n2), BF16), vm((nz * R, n2), BF16),
        vm((nz * piece, width), BF16), vm((nz * piece, width), BF16),
    ]
    sems = [DMA((ns,)), DMA((ns,)), DMA((nd,)), DMA((nd,))] + [DMA((ns,))] * 8 + [DMA((2,)), DMA((2,))]
    return pl.pallas_call(
        functools.partial(forward_kernel, ns, nd),
        out_shape=outs,
        in_specs=vmem(9),
        out_specs=vmem(len(outs)),
        scratch_shapes=scratch + sems + gather_sems(nz) * 4,
        compiler_params=pltpu.CompilerParams(
            collective_id=0, has_side_effects=True, vmem_limit_bytes=60 << 20
        ),
        cost_estimate=pl.CostEstimate(flops=28_000_000_000, bytes_accessed=30_000_000, transcendentals=6_000_000),
    )(x, gains, wqkv_mine, wout_mine, cot, gu_mine, dn_mine, cos, sin)


class Scatter:
    def __init__(self, at, pieces, inbox, final, out, sems):
        self.at, self.pieces, self.inbox, self.final, self.out = at, pieces, inbox, final, out
        self.send, self.recv, self.osend, self.orecv, self.local = sems
        self.rows = final.shape[0]

    def copy(self, j):
        at = self.at
        piece = self.pieces.at[block_of(at.z_index(j), self.rows)]
        return remote(piece, self.inbox.at[j - 1], self.send.at[j], self.recv.at[j], at.z_device(at.z_index(j)))

    def spread(self, j):
        at = self.at
        return remote(self.final, self.out.at[at.s], self.osend.at[j], self.orecv.at[j], at.seq_to(j))

    def keep(self):
        return pltpu.make_async_copy(self.final, self.out.at[self.at.s], self.local.at[0])

    def start(self):
        for j in range(1, self.at.nz):
            self.copy(j).start()

    def total(self):
        for j in range(1, self.at.nz):
            self.copy(j).wait_recv()
        acc = self.pieces[block_of(self.at.zz, self.rows), :].astype(F32)
        for j in range(1, self.at.nz):
            acc = acc + self.inbox[j - 1].astype(F32)
        self.final[...] = acc.astype(BF16)
        self.keep().start()
        for j in range(1, self.at.ns):
            self.spread(j).start()

    def drain(self):
        self.keep().wait()
        for j in range(1, self.at.ns):
            self.spread(j).wait()
        for j in range(1, self.at.nz):
            self.copy(j).wait_send()


def scatter_sems(ns, nz):
    return [DMA((nz,)), DMA((nz,)), DMA((ns,)), DMA((ns,)), DMA((1,))]


def backward_kernel(
    ns, nd, x, normed, projT, qT, kT, krows, vrows, inv, mixT, mrowsT, wout, wqkv, gsum, gres, osend, oown, guown,
    dnown, gsecond, cos, sin,
    outputs, gstream, guall, dnall, qkvall, outall, small,
    guz, guf, dnz, dnf, orecv, gmr, grows, gT, qrows, gk, gv, gqT, gprojT, gproj, nisend, nirecv, niown,
    qk2, qkr, qkown, qkz, qkf, go2, gor, gosend, gorecv, goown, goz, gof, sm0, sm1, sm2, sm3,
    os_, or_, ms, mr, nis, nir, ss, sr, gos, gorc, s1, r1, s2, r2, *sems,
):
    at = Place(ns, nd)
    s, d, nz, core = at.s, at.d, at.nz, at.core
    T, width = x.shape
    L = ns * T
    R = guf.shape[0]
    hq, hk = H // ns, KV // ns
    group = hq // hk
    qw, kw = hq * HD, hk * HD
    half = HD // 2
    own = block_of(s, T)
    at.greet()
    dn_sum = Scatter(at, dnown, dnz, dnf, dnall, sems[0:5])
    gu_sum = Scatter(at, guown, guz, guf, guall, sems[5:10])
    qkv_sum = Scatter(at, qkown, qkz, qkf, qkvall, sems[10:15])
    out_sum = Scatter(at, goown, goz, gof, outall, sems[15:20])
    dn_sum.start()
    gu_sum.start()

    rback = gres[...].astype(BF16)

    def mixed_back(p):
        return remote(gmr.at[p], grows.at[own], ms.at[p], mr.at[s], (d, p))

    for p in range(ns):
        gmr[p] = mm_nt(rback, wout[p * qw : (p + 1) * qw, :]).astype(BF16)
        pl.when(s != p)(mixed_back(p).start)
    grows[own, :] = gmr[s]

    for k in range(nd):
        go2[k % 2, (k // 2) * R : (k // 2 + 1) * R, :] = mm(mrowsT[k * R : (k + 1) * R, :], rback).astype(BF16)
    go_copy = remote(go2.at[1 - core], gor, ss.at[0], sr.at[0], at.sib)
    go_copy.start()
    for i in range(hk):
        qrows[i, :, :] = jnp.transpose(qT[i * group * HD : (i + 1) * group * HD, :])
    go_copy.wait_recv()
    cw = width // ns
    for p in range(ns):
        c = pl.ds(p * cw, cw)
        gosend[p] = (go2[core, :, c].astype(F32) + gor[:, c].astype(F32)).astype(BF16)

    for j in range(1, ns):
        src = at.seq_from(j)
        remote(gmr.at[0], grows.at[block_of(src, T)], ms.at[0], mr.at[src], (d, src)).wait_recv()
    for i in range(ns):
        rows = pl.ds(i * T, T)
        gT[:, rows] = jnp.transpose(grows[rows, :])

    def gout_copy(j):
        return remote(gosend.at[at.seq_to(j)[1]], gorecv.at[j - 1], gos.at[j], gorc.at[j], at.seq_to(j))

    def out_copy(j):
        return remote(osend.at[j - 1], orecv.at[ns - j - 1], os_.at[j], or_.at[ns - j], at.seq_to(ns - j))

    for j in range(1, ns):
        gout_copy(j).start()
    for j in range(1, ns):
        out_copy(j).start()

    causal = lax.broadcasted_iota(jnp.int32, (T, T), 0) <= lax.broadcasted_iota(jnp.int32, (T, T), 1)
    causal = jnp.concatenate([causal] * group, axis=1)
    gk[...] = jnp.zeros_like(gk)
    gv[...] = jnp.zeros_like(gv)

    def key_head(kv, carry):
        krow = block_of(kv, HD)
        lanes = block_of(kv, group * HD)
        for rb in range(ns):
            cols = pl.ds(rb * T, T)

            def side(ref):
                return jnp.concatenate(
                    [ref[block_of(kv * group + u, HD), cols] for u in range(group)], axis=1
                )

            q, g = side(qT), side(gT)
            one = jnp.concatenate([inv[kv * group + u, :, cols] for u in range(group)], axis=1)
            m = jnp.concatenate(
                [mixT[rb, block_of(kv * group + u, HD), :] for u in range(group)], axis=1
            )
            delta = jnp.sum(g.astype(F32) * m.astype(F32), axis=0, keepdims=True)
            gr, qr = grows[cols, lanes], qrows[kv, cols, :]
            gr = jnp.concatenate([gr[:, u * HD : (u + 1) * HD] for u in range(group)], axis=0)
            qr = jnp.concatenate([qr[:, u * HD : (u + 1) * HD] for u in range(group)], axis=0)
            gq = jnp.zeros((HD, group * T), F32)
            for part, masked in ((pl.ds(0, rb * T), False), (cols, True)):
                if rb == 0 and not masked:
                    continue
                p = jnp.exp(mm(krows[kv, part, :], q)) * one
                if masked:
                    p = jnp.where(causal, p, 0.0)
                gp = mm(vrows[kv, part, :], g)
                ds = (p * (gp - delta)).astype(BF16)
                gv[kv, part, :] += mm(p.astype(BF16), gr)
                gk[kv, part, :] += mm(ds, qr)
                gq = gq + mm(kT[krow, part], ds)
            gq = gq * HD**-0.5
            for u in range(group):
                gqT[block_of(kv * group + u, HD), cols] = gq[:, u * T : (u + 1) * T]
        return carry

    lax.fori_loop(0, hk, key_head, 0)

    columns = jnp.transpose(gsum[:, : 2 * HD])
    gain_q, gain_k = columns[:HD, 2:3], columns[HD:, 2:3]

    def norm_column(row, g, gain):
        a, b = g[:half], g[half:]
        g = jnp.concatenate([a * cos[...] + b * sin[...], b * cos[...] - a * sin[...]], axis=0)
        u = projT[row, :]
        scale = lax.rsqrt(jnp.mean(u * u, axis=0, keepdims=True) + EPSILON)
        us = u * scale
        weighted = g * gain
        inner = jnp.mean(weighted * us, axis=0, keepdims=True)
        gprojT[row, :] = (scale * (weighted - us * inner)).astype(BF16)
        return jnp.sum(g * us, axis=1, keepdims=True)

    def query_back(h, acc):
        row = block_of(h, HD)
        return acc + norm_column(row, gqT[row, :], gain_q)

    gain_grad_q = lax.fori_loop(0, hq, query_back, jnp.zeros((HD, 1), F32))
    gain_grad_k = jnp.zeros((HD, 1), F32)
    for i in range(hk):
        gain_grad_k = gain_grad_k + norm_column(pl.ds(qw + i * HD, HD), jnp.transpose(gk[i]), gain_k)
        gprojT[qw + kw + i * HD : qw + kw + (i + 1) * HD, :] = jnp.transpose(gv[i]).astype(BF16)

    def ni_copy(j):
        return remote(nisend.at[j - 1], nirecv.at[j - 1], nis.at[j], nir.at[j], at.seq_to(j))

    for i in range(ns):
        rows = pl.ds(i * T, T)
        gproj[rows, :] = jnp.transpose(gprojT[:, rows])
    for j in list(range(1, ns)) + [0]:
        part = mm_nt(gproj[block_of(at.seq_to(j)[1], T), :], wqkv[...])
        if j:
            nisend[j - 1] = part.astype(BF16)
            ni_copy(j).start()
        else:
            niown[...] = part
    for k in range(nd):
        part = mm(gprojT[...], normed[:, k * R : (k + 1) * R])
        qk2[k % 2, (k // 2) * R : (k // 2 + 1) * R, :] = jnp.transpose(part).astype(BF16)
    qk_copy = remote(qk2.at[1 - core], qkr, ss.at[1], sr.at[1], at.sib)
    qk_copy.start()
    for j in range(1, ns):
        gout_copy(j).wait_recv()
    acc = gosend[s].astype(F32)
    for j in range(1, ns):
        acc = acc + gorecv[j - 1].astype(F32)
    goown[...] = acc.astype(BF16)
    out_sum.start()
    qk_copy.wait_recv()
    qkown[...] = (qk2[core].astype(F32) + qkr[...].astype(F32)).astype(BF16)
    qkv_sum.start()
    dn_sum.total()

    for j in range(1, ns):
        ni_copy(j).wait_recv()
    gni = niown[...]
    for j in range(1, ns):
        gni = gni + nirecv[j - 1].astype(F32)
    stream = x[...].astype(F32)
    scale = lax.rsqrt(jnp.mean(stream * stream, axis=-1, keepdims=True) + EPSILON)
    unit = stream * scale
    weighted = gni * gsum[0:1, :]
    gstream[...] = gres[...] + scale * (weighted - unit * jnp.mean(weighted * unit, axis=-1, keepdims=True))
    first = jnp.sum(gni * unit, axis=0, keepdims=True)
    qk = jnp.broadcast_to(jnp.concatenate([gain_grad_q, gain_grad_k], axis=0), (2 * HD, 128))
    sm0[0:1, :] = first
    sm0[1:2, :] = gsecond[0:1, :]
    sm0[2:8, :] = jnp.zeros((6, width), F32)
    sm0[2:3, : 2 * HD] = jnp.transpose(qk)[0:1, :]

    def small_seq(j):
        return remote(sm0, sm1.at[j - 1], s1.at[j], r1.at[j], at.seq_to(j))

    def small_dp(j):
        return remote(sm2, sm3.at[j - 1], s2.at[j], r2.at[j], at.dp_to(j))

    for j in range(1, ns):
        small_seq(j).start()
    for j in range(1, ns):
        out_copy(j).wait_recv()
    acc = oown[...]
    for j in range(1, ns):
        acc = acc + orecv[j - 1].astype(F32)
    outputs[...] = acc.astype(BF16)
    for j in range(1, ns):
        small_seq(j).wait_recv()
    acc = sm0[...]
    for j in range(1, ns):
        acc = acc + sm1[j - 1]
    sm2[...] = acc
    for j in range(1, nd):
        small_dp(j).start()
    out_sum.total()
    qkv_sum.total()
    gu_sum.total()
    for j in range(1, nd):
        small_dp(j).wait_recv()
    for j in range(1, nd):
        acc = acc + sm3[j - 1]
    small[...] = acc

    for p in range(ns):
        pl.when(s != p)(mixed_back(p).wait_send)
    go_copy.wait_send()
    qk_copy.wait_send()
    for j in range(1, ns):
        gout_copy(j).wait_send()
        out_copy(j).wait_send()
        ni_copy(j).wait_send()
        small_seq(j).wait_send()
    for j in range(1, nd):
        small_dp(j).wait_send()
    for t in (dn_sum, out_sum, qkv_sum, gu_sum):
        t.drain()


def backward(ns, nd, piece, x, normed, projT, qT, kT, krows, vrows, inv, mixT, mrowsT, wout, wqkv, gsum, gres, osend,
             oown, guown, dnown, gsecond):
    T, width = x.shape
    L = ns * T
    nz = nd // 2
    n2 = guown.shape[1]
    R = guown.shape[0] // nz
    hq, hk = H // ns, KV // ns
    qw, kw = hq * HD, hk * HD
    pw = qw + 2 * kw
    cw = width // ns
    cos, sin = rope_columns(L)
    sh, vm = jax.ShapeDtypeStruct, pltpu.VMEM
    outs = (
        sh((T, width), BF16), sh((T, width), F32), sh((ns, R, n2), BF16), sh((ns, piece, width), BF16),
        sh((ns, R, pw), BF16), sh((ns, R, cw), BF16), sh((8, width), F32),
    )
    hbm = pl.BlockSpec(memory_space=pl.ANY)
    scratch = [
        vm((nz - 1, R, n2), BF16), vm((R, n2), BF16), vm((nz - 1, piece, width), BF16), vm((piece, width), BF16),
        vm((ns - 1, T, width), BF16), vm((ns, T, qw), BF16), vm((L, qw), BF16), vm((qw, L), BF16),
        vm((hk, L, qw // hk), BF16), vm((hk, L, HD), F32), vm((hk, L, HD), F32), vm((qw, L), F32), vm((pw, L), BF16),
        vm((L, pw), BF16), vm((ns - 1, T, width), BF16), vm((ns - 1, T, width), BF16), vm((T, width), F32),
        vm((2, nz * R, pw), BF16), vm((nz * R, pw), BF16), vm((nz * R, pw), BF16), vm((nz - 1, R, pw), BF16),
        vm((R, pw), BF16), vm((2, nz * R, width), BF16), vm((nz * R, width), BF16), vm((ns, nz * R, cw), BF16),
        vm((ns - 1, nz * R, cw), BF16), vm((nz * R, cw), BF16), vm((nz - 1, R, cw), BF16), vm((R, cw), BF16),
        vm((8, width), F32), vm((ns - 1, 8, width), F32), vm((8, width), F32), vm((nd - 1, 8, width), F32),
    ]
    sems = [DMA((ns,))] * 6 + [DMA((2,)), DMA((2,))] + [DMA((ns,))] * 4 + [DMA((nd,)), DMA((nd,))]
    return pl.pallas_call(
        functools.partial(backward_kernel, ns, nd),
        out_shape=outs,
        in_specs=vmem(21),
        out_specs=vmem(2) + [hbm] * 4 + vmem(1),
        scratch_shapes=scratch + sems + scatter_sems(ns, nz) * 4,
        compiler_params=pltpu.CompilerParams(
            collective_id=1, has_side_effects=True, vmem_limit_bytes=60 << 20
        ),
        cost_estimate=pl.CostEstimate(flops=10_000_000_000, bytes_accessed=30_000_000, transcendentals=6_000_000),
    )(x, normed, projT, qT, kT, krows, vrows, inv, mixT, mrowsT, wout, wqkv, gsum, gres, osend, oown, guown, dnown,
      gsecond, cos, sin)


def finish_kernel(ns, nd, piece, guall, qkvall, outall, gate, up, qkv, out):
    hq, hk = H // ns, KV // ns
    qw, kw = hq * HD, hk * HD
    pad = guall.shape[2] // 2 // nd
    parts = [guall[i].astype(F32) for i in range(ns)]
    for ref, base in ((gate, 0), (up, nd * pad)):
        ref[...] = jnp.concatenate(
            [parts[i][:, base + k * pad : base + k * pad + piece] for k in range(nd) for i in range(ns)], axis=1
        )
    parts = [qkvall[i].astype(F32) for i in range(ns)]
    qkv[...] = jnp.concatenate(
        [p[:, :qw] for p in parts] + [p[:, qw : qw + kw] for p in parts] + [p[:, qw + kw :] for p in parts], axis=1
    )
    out[...] = jnp.concatenate([outall[i].astype(F32) for i in range(ns)], axis=1)


def finish(ns, nd, piece, guall, qkvall, outall):
    R = guall.shape[1]
    rows = R // 4
    ff = ns * nd * piece
    widths = (ff, ff, ns * qkvall.shape[2], ns * outall.shape[2])
    return pl.pallas_call(
        functools.partial(finish_kernel, ns, nd, piece),
        grid=(4,),
        out_shape=[jax.ShapeDtypeStruct((R, w), F32) for w in widths],
        in_specs=[pl.BlockSpec((ns, rows, a.shape[2]), lambda i: (0, i, 0)) for a in (guall, qkvall, outall)],
        out_specs=[pl.BlockSpec((rows, w), lambda i: (i, 0)) for w in widths],
        compiler_params=pltpu.CompilerParams(vmem_limit_bytes=40 << 20),
    )(guall, qkvall, outall)


def shards(inputs, cotangent, first_gain, w_qkv, qk_gain, w_out, second_gain, w_gate, w_up, w_down):
    width = inputs.shape[2]
    ns, nd = lax.axis_size("seq"), lax.axis_size("dp")
    s, d = lax.axis_index("seq"), lax.axis_index("dp")
    qw, kw = H // ns * HD, KV // ns * HD
    piece = w_down.shape[0] // ns
    pad = -piece % 16

    qkv_mine = jnp.concatenate(
        [
            lax.dynamic_slice_in_dim(w_qkv, s * qw, qw, 1),
            lax.dynamic_slice_in_dim(w_qkv, H * HD + s * kw, kw, 1),
            lax.dynamic_slice_in_dim(w_qkv, (H + KV) * HD + s * kw, kw, 1),
        ],
        axis=1,
    )

    def slice_ff(w):
        w = w.reshape(w.shape[0], nd, ns, piece)[:, :, s, :]
        return jnp.pad(w, ((0, 0), (0, 0), (0, pad))).reshape(w.shape[0], nd * (piece + pad))

    gu_mine = jnp.concatenate([slice_ff(w_gate), slice_ff(w_up)], axis=1)
    dn_mine = jnp.pad(lax.dynamic_slice_in_dim(w_down, s * piece, piece, 0), ((0, pad), (0, 0)))
    gains = jnp.zeros((8, width), F32)
    gains = lax.dynamic_update_slice(gains, first_gain[None], (0, d * first_gain.shape[0]))
    gains = lax.dynamic_update_slice(gains, second_gain[None], (1, d * second_gain.shape[0]))
    gains = lax.dynamic_update_slice(gains, qk_gain[None], (2, d * qk_gain.shape[0]))
    x = inputs[0]
    kept = forward(ns, nd, x, gains, qkv_mine, w_out, cotangent[0], gu_mine, dn_mine)
    outputs, gstream, guall, dnall, qkvall, outall, small = backward(ns, nd, piece + pad, x, *kept)
    gate, up, qkv, out = finish(ns, nd, piece, guall, qkvall, outall)
    down = dnall[:, :piece].reshape(w_down.shape).astype(F32)
    gl, ql = first_gain.shape[0], qk_gain.shape[0]
    first = lax.dynamic_slice(small, (0, d * gl), (1, gl))[0]
    second = lax.dynamic_slice(small, (1, d * gl), (1, gl))[0]
    qk = lax.dynamic_slice(small, (2, d * ql), (1, ql))[0]
    return (outputs[None], gstream[None], first, qkv, qk, out, second, gate, up, down)


def solution(mesh):
    act = P("dp", "seq", None)
    vec, mat = P("dp"), P("dp", None)
    in_specs = (act, act, vec, mat, vec, mat, vec, mat, mat, mat)
    out_specs = (act, act, vec, mat, vec, mat, vec, mat, mat, mat)
    return jax.shard_map(shards, mesh=mesh, in_specs=in_specs, out_specs=out_specs, check_vma=False)
```

```python
import functools

import jax
import jax.numpy as jnp
import numpy as np
from jax import lax
from jax.experimental import pallas as pl
from jax.experimental.pallas import tpu as pltpu
from jax.sharding import PartitionSpec as P

H = 16
KV = 8
HD = 64
EPSILON = 1e-06
THETA_BASE = 1000000.0
F32 = jnp.float32
BF16 = jnp.bfloat16
VMEM_LIMIT = 61 << 20


def rope_columns(length):
    inverse = np.float32(THETA_BASE) ** (-np.arange(0, HD, 2).astype(np.float32) / np.float32(HD))
    angles = (np.arange(length, dtype=np.float32)[None, :] * inverse.astype(np.float32)[:, None]).astype(np.float32)
    angles = angles.astype(np.float64)
    return jnp.asarray(np.cos(angles), F32), jnp.asarray(np.sin(angles), F32)


MESH = pl.DeviceIdType.MESH
DMA = pltpu.SemaphoreType.DMA


def mm(a, b):
    return jnp.dot(a, b, preferred_element_type=F32)


def mm_nt(a, b):
    return lax.dot_general(a, b, (((1,), (1,)), ((), ())), preferred_element_type=F32)


def remote(src, dst, send, recv, device):
    return pltpu.make_async_remote_copy(
        src_ref=src, dst_ref=dst, send_sem=send, recv_sem=recv, device_id=device, device_id_type=MESH
    )


def block_of(index, size):
    return pl.ds(pl.multiple_of(index * size, size), size)


class Place:
    def __init__(self, ns, nd):
        self.ns, self.nd, self.nz = ns, nd, nd // 2
        self.d, self.s = lax.axis_index("dp"), lax.axis_index("seq")
        self.zz, self.core = self.d // 2, lax.rem(self.d, 2)
        self.sib = (self.d + 1 - 2 * self.core, self.s)

    def seq_to(self, j):
        return (self.d, lax.rem(self.s + j, self.ns))

    def seq_from(self, j):
        return lax.rem(self.s + self.ns - j, self.ns)

    def dp_to(self, j):
        return (lax.rem(self.d + j, self.nd), self.s)

    def z_index(self, j):
        return lax.rem(self.zz + j, self.nz)

    def z_from(self, j):
        return lax.rem(self.zz + self.nz - j, self.nz)

    def z_device(self, z):
        return (2 * z + self.core, self.s)

    def greet(self):
        bar = pltpu.get_barrier_semaphore()
        for j in range(1, self.nd):
            pl.semaphore_signal(bar, inc=1, device_id=self.dp_to(j), device_id_type=MESH)
        for j in range(1, self.ns):
            pl.semaphore_signal(bar, inc=1, device_id=self.seq_to(j), device_id_type=MESH)
        pl.semaphore_wait(bar, self.nd + self.ns - 2)


class Gather:
    def __init__(self, at, src, dst, sems, relayed=True):
        self.at, self.src, self.dst, self.relayed = at, src, dst, relayed
        self.send, self.recv, self.fsend, self.frecv, self.rsend, self.local = sems
        self.rows = src.shape[0]

    def piece(self, z):
        return self.dst.at[block_of(2 * z + self.at.core, self.rows)]

    def direct(self, j):
        at = self.at
        return remote(self.src, self.piece(at.zz), self.send.at[j], self.recv.at[j], at.z_device(at.z_index(j)))

    def near(self, j):
        at = self.at
        away = at.z_index(j) - at.zz
        return (away < at.nz - 1) & (away > 1 - at.nz) if self.relayed else away != 0

    def across(self, j):
        piece = self.src if j == 0 else self.piece(self.at.z_from(j))
        return remote(piece, self.piece(self.at.z_from(j)), self.fsend.at[j], self.frecv.at[j], self.at.sib)

    def relay(self, j):
        nz = self.at.nz
        legs = []
        if not self.relayed:
            return legs
        if j == nz - 2:
            legs.append((nz - 2, 0, nz - 1, nz - 1, 0))
        if j == 2:
            legs.append((1, nz - 1, 0, 1, 1))
        out = []
        for here, origin, target, index, k in legs:
            piece = self.piece(origin)
            copy = remote(piece, piece, self.rsend.at[k], self.recv.at[index], self.at.z_device(target))
            out.append((self.at.zz == here, copy))
        return out

    def order(self):
        nz = self.at.nz
        return list(range(2, nz - 1)) + [1, nz - 1]

    def start(self):
        at = self.at
        for j in range(1, at.nz):

            @pl.when(self.near(j))
            def _():
                self.direct(j).start()

        self.across(0).start()
        self.mine().start()

    def mine(self):
        return pltpu.make_async_copy(self.src, self.dst.at[block_of(self.at.d, self.rows)], self.local.at[0])

    def arrive(self):
        for j in self.order():
            self.direct(j).wait_recv()
            for here, copy in self.relay(j):
                pl.when(here)(copy.start)
            self.across(j).start()

    def finish(self):
        for j in range(self.at.nz):
            self.across(j).wait_recv()
        self.mine().wait()

    def drain(self):
        for j in range(self.at.nz):
            self.across(j).wait_send()
            if j:
                pl.when(self.near(j))(self.direct(j).wait_send)
                for here, copy in self.relay(j):
                    pl.when(here)(copy.wait_send)


def gather_sems(nz):
    return [DMA((nz,)), DMA((nz,)), DMA((nz,)), DMA((nz,)), DMA((2,)), DMA((1,))]


class Scatter:
    def __init__(self, at, pieces, inbox, final, out, sems):
        self.at, self.pieces, self.inbox, self.final, self.out = at, pieces, inbox, final, out
        self.send, self.recv, self.osend, self.orecv, self.local = sems
        self.rows = final.shape[0]

    def copy(self, j):
        at = self.at
        piece = self.pieces.at[block_of(at.z_index(j), self.rows)]
        return remote(piece, self.inbox.at[j - 1], self.send.at[j], self.recv.at[j], at.z_device(at.z_index(j)))

    def spread(self, j):
        at = self.at
        return remote(self.final, self.out.at[at.s], self.osend.at[j], self.orecv.at[j], at.seq_to(j))

    def keep(self):
        return pltpu.make_async_copy(self.final, self.out.at[self.at.s], self.local.at[0])

    def start(self):
        for j in range(1, self.at.nz):
            self.copy(j).start()

    def total(self):
        for j in range(1, self.at.nz):
            self.copy(j).wait_recv()
        acc = self.pieces[block_of(self.at.zz, self.rows), :].astype(F32)
        for j in range(1, self.at.nz):
            acc = acc + self.inbox[j - 1].astype(F32)
        self.final[...] = acc.astype(BF16)
        self.keep().start()
        for j in range(1, self.at.ns):
            self.spread(j).start()

    def drain(self):
        self.keep().wait()
        for j in range(1, self.at.ns):
            self.spread(j).wait()
        for j in range(1, self.at.nz):
            self.copy(j).wait_send()


def scatter_sems(ns, nz):
    return [DMA((nz,)), DMA((nz,)), DMA((ns,)), DMA((ns,)), DMA((1,))]


def block_kernel(
    ns, nd, x, gain1, gain2, gainqk, wqkv_rows, wout_mine, cot, wgate, wup, wdown, cos, sin,
    outputs, gstream, gateall, upall, dnall, qkvall, outall, small,
    normed, projT, qT, kT, krows, vrows, inv, mixT, mrowsT, wout, wqkv, gsum, osend, oown, gsecond,
    vT, resid, cotall, xall, gains, gbuf, wqkv_mine, gu_mine, gu, dn, hrow, hT, gb, gsend, grecv, gown, nmT,
    gur, uur, dnr,
    gaz, gaf, upz, upf, dnz, dnf, gmr, grows, qrows, gk, gv, gqT, qkr, qkown, qkz, qkf,
    gor, gorecv, goown, goz, gof, sm0, sm1, sm2, sm3,
    xs, xr, gs, gr, cs, cr, ms, mr, ns_, nr, ps, pr, ss, sr, loc, wl,
    os_, or_, bs, br, nis, nir, ss2, sr2, gos, gorc, s1, r1, s2, r2, *sems,
):
    at = Place(ns, nd)
    s, d, nz, core = at.s, at.d, at.nz, at.core
    T, width = x.shape
    L = ns * T
    R = wqkv_mine.shape[0]
    cw = width // ns
    n = dn.shape[0]
    piece = n // nd
    gl, ql = gain1.shape[1], gainqk.shape[1]
    dn_mine = wdown.at[block_of(s, piece)] if wdown.shape[0] == ns * piece else wdown
    hq, hk = H // ns, KV // ns
    group = hq // hk
    qw, kw = hq * HD, hk * HD
    own = block_of(s, T)
    pw = qw + 2 * kw
    gains[...] = jnp.zeros_like(gains)
    gains[0:1, :gl] = gain1[...]
    gains[1:2, :gl] = gain2[...]
    gains[2:3, :ql] = gainqk[...]
    for i in range(ns):

        @pl.when(s == i)
        def _():
            cuts = ((i * qw, qw), (H * HD + i * kw, kw), ((H + KV) * HD + i * kw, kw))
            wqkv_mine[...] = jnp.concatenate([wqkv_rows[:, a : a + b] for a, b in cuts], axis=1)

    at.greet()

    x_copies = [remote(x, xall.at[own], xs.at[j], xr.at[j], at.seq_to(j)) for j in range(1, ns)]
    g_copies = [remote(gains, gbuf.at[d], gs.at[j], gr.at[j], at.dp_to(j)) for j in range(1, nd)]
    c_copies = [remote(cot, cotall.at[own], cs.at[j], cr.at[j], at.seq_to(j)) for j in range(1, ns)]
    take_qkv = Gather(at, wqkv_mine, wqkv, sems[0:6], relayed=False)
    take_out = Gather(at, wout_mine, wout, sems[6:12], relayed=False)
    take_gu = Gather(at, gu_mine, gu, sems[12:18])
    take_dn = Gather(at, dn_mine, dn, sems[18:24])
    for c in g_copies + x_copies:
        c.start()
    take_qkv.start()
    take_out.start()
    xall[own, :] = x[...]
    gbuf[d] = gains[...]
    cot_local = pltpu.make_async_copy(cot, cotall.at[own], loc.at[0])
    cot_local.start()
    ff = wgate.shape[1]
    parts = max(1, -(-ff // (2 * n)))
    while nd % parts:
        parts += 1
    span = ff // parts
    stage = []
    for i, w in enumerate((wgate, wup)):
        for k in range(parts):
            row = pl.ds((i * parts + k) * R, R)
            stage.append(
                pltpu.make_async_copy(w.at[:, pl.ds(k * span, span)], gb.at[row, pl.ds(0, span)], wl.at[i, k])
            )
    for c in stage:
        c.start()
    for c in stage:
        c.wait()
    real = wgate.shape[1] // nd // ns
    gap = [jnp.zeros((R, piece - real), BF16)] if piece > real else []
    for i in range(ns):

        @pl.when(s == i)
        def _():
            cuts = []
            for w in range(2):
                for k in range(nd):
                    a = (k * ns + i) * real
                    row = (w * parts + a // span) * R
                    cuts += [gb[row : row + R, a % span : a % span + real]] + gap
            gu_mine[...] = jnp.concatenate(cuts, axis=1)

    for c in g_copies:
        c.wait_recv()
    gain_in = jnp.concatenate([gbuf[k][0:1, :gl] for k in range(nd)], axis=1)
    gain_mid = jnp.concatenate([gbuf[k][1:2, :gl] for k in range(nd)], axis=1)
    gain_qk = jnp.concatenate([gbuf[k][2:3, :ql] for k in range(nd)], axis=1)
    gsum[...] = jnp.zeros_like(gsum)
    gsum[0:1, :] = gain_in
    gsum[1:2, :] = gain_mid
    gsum[2:3, : 2 * HD] = gain_qk
    columns = jnp.transpose(jnp.broadcast_to(gain_qk, (8, 2 * HD)))
    gain_q, gain_k = columns[:HD, 0:1], columns[HD:, 0:1]
    for j in range(ns):
        rows = block_of(at.seq_from(j), T)
        if j:
            x_copies[j - 1].wait_recv()
        xc = xall[rows, :].astype(F32)
        scale = lax.rsqrt(jnp.mean(xc * xc, axis=-1, keepdims=True) + EPSILON)
        normed[rows, :] = (xc * scale * gain_in).astype(BF16)
    for c in c_copies:
        c.start()
    take_qkv.arrive()
    take_qkv.finish()
    for j in range(ns):
        rows = pl.ds(j * T, T)
        proj = mm(normed[rows, :], wqkv[...])
        projT[:, rows] = jnp.transpose(proj[:, : qw + kw])
        val = proj[:, qw + kw :]
        vT[:, rows] = jnp.transpose(val).astype(BF16)
        for i in range(hk):
            vrows[i, rows, :] = val[:, i * HD : (i + 1) * HD].astype(BF16)

    half = HD // 2

    def rope(row, gain, factor):
        u = projT[row, :]
        scale = lax.rsqrt(jnp.mean(u * u, axis=0, keepdims=True) + EPSILON)
        u = u * scale * gain
        a, b = u[:half], u[half:]
        return jnp.concatenate([a * cos[...] - b * sin[...], b * cos[...] + a * sin[...]], axis=0) * factor

    def rope_query(h, carry):
        row = block_of(h, HD)
        qT[row, :] = rope(row, gain_q, HD**-0.5).astype(BF16)
        return carry

    lax.fori_loop(0, hq, rope_query, 0)
    for i in range(hk):
        r = rope(pl.ds(qw + i * HD, HD), gain_k, 1.0)
        kT[i * HD : (i + 1) * HD, :] = r.astype(BF16)
        krows[i, :, :] = jnp.transpose(r).astype(BF16)

    keep = lax.broadcasted_iota(jnp.int32, (T, T), 0) <= lax.broadcasted_iota(jnp.int32, (T, T), 1)
    block = block_of(s, qw)

    def mixed_out(rb):
        return remote(mixT.at[rb], mrowsT.at[block], ms.at[rb], mr.at[s], (d, rb))

    for rb in range(ns):
        cols = pl.ds(rb * T, T)
        span = rb * T

        def head(h, carry):
            kv = h // group
            row, vrow = block_of(h, HD), block_of(kv, HD)
            q = qT[row, cols]
            p = jnp.where(keep, jnp.exp(mm(krows[kv, cols, :], q)), 0.0)
            tot = jnp.sum(p, axis=0, keepdims=True)
            m = mm(vT[vrow, cols], p.astype(BF16))
            if span:
                p = jnp.exp(mm(krows[kv, 0:span, :], q))
                tot = tot + jnp.sum(p, axis=0, keepdims=True)
                m = m + mm(vT[vrow, 0:span], p.astype(BF16))
            one = 1.0 / tot
            inv[h, :, cols] = one
            mixT[rb, row, :] = (m * one).astype(BF16)
            return carry

        lax.fori_loop(0, hq, head, 0)
        pl.when(s != rb)(mixed_out(rb).start)
        if rb == 0:
            take_gu.start()
        if rb == ns - 1:
            take_out.arrive()

    mrowsT[block, :] = mixT[s]
    for j in range(1, ns):
        src = at.seq_from(j)
        remote(mixT.at[0], mrowsT.at[block_of(src, qw)], ms.at[0], mr.at[src], (d, src)).wait_recv()
    take_out.finish()
    residual = x[...].astype(F32) + mm(jnp.transpose(mrowsT[...]), wout[...])
    resid[...] = residual
    scale_mid = lax.rsqrt(jnp.mean(residual * residual, axis=-1, keepdims=True) + EPSILON)
    xall[own, :] = (residual * scale_mid * gain_mid).astype(BF16)
    n_copies = [
        remote(xall.at[own], xall.at[own], ns_.at[j], nr.at[j], at.seq_to(j)) for j in range(1, ns)
    ]
    for c in n_copies:
        c.start()
    take_dn.start()
    take_gu.arrive()
    take_gu.finish()

    ft = 384 if n % 384 == 0 else 128
    nt = n // ft
    wt = 256
    for j in range(ns):
        rows = block_of(at.seq_from(j), T)
        if j:
            n_copies[j - 1].wait_recv()

        def pre_tile(i, carry):
            f = block_of(i, ft)
            gb[rows, f] = mm(xall[rows, :], gu[:, f]).astype(BF16)
            return carry

        lax.fori_loop(0, 2 * nt, pre_tile, 0)
    for c in c_copies:
        c.wait_recv()
    cot_local.wait()
    take_dn.arrive()
    take_dn.finish()
    p_copies = []
    for j in range(ns):
        rows = block_of(at.seq_from(j), T)

        def hidden_tile(i, carry):
            f, f2 = block_of(i, ft), block_of(i + nt, ft)
            gate, up = gb[rows, f].astype(F32), gb[rows, f2].astype(F32)
            sig = 1.0 / (1.0 + jnp.exp(-gate))
            act = gate * sig
            back = mm_nt(cotall[rows, :], dn[f, :])
            hid = act * up
            hrow[:, f] = hid.astype(BF16)
            hT[f, rows] = jnp.transpose(hid).astype(BF16)
            gb[rows, f] = (back * up * sig * (1.0 + gate * (1.0 - sig))).astype(BF16)
            gb[rows, f2] = (back * act).astype(BF16)
            return carry

        lax.fori_loop(0, nt, hidden_tile, 0)

        def back_tile(i, carry):
            w = block_of(i, wt)
            part = mm_nt(gb[rows, :], gu[w, :])
            if j:
                gsend[j - 1, :, w] = part.astype(BF16)
            else:
                gown[:, w] = part
            return carry

        lax.fori_loop(0, width // wt, back_tile, 0)
        if j:
            c = remote(gsend.at[j - 1], grecv.at[ns - j - 1], ps.at[j], pr.at[ns - j], at.seq_to(ns - j))
            c.start()
            p_copies.append(c)

        def out_tile(i, carry):
            w = block_of(i, wt)
            part = mm(hrow[...], dn[:, w])
            if j:
                osend[j - 1, :, w] = part.astype(BF16)
            else:
                oown[:, w] = part + resid[:, w]
            return carry

        lax.fori_loop(0, width // wt, out_tile, 0)

    for c in n_copies:
        c.wait_send()
    take_gu.drain()
    take_dn.drain()
    for k in range(nd):
        nmT[k % 2, (k // 2) * R : (k // 2 + 1) * R, :] = jnp.transpose(xall[:, k * R : (k + 1) * R])

    half_gu, half_dn = nz * R, nz * piece
    dns, dnown = dn.at[pl.ds(0, half_dn)], dn.at[pl.ds(half_dn, half_dn)]
    gus, gateown = (gu.at[pl.ds(i * half_gu, half_gu), pl.ds(0, n)] for i in range(2))
    uus, upown = (gu.at[pl.ds(i * half_gu, half_gu), pl.ds(n, n)] for i in range(2))

    def dn_rows(c, i):
        return hT[block_of(2 * i + c, piece), :]

    tiles = nt
    tw = n // tiles

    def other(buf, base):
        def tile(i, carry):
            f = block_of(i, tw)
            buf[:, f] = mm(nmT[1 - core], gb[:, pl.ds(pl.multiple_of(base + i * tw, 128), tw)]).astype(BF16)
            return carry

        lax.fori_loop(0, tiles, tile, 0)

    def summed(buf, got, base):
        def tile(i, carry):
            f = block_of(i, tw)
            part = mm(nmT[core], gb[:, pl.ds(pl.multiple_of(base + i * tw, 128), tw)])
            buf[:, f] = (part + got[:, f].astype(F32)).astype(BF16)
            return carry

        lax.fori_loop(0, tiles, tile, 0)

    dn_copy = remote(dns, dnr, ss.at[0], sr.at[0], at.sib)
    gate_copy = remote(gus, gur, ss.at[1], sr.at[1], at.sib)
    up_copy = remote(uus, uur, ss.at[2], sr.at[2], at.sib)

    def dn_other(i, carry):
        dns[block_of(i, piece), :] = mm(dn_rows(1 - core, i), cotall[...]).astype(BF16)
        return carry

    lax.fori_loop(0, nz, dn_other, 0)
    dn_copy.start()
    other(gus, 0)
    gate_copy.start()
    other(uus, n)
    up_copy.start()
    dn_copy.wait_recv()

    def dn_mine_sum(i, carry):
        r = block_of(i, piece)
        dnown[r, :] = (mm(dn_rows(core, i), cotall[...]) + dnr[r, :].astype(F32)).astype(BF16)
        return carry

    lax.fori_loop(0, nz, dn_mine_sum, 0)
    gate_copy.wait_recv()
    summed(gateown, gur, 0)
    up_copy.wait_recv()
    summed(upown, uur, n)

    for c in p_copies:
        c.wait()
    gnm = gown[...]
    for j in range(1, ns):
        gnm = gnm + grecv[j - 1].astype(F32)
    residual = resid[...]
    scale_mid = lax.rsqrt(jnp.mean(residual * residual, axis=-1, keepdims=True) + EPSILON)
    gsecond[...] = jnp.broadcast_to(jnp.sum(gnm * residual * scale_mid, axis=0, keepdims=True), (8, width))
    weighted = gnm * gain_mid
    gown[...] = (
        cotall[own, :].astype(F32)
        + scale_mid * weighted
        - residual * (scale_mid * scale_mid * scale_mid) * jnp.mean(weighted * residual, axis=-1, keepdims=True)
    )
    dn_sum = Scatter(at, dnown, dnz, dnf, dnall, sems[24:29])
    gate_sum = Scatter(at, gateown, gaz, gaf, gateall, sems[29:34])
    up_sum = Scatter(at, upown, upz, upf, upall, sems[44:49])
    qkv_sum = Scatter(at, qkown, qkz, qkf, qkvall, sems[34:39])
    out_sum = Scatter(at, goown, goz, gof, outall, sems[39:44])
    dn_sum.start()
    gate_sum.start()

    rback = gown[...].astype(BF16)

    def mixed_back(p):
        return remote(gmr.at[p], grows.at[own], bs.at[p], br.at[s], (d, p))

    for p in range(ns):
        gmr[p] = mm_nt(rback, wout[p * qw : (p + 1) * qw, :]).astype(BF16)
        pl.when(s != p)(mixed_back(p).start)
    grows[own, :] = gmr[s]

    for k in range(nd):
        nmT[k % 2, (k // 2) * R : (k // 2 + 1) * R, :] = mm(mrowsT[k * R : (k + 1) * R, :], rback).astype(BF16)
    go_copy = remote(nmT.at[1 - core], gor, ss2.at[0], sr2.at[0], at.sib)
    go_copy.start()
    for i in range(hk):
        qrows[i, :, :] = jnp.transpose(qT[i * group * HD : (i + 1) * group * HD, :])
    go_copy.wait_recv()
    gate_copy.wait_send()
    up_copy.wait_send()
    for p in range(ns):
        c = pl.ds(p * cw, cw)
        gu[0:half_gu, c] = (nmT[core, :, c].astype(F32) + gor[:, c].astype(F32)).astype(BF16)

    for j in range(1, ns):
        src = at.seq_from(j)
        remote(gmr.at[0], grows.at[block_of(src, T)], bs.at[0], br.at[src], (d, src)).wait_recv()
    for i in range(ns):
        rows = pl.ds(i * T, T)
        hT[pw : pw + qw, rows] = jnp.transpose(grows[rows, :])

    def gout_copy(j):
        return remote(gu.at[pl.ds(0, half_gu), block_of(at.seq_to(j)[1], cw)], gorecv.at[j - 1], gos.at[j], gorc.at[j], at.seq_to(j))

    def out_copy(j):
        return remote(osend.at[j - 1], xall.at[pl.ds((ns - j - 1) * T, T)], os_.at[j], or_.at[ns - j], at.seq_to(ns - j))

    for j in range(1, ns):
        gout_copy(j).start()

    causal = lax.broadcasted_iota(jnp.int32, (T, T), 0) <= lax.broadcasted_iota(jnp.int32, (T, T), 1)
    causal = jnp.concatenate([causal] * group, axis=1)
    gk[...] = jnp.zeros_like(gk)
    gv[...] = jnp.zeros_like(gv)

    def key_head(kv, carry):
        krow = block_of(kv, HD)
        lanes = block_of(kv, group * HD)
        for rb in range(ns):
            cols = pl.ds(rb * T, T)

            def side(ref, base):
                return jnp.concatenate(
                    [ref[pl.ds(pl.multiple_of(base + (kv * group + u) * HD, HD), HD), cols] for u in range(group)],
                    axis=1,
                )

            q, g = side(qT, 0), side(hT, pw)
            one = jnp.concatenate([inv[kv * group + u, :, cols] for u in range(group)], axis=1)
            m = jnp.concatenate(
                [mixT[rb, block_of(kv * group + u, HD), :] for u in range(group)], axis=1
            )
            delta = jnp.sum(g.astype(F32) * m.astype(F32), axis=0, keepdims=True)
            gr, qr = grows[cols, lanes], qrows[kv, cols, :]
            gr = jnp.concatenate([gr[:, u * HD : (u + 1) * HD] for u in range(group)], axis=0)
            qr = jnp.concatenate([qr[:, u * HD : (u + 1) * HD] for u in range(group)], axis=0)
            gq = jnp.zeros((HD, group * T), F32)
            for part, masked in ((pl.ds(0, rb * T), False), (cols, True)):
                if rb == 0 and not masked:
                    continue
                p = jnp.exp(mm(krows[kv, part, :], q)) * one
                if masked:
                    p = jnp.where(causal, p, 0.0)
                gp = mm(vrows[kv, part, :], g)
                ds = (p * (gp - delta)).astype(BF16)
                gv[kv, part, :] += mm(p.astype(BF16), gr)
                gk[kv, part, :] += mm(ds, qr)
                gq = gq + mm(kT[krow, part], ds)
            gq = gq * HD**-0.5
            for u in range(group):
                gqT[block_of(kv * group + u, HD), cols] = gq[:, u * T : (u + 1) * T]
        return carry

    lax.fori_loop(0, hk, key_head, 0)

    columns = jnp.transpose(gsum[:, : 2 * HD])
    gain_q, gain_k = columns[:HD, 2:3], columns[HD:, 2:3]

    def norm_column(row, g, gain):
        a, b = g[:half], g[half:]
        g = jnp.concatenate([a * cos[...] + b * sin[...], b * cos[...] - a * sin[...]], axis=0)
        u = projT[row, :]
        scale = lax.rsqrt(jnp.mean(u * u, axis=0, keepdims=True) + EPSILON)
        us = u * scale
        weighted = g * gain
        inner = jnp.mean(weighted * us, axis=0, keepdims=True)
        hT[row, :] = (scale * (weighted - us * inner)).astype(BF16)
        return jnp.sum(g * us, axis=1, keepdims=True)

    def query_back(h, acc):
        row = block_of(h, HD)
        return acc + norm_column(row, gqT[row, :], gain_q)

    gain_grad_q = lax.fori_loop(0, hq, query_back, jnp.zeros((HD, 1), F32))
    gain_grad_k = jnp.zeros((HD, 1), F32)
    for i in range(hk):
        gain_grad_k = gain_grad_k + norm_column(pl.ds(qw + i * HD, HD), jnp.transpose(gk[i]), gain_k)
        hT[qw + kw + i * HD : qw + kw + (i + 1) * HD, :] = jnp.transpose(gv[i]).astype(BF16)

    up_sum.start()

    def ni_copy(j):
        return remote(gsend.at[j - 1], grecv.at[j - 1], nis.at[j], nir.at[j], at.seq_to(j))

    for i in range(ns):
        rows = pl.ds(i * T, T)
        cotall[rows, 0:pw] = jnp.transpose(hT[0:pw, rows])
    for j in list(range(1, ns)) + [0]:
        part = mm_nt(cotall[block_of(at.seq_to(j)[1], T), 0:pw], wqkv[...])
        if j:
            gsend[j - 1] = part.astype(BF16)
            ni_copy(j).start()
        else:
            resid[...] = part
    for j in range(1, ns):
        out_copy(j).start()
    for k in range(nd):
        part = mm(hT[0:pw, :], normed[:, k * R : (k + 1) * R])
        gb[((k % 2) * nz + k // 2) * R : ((k % 2) * nz + k // 2 + 1) * R, 0:pw] = jnp.transpose(part).astype(BF16)
    qk_copy = remote(gb.at[block_of(1 - core, nz * R), pl.ds(0, pw)], qkr, ss2.at[1], sr2.at[1], at.sib)
    qk_copy.start()
    for j in range(1, ns):
        gout_copy(j).wait_recv()
    acc = gu[0:half_gu, block_of(s, cw)].astype(F32)
    for j in range(1, ns):
        acc = acc + gorecv[j - 1].astype(F32)
    goown[...] = acc.astype(BF16)
    out_sum.start()
    qk_copy.wait_recv()
    qkown[...] = (gb[block_of(core, nz * R), pl.ds(0, pw)].astype(F32) + qkr[...].astype(F32)).astype(BF16)
    qkv_sum.start()
    dn_sum.total()
    gate_sum.total()

    for j in range(1, ns):
        ni_copy(j).wait_recv()
    gni = resid[...]
    for j in range(1, ns):
        gni = gni + grecv[j - 1].astype(F32)
    stream = x[...].astype(F32)
    scale = lax.rsqrt(jnp.mean(stream * stream, axis=-1, keepdims=True) + EPSILON)
    unit = stream * scale
    weighted = gni * gsum[0:1, :]
    gown[...] = gown[...] + scale * (weighted - unit * jnp.mean(weighted * unit, axis=-1, keepdims=True))
    stream_store = pltpu.make_async_copy(gown, gstream, loc.at[2])
    stream_store.start()
    first = jnp.sum(gni * unit, axis=0, keepdims=True)
    qk = jnp.broadcast_to(jnp.concatenate([gain_grad_q, gain_grad_k], axis=0), (2 * HD, 128))
    sm0[0:1, :] = first
    sm0[1:2, :] = gsecond[0:1, :]
    sm0[2:8, :] = jnp.zeros((6, width), F32)
    sm0[2:3, : 2 * HD] = jnp.transpose(qk)[0:1, :]

    def small_seq(j):
        return remote(sm0, sm1.at[j - 1], s1.at[j], r1.at[j], at.seq_to(j))

    def small_dp(j):
        return remote(sm2, sm3.at[j - 1], s2.at[j], r2.at[j], at.dp_to(j))

    for j in range(1, ns):
        small_seq(j).start()
    up_sum.total()
    for j in range(1, ns):
        out_copy(j).wait_recv()
    acc = oown[...]
    for j in range(1, ns):
        acc = acc + xall[pl.ds((j - 1) * T, T), :].astype(F32)
    last = pl.ds((ns - 1) * T, T)
    xall[last, :] = acc.astype(BF16)
    out_store = pltpu.make_async_copy(xall.at[last], outputs, loc.at[1])
    out_store.start()
    for j in range(1, ns):
        small_seq(j).wait_recv()
    acc = sm0[...]
    for j in range(1, ns):
        acc = acc + sm1[j - 1]
    sm2[...] = acc
    for j in range(1, nd):
        small_dp(j).start()
    out_sum.total()
    qkv_sum.total()
    for j in range(1, nd):
        small_dp(j).wait_recv()
    for j in range(1, nd):
        acc = acc + sm3[j - 1]
    small[...] = acc

    for p in range(ns):
        pl.when(s != p)(mixed_back(p).wait_send)
    go_copy.wait_send()
    qk_copy.wait_send()
    for j in range(1, ns):
        gout_copy(j).wait_send()
        out_copy(j).wait_send()
        ni_copy(j).wait_send()
        small_seq(j).wait_send()
    for j in range(1, nd):
        small_dp(j).wait_send()
    for rb in range(ns):
        pl.when(s != rb)(mixed_out(rb).wait_send)
    for c in x_copies + g_copies + c_copies + [dn_copy]:
        c.wait_send()
    for t in (take_qkv, take_out):
        t.drain()
    for t in (dn_sum, out_sum, qkv_sum, gate_sum, up_sum):
        t.drain()
    out_store.wait()
    stream_store.wait()


def vmem(n):
    return [pl.BlockSpec(memory_space=pltpu.VMEM)] * n


def block(ns, nd, piece, x, gain1, gain2, gainqk, w_qkv, w_out, cot, w_gate, w_up, w_down):
    T, width = x.shape
    L = ns * T
    R = w_qkv.shape[0]
    n = nd * piece
    n2 = 2 * n
    nz = nd // 2
    hq, hk = H // ns, KV // ns
    qw, kw = hq * HD, hk * HD
    pw = qw + 2 * kw
    cw = width // ns
    cos, sin = rope_columns(L)
    sh, vm = jax.ShapeDtypeStruct, pltpu.VMEM
    outs = (
        sh((T, width), BF16), sh((T, width), F32), sh((ns, R, n), BF16), sh((ns, R, n), BF16),
        sh((ns, piece, width), BF16), sh((ns, R, pw), BF16), sh((ns, R, cw), BF16), sh((8, width), F32),
    )
    hbm = pl.BlockSpec(memory_space=pl.ANY)
    scratch = [
        vm((L, width), BF16), vm((qw + kw, L), F32), vm((qw, L), BF16), vm((kw, L), BF16),
        vm((hk, L, HD), BF16), vm((hk, L, HD), BF16), vm((hq, 1, L), F32), vm((ns, qw, T), BF16),
        vm((H * HD, T), BF16), vm((H * HD, width), BF16), vm((width, pw), BF16), vm((8, width), F32),
        vm((ns - 1, T, width), BF16), vm((T, width), F32), vm((8, width), F32),
        vm((kw, L), BF16), vm((T, width), F32), vm((L, width), BF16), vm((L, width), BF16), vm((8, 128), F32),
        vm((nd, 8, 128), F32), vm((R, pw), BF16), vm((R, n2), BF16), vm((nd * R, n2), BF16), vm((n, width), BF16),
        vm((T, n), BF16), vm((n, L), BF16), vm((L, n2), BF16), vm((ns - 1, T, width), BF16),
        vm((ns - 1, T, width), BF16), vm((T, width), F32), vm((2, nz * R, L), BF16),
        vm((nz * R, n), BF16), vm((nz * R, n), BF16), vm((nz * piece, width), BF16),
        vm((nz - 1, R, n), BF16), vm((R, n), BF16), vm((nz - 1, R, n), BF16), vm((R, n), BF16),
        vm((nz - 1, piece, width), BF16), vm((piece, width), BF16), vm((ns, T, qw), BF16), vm((L, qw), BF16),
        vm((hk, L, qw // hk), BF16), vm((hk, L, HD), F32), vm((hk, L, HD), F32), vm((qw, L), F32),
        vm((nz * R, pw), BF16), vm((nz * R, pw), BF16), vm((nz - 1, R, pw), BF16), vm((R, pw), BF16),
        vm((nz * R, width), BF16), vm((ns - 1, nz * R, cw), BF16), vm((nz * R, cw), BF16),
        vm((nz - 1, R, cw), BF16), vm((R, cw), BF16),
        vm((8, width), F32), vm((ns - 1, 8, width), F32), vm((8, width), F32), vm((nd - 1, 8, width), F32),
    ]
    sems = [DMA((ns,)), DMA((ns,)), DMA((nd,)), DMA((nd,))] + [DMA((ns,))] * 8 + [DMA((3,)), DMA((3,))]
    sems += [DMA((3,)), DMA((2, 8))]
    sems += [DMA((ns,))] * 6 + [DMA((2,)), DMA((2,))] + [DMA((ns,))] * 4 + [DMA((nd,)), DMA((nd,))]
    return pl.pallas_call(
        functools.partial(block_kernel, ns, nd),
        out_shape=outs,
        in_specs=vmem(5) + [hbm] * 5 + vmem(2),
        out_specs=[hbm] * 7 + vmem(1),
        scratch_shapes=scratch + sems + gather_sems(nz) * 4 + scatter_sems(ns, nz) * 5,
        compiler_params=pltpu.CompilerParams(
            collective_id=0, has_side_effects=True, vmem_limit_bytes=VMEM_LIMIT
        ),
        cost_estimate=pl.CostEstimate(flops=38_000_000_000, bytes_accessed=40_000_000, transcendentals=12_000_000),
    )(x, gain1, gain2, gainqk, w_qkv, w_out, cot, w_gate, w_up, w_down, cos, sin)


def finish_kernel(ns, nd, piece, gateall, upall, qkvall, outall, dnall, gate, up, qkv, out, down):
    hq, hk = H // ns, KV // ns
    qw, kw = hq * HD, hk * HD
    pad = gateall.shape[2] // nd
    for ref, got in ((gate, gateall), (up, upall)):
        parts = [got[i].astype(F32) for i in range(ns)]
        ref[...] = jnp.concatenate(
            [parts[i][:, k * pad : k * pad + piece] for k in range(nd) for i in range(ns)], axis=1
        )
    parts = [qkvall[i].astype(F32) for i in range(ns)]
    qkv[...] = jnp.concatenate(
        [p[:, :qw] for p in parts] + [p[:, qw : qw + kw] for p in parts] + [p[:, qw + kw :] for p in parts], axis=1
    )
    out[...] = jnp.concatenate([outall[i].astype(F32) for i in range(ns)], axis=1)
    down[...] = jnp.concatenate([dnall[i].astype(F32)[:piece] for i in range(dnall.shape[0])], axis=0)


def finish(ns, nd, piece, gateall, upall, qkvall, outall, dnall):
    R = gateall.shape[1]
    steps = 4
    rows = R // steps
    ff = ns * nd * piece
    width = dnall.shape[2]
    widths = (ff, ff, ns * qkvall.shape[2], ns * outall.shape[2])
    many = ns // steps
    ins = [pl.BlockSpec((ns, rows, a.shape[2]), lambda i: (0, i, 0)) for a in (gateall, upall, qkvall, outall)]
    ins.append(pl.BlockSpec((many,) + dnall.shape[1:], lambda i: (i, 0, 0)))
    outs = [pl.BlockSpec((rows, w), lambda i: (i, 0)) for w in widths]
    outs.append(pl.BlockSpec((many * piece, width), lambda i: (i, 0)))
    return pl.pallas_call(
        functools.partial(finish_kernel, ns, nd, piece),
        grid=(steps,),
        out_shape=[jax.ShapeDtypeStruct((R, w), F32) for w in widths]
        + [jax.ShapeDtypeStruct((ns * piece, width), F32)],
        in_specs=ins,
        out_specs=outs,
        compiler_params=pltpu.CompilerParams(vmem_limit_bytes=40 << 20),
    )(gateall, upall, qkvall, outall, dnall)


def shards(inputs, cotangent, first_gain, w_qkv, qk_gain, w_out, second_gain, w_gate, w_up, w_down):
    ns, nd = lax.axis_size("seq"), lax.axis_size("dp")
    s, d = lax.axis_index("seq"), lax.axis_index("dp")
    piece = w_down.shape[0] // ns
    pad = -piece % 16
    down_rows = w_down
    if pad:
        down_rows = jnp.pad(lax.dynamic_slice_in_dim(w_down, s * piece, piece, 0), ((0, pad), (0, 0)))
    x = inputs[0]
    outputs, gstream, gateall, upall, dnall, qkvall, outall, small = block(
        ns, nd, piece + pad, x, first_gain[None], second_gain[None], qk_gain[None], w_qkv, w_out, cotangent[0],
        w_gate, w_up, down_rows,
    )
    gate, up, qkv, out, down = finish(ns, nd, piece, gateall, upall, qkvall, outall, dnall)
    gl, ql = first_gain.shape[0], qk_gain.shape[0]
    first = lax.dynamic_slice(small, (0, d * gl), (1, gl))[0]
    second = lax.dynamic_slice(small, (1, d * gl), (1, gl))[0]
    qk = lax.dynamic_slice(small, (2, d * ql), (1, ql))[0]
    return (outputs[None], gstream[None], first, qkv, qk, out, second, gate, up, down)


def solution(mesh):
    act = P("dp", "seq", None)
    vec, mat = P("dp"), P("dp", None)
    in_specs = (act, act, vec, mat, vec, mat, vec, mat, mat, mat)
    out_specs = (act, act, vec, mat, vec, mat, vec, mat, mat, mat)
    return jax.shard_map(shards, mesh=mesh, in_specs=in_specs, out_specs=out_specs, check_vma=False)
```

```python
import functools

import jax
import jax.numpy as jnp
import numpy as np
from jax import lax
from jax.experimental import pallas as pl
from jax.experimental.pallas import tpu as pltpu
from jax.sharding import PartitionSpec as P

H = 16
KV = 8
HD = 64
EPSILON = 1e-06
THETA_BASE = 1000000.0
F32 = jnp.float32
BF16 = jnp.bfloat16
VMEM_LIMIT = 61 << 20


def rope_columns(length):
    inverse = np.float32(THETA_BASE) ** (-np.arange(0, HD, 2).astype(np.float32) / np.float32(HD))
    angles = (np.arange(length, dtype=np.float32)[None, :] * inverse.astype(np.float32)[:, None]).astype(np.float32)
    angles = angles.astype(np.float64)
    return jnp.asarray(np.cos(angles), F32), jnp.asarray(np.sin(angles), F32)


MESH = pl.DeviceIdType.MESH
DMA = pltpu.SemaphoreType.DMA


def mm(a, b):
    return jnp.dot(a, b, preferred_element_type=F32)


def mm_nt(a, b):
    return lax.dot_general(a, b, (((1,), (1,)), ((), ())), preferred_element_type=F32)


def remote(src, dst, send, recv, device):
    return pltpu.make_async_remote_copy(
        src_ref=src, dst_ref=dst, send_sem=send, recv_sem=recv, device_id=device, device_id_type=MESH
    )


def block_of(index, size):
    return pl.ds(pl.multiple_of(index * size, size), size)


class Place:
    def __init__(self, ns, nd):
        self.ns, self.nd, self.nz = ns, nd, nd // 2
        self.d, self.s = lax.axis_index("dp"), lax.axis_index("seq")
        self.zz, self.core = self.d // 2, lax.rem(self.d, 2)
        self.sib = (self.d + 1 - 2 * self.core, self.s)

    def seq_to(self, j):
        return (self.d, lax.rem(self.s + j, self.ns))

    def seq_from(self, j):
        return lax.rem(self.s + self.ns - j, self.ns)

    def across(self):
        return (self.s + 1 - 2 * lax.rem(self.s, 2), lax.rem(self.s + 2, 4), 3 - self.s)

    def gather_rank(self, j):
        if j == 0:
            return self.s
        return self.across()[j - 1] if self.ns == 4 else self.seq_from(j)

    def reduce_rank(self, j):
        if j == 0:
            return self.s
        x, y, o = self.across()
        return (o, x, y)[j - 1] if self.ns == 4 else lax.rem(self.s + j, self.ns)

    def dp_to(self, j):
        return (lax.rem(self.d + j, self.nd), self.s)

    def z_index(self, j):
        return lax.rem(self.zz + j, self.nz)

    def z_from(self, j):
        return lax.rem(self.zz + self.nz - j, self.nz)

    def z_device(self, z):
        return (2 * z + self.core, self.s)

    def greet(self):
        bar = pltpu.get_barrier_semaphore()
        for j in range(1, self.nd):
            pl.semaphore_signal(bar, inc=1, device_id=self.dp_to(j), device_id_type=MESH)
        for j in range(1, self.ns):
            pl.semaphore_signal(bar, inc=1, device_id=self.seq_to(j), device_id_type=MESH)
        pl.semaphore_wait(bar, self.nd + self.ns - 2)


class SeqGather:
    def __init__(self, at, src, dst, sems):
        self.at, self.src, self.dst = at, src, dst
        self.send, self.recv = sems
        self.half = src.shape[0] // 2

    def direct(self, j):
        at = self.at
        to = at.across()[j - 1] if at.ns == 4 else at.seq_to(j)[1]
        return remote(self.src, self.dst(at.s), self.send.at[j], self.recv.at[j], (at.d, to))

    def forward(self, i):
        at = self.at
        part = self.dst(at.across()[i]).at[pl.ds(i * self.half, self.half)]
        return remote(part, part, self.send.at[3 + i], self.recv.at[3 + i], (at.d, at.across()[1 - i]))

    def near(self):
        return range(1, 3 if self.at.ns == 4 else self.at.ns)

    def start(self):
        for j in self.near():
            self.direct(j).start()

    def hop(self):
        if self.at.ns == 4:
            for i in range(2):
                self.direct(i + 1).wait_recv()
                self.forward(i).start()

    def wait(self, j):
        if self.at.ns != 4:
            self.direct(j).wait_recv()
        elif j == 3:
            for i in range(2):
                self.forward(i).wait_recv()

    def finish(self):
        for j in range(1, self.at.ns):
            self.wait(j)

    def drain(self):
        for j in self.near():
            self.direct(j).wait_send()
        if self.at.ns == 4:
            for i in range(2):
                self.forward(i).wait_send()


def seq_sems(ns):
    return [DMA((max(ns, 6),)), DMA((max(ns, 6),))]


class SeqReduce:
    def __init__(self, at, rows, stage, inbox, sems):
        self.at, self.rows, self.stage, self.inbox = at, rows, stage, inbox
        self.send, self.recv = sems

    def part(self, ref, block, half=None):
        if half is None:
            return ref.at[pl.ds(block * self.rows, self.rows)]
        h = self.rows // 2
        return ref.at[pl.ds(block * self.rows + half * h, h)]

    def leg(self, k):
        at = self.at
        if at.ns != 4:
            src, dst, to = self.part(self.stage, k - 1), self.part(self.inbox, k - 1), at.seq_to(k)[1]
        else:
            b, h, i, n = ((0, 0, 2, 0), (0, 1, 2, 1), (1, 0, 0, 0), (2, 1, 1, 1), (2, 0, 1, 1), (1, 1, 0, 0))[k]
            src, dst, to = self.part(self.stage, b, h), self.part(self.inbox, i, h), at.across()[n]
        return remote(src, dst, self.send.at[k], self.recv.at[k], (at.d, to))

    def push(self, j):
        for k in (j,) if self.at.ns != 4 else ((), (0, 1), (2,), (3,))[j]:
            self.leg(k).start()

    def hop(self):
        if self.at.ns != 4:
            return
        h = self.rows // 2
        for k, b in ((0, 2), (1, 1)):
            self.leg(k).wait_recv()
            mine, came = pl.ds(b * self.rows + k * h, h), pl.ds(2 * self.rows + k * h, h)
            self.stage[mine, :] = (self.stage[mine, :].astype(F32) + self.inbox[came, :].astype(F32)).astype(BF16)
            self.leg(4 + k).start()

    def total(self, acc):
        four = self.at.ns == 4
        for k in range(2, 6) if four else range(1, self.at.ns):
            self.leg(k).wait_recv()
        for b in range(2 if four else self.at.ns - 1):
            acc = acc + self.inbox[b * self.rows : (b + 1) * self.rows, :].astype(F32)
        return acc

    def drain(self):
        for k in range(6) if self.at.ns == 4 else range(1, self.at.ns):
            self.leg(k).wait_send()


class Gather:
    def __init__(self, at, src, dst, sems, relayed=True):
        self.at, self.src, self.dst, self.relayed = at, src, dst, relayed
        self.send, self.recv, self.fsend, self.frecv, self.rsend, self.local = sems
        self.rows = src.shape[0]

    def piece(self, z):
        return self.dst.at[block_of(2 * z + self.at.core, self.rows)]

    def direct(self, j):
        at = self.at
        return remote(self.src, self.piece(at.zz), self.send.at[j], self.recv.at[j], at.z_device(at.z_index(j)))

    def near(self, j):
        at = self.at
        away = at.z_index(j) - at.zz
        return (away < at.nz - 1) & (away > 1 - at.nz) if self.relayed else away != 0

    def across(self, j):
        piece = self.src if j == 0 else self.piece(self.at.z_from(j))
        return remote(piece, self.piece(self.at.z_from(j)), self.fsend.at[j], self.frecv.at[j], self.at.sib)

    def relay(self, j):
        nz = self.at.nz
        legs = []
        if not self.relayed:
            return legs
        if j == nz - 2:
            legs.append((nz - 2, 0, nz - 1, nz - 1, 0))
        if j == 2:
            legs.append((1, nz - 1, 0, 1, 1))
        out = []
        for here, origin, target, index, k in legs:
            piece = self.piece(origin)
            copy = remote(piece, piece, self.rsend.at[k], self.recv.at[index], self.at.z_device(target))
            out.append((self.at.zz == here, copy))
        return out

    def order(self):
        nz = self.at.nz
        return sorted({2, nz - 2}), list(range(3, nz - 2)) + [1, nz - 1]

    def start(self):
        first, rest = self.order()
        for j in first + rest:
            pl.when(self.near(j))(self.direct(j).start)
        self.across(0).start()
        self.mine().start()

    def mine(self):
        return pltpu.make_async_copy(self.src, self.dst.at[block_of(self.at.d, self.rows)], self.local.at[0])

    def hop(self):
        for j in self.order()[0]:
            self.direct(j).wait_recv()
            for here, copy in self.relay(j):
                pl.when(here)(copy.start)
            self.across(j).start()

    def arrive(self):
        for j in self.order()[1]:
            self.direct(j).wait_recv()
            self.across(j).start()

    def finish(self):
        for j in range(self.at.nz):
            self.across(j).wait_recv()
        self.mine().wait()

    def drain(self):
        for j in range(self.at.nz):
            self.across(j).wait_send()
            if j:
                pl.when(self.near(j))(self.direct(j).wait_send)
                for here, copy in self.relay(j):
                    pl.when(here)(copy.wait_send)


def gather_sems(nz):
    return [DMA((nz,)), DMA((nz,)), DMA((nz,)), DMA((nz,)), DMA((2,)), DMA((1,))]


class Scatter:
    def __init__(self, at, pieces, inbox, final, out, sems):
        self.at, self.pieces, self.inbox, self.final, self.out = at, pieces, inbox, final, out
        self.send, self.recv, osend, orecv, self.local, self.rsend, self.rrecv = sems
        self.rows = final.shape[0]
        self.share = SeqGather(at, final, lambda r: out.at[r], (osend, orecv))

    def piece(self, z):
        return self.pieces.at[block_of(z, self.rows)]

    def copy(self, j):
        at = self.at
        z = at.z_index(j)
        return remote(self.piece(z), self.inbox.at[j - 1], self.send.at[j], self.recv.at[j], at.z_device(z))

    def far_copy(self, target, via):
        slot = self.inbox.at[self.at.nz - 1]
        return remote(self.piece(target), slot, self.rsend.at[0], self.rrecv.at[0], self.at.z_device(via))

    def far(self):
        nz = self.at.nz
        return ((0, nz - 1, 1, nz - 2), (nz - 1, 0, nz - 2, 2))

    def near(self, away):
        return (away < self.at.nz - 1) & (away > 1 - self.at.nz)

    def free(self, j):
        go = self.near(self.at.z_index(j) - self.at.zz)
        for _, _, via, k in self.far():
            if k == j:
                go = go & (self.at.zz != via)
        return go

    def start(self):
        at = self.at
        for origin, target, via, _ in self.far():
            pl.when(at.zz == origin)(self.far_copy(target, via).start)
        for j in range(1, at.nz):
            pl.when(self.free(j))(self.copy(j).start)
            away = at.z_from(j) - at.zz

            @pl.when((away >= at.nz - 1) | (away <= 1 - at.nz))
            def _():
                self.inbox[j - 1] = jnp.zeros_like(self.inbox[j - 1])

    def relay(self):
        at = self.at
        for _, target, via, j in self.far():

            @pl.when(at.zz == via)
            def _():
                self.far_copy(target, via).wait_recv()
                rows = block_of(target, self.rows)
                both = self.pieces[rows, :].astype(F32) + self.inbox[at.nz - 1].astype(F32)
                self.pieces[rows, :] = both.astype(BF16)
                self.copy(j).start()

    def keep(self):
        return pltpu.make_async_copy(self.final, self.out.at[self.at.s], self.local.at[0])

    def total(self):
        at = self.at
        for j in range(1, at.nz):
            pl.when(self.near(at.z_from(j) - at.zz))(self.copy(j).wait_recv)
        acc = self.pieces[block_of(self.at.zz, self.rows), :].astype(F32)
        for j in range(1, self.at.nz):
            acc = acc + self.inbox[j - 1].astype(F32)
        self.final[...] = acc.astype(BF16)
        self.keep().start()
        self.share.start()

    def drain(self):
        self.keep().wait()
        self.share.finish()
        self.share.drain()
        at = self.at
        for j in range(1, at.nz):
            pl.when(self.near(at.z_index(j) - at.zz))(self.copy(j).wait_send)
        for origin, target, via, _ in self.far():
            pl.when(at.zz == origin)(self.far_copy(target, via).wait_send)


def scatter_sems(ns, nz):
    return [DMA((nz,)), DMA((nz,))] + seq_sems(ns) + [DMA((1,)), DMA((1,)), DMA((1,))]


def block_kernel(
    ns, nd, x, gain1, gain2, gainqk, wqkv_rows, wout_mine, cot, wgate, wup, wdown, cos, sin,
    outputs, gstream, gateall, upall, dnall, qkvall, outall, small,
    normed, projT, qT, kT, krows, vrows, inv, mixT, mrowsT, wout, wqkv, gsum, osend, oown, gsecond,
    vT, resid, cotall, xall, gains, gbuf, wqkv_mine, gu_mine, gu, dn, hrow, hT, gb, gsend, grecv, gown, nmT,
    gur, uur, dnr,
    gaz, gaf, upz, upf, dnz, dnf, gmr, grows, qrows, gk, gv, gqT, qkr, qkown, qkz, qkf,
    gor, gorecv, goown, goz, gof, sm0, sm1, sm2, sm3,
    xs, xr, gs, gr, cs, cr, ms, mr, ns_, nr, ps, pr, ss, sr, loc, wl,
    os_, or_, bs, br, nis, nir, ss2, sr2, gos, gorc, s1, r1, s2, r2, *sems,
):
    at = Place(ns, nd)
    s, d, nz, core = at.s, at.d, at.nz, at.core
    T, width = x.shape
    L = ns * T
    R = wqkv_mine.shape[0]
    cw = width // ns
    n = dn.shape[0]
    piece = n // nd
    gl, ql = gain1.shape[1], gainqk.shape[1]
    dn_mine = wdown.at[block_of(s, piece)] if wdown.shape[0] == ns * piece else wdown
    hq, hk = H // ns, KV // ns
    group = hq // hk
    qw, kw = hq * HD, hk * HD
    own = block_of(s, T)
    pw = qw + 2 * kw
    gains[...] = jnp.zeros_like(gains)
    gains[0:1, :gl] = gain1[...]
    gains[1:2, :gl] = gain2[...]
    gains[2:3, :ql] = gainqk[...]
    for i in range(ns):

        @pl.when(s == i)
        def _():
            cuts = ((i * qw, qw), (H * HD + i * kw, kw), ((H + KV) * HD + i * kw, kw))
            wqkv_mine[...] = jnp.concatenate([wqkv_rows[:, a : a + b] for a, b in cuts], axis=1)

    at.greet()

    share_x = SeqGather(at, x, lambda r: xall.at[block_of(r, T)], (xs, xr))
    g_copies = [remote(gains, gbuf.at[d], gs.at[j], gr.at[j], at.dp_to(j)) for j in range(1, nd)]
    share_cot = SeqGather(at, cot, lambda r: cotall.at[block_of(r, T)], (cs, cr))
    share_nm = SeqGather(at, xall.at[own], lambda r: xall.at[block_of(r, T)], (ns_, nr))
    take_qkv = Gather(at, wqkv_mine, wqkv, sems[0:6], relayed=False)
    take_out = Gather(at, wout_mine, wout, sems[6:12], relayed=False)
    take_gate = Gather(at, gu_mine.at[:, pl.ds(0, n)], gu.at[:, pl.ds(0, n)], sems[12:18])
    take_up = Gather(at, gu_mine.at[:, pl.ds(n, n)], gu.at[:, pl.ds(n, n)], sems[59:65])
    take_dn = Gather(at, dn_mine, dn, sems[18:24])
    for c in g_copies:
        c.start()
    share_x.start()
    take_qkv.start()
    take_out.start()
    xall[own, :] = x[...]
    gbuf[d] = gains[...]
    cot_local = pltpu.make_async_copy(cot, cotall.at[own], loc.at[0])
    cot_local.start()
    ff = wgate.shape[1]
    parts = max(1, -(-ff // (2 * n)))
    while nd % parts:
        parts += 1
    span = ff // parts
    stage = []
    for i, w in enumerate((wgate, wup)):
        for k in range(parts):
            row = pl.ds((i * parts + k) * R, R)
            stage.append(
                pltpu.make_async_copy(w.at[:, pl.ds(k * span, span)], gb.at[row, pl.ds(0, span)], wl.at[i, k])
            )
    for c in stage:
        c.start()
    for c in stage:
        c.wait()
    real = wgate.shape[1] // nd // ns
    gap = [jnp.zeros((R, piece - real), BF16)] if piece > real else []
    for i in range(ns):

        @pl.when(s == i)
        def _():
            cuts = []
            for w in range(2):
                for k in range(nd):
                    a = (k * ns + i) * real
                    row = (w * parts + a // span) * R
                    cuts += [gb[row : row + R, a % span : a % span + real]] + gap
            gu_mine[...] = jnp.concatenate(cuts, axis=1)

    for c in g_copies:
        c.wait_recv()
    gain_in = jnp.concatenate([gbuf[k][0:1, :gl] for k in range(nd)], axis=1)
    gain_mid = jnp.concatenate([gbuf[k][1:2, :gl] for k in range(nd)], axis=1)
    gain_qk = jnp.concatenate([gbuf[k][2:3, :ql] for k in range(nd)], axis=1)
    gsum[...] = jnp.zeros_like(gsum)
    gsum[0:1, :] = gain_in
    gsum[1:2, :] = gain_mid
    gsum[2:3, : 2 * HD] = gain_qk
    columns = jnp.transpose(jnp.broadcast_to(gain_qk, (8, 2 * HD)))
    gain_q, gain_k = columns[:HD, 0:1], columns[HD:, 0:1]
    for j in range(ns):
        rows = block_of(at.gather_rank(j), T)
        if j == 1:
            share_x.hop()
        if j:
            share_x.wait(j)
        xc = xall[rows, :].astype(F32)
        scale = lax.rsqrt(jnp.mean(xc * xc, axis=-1, keepdims=True) + EPSILON)
        normed[rows, :] = (xc * scale * gain_in).astype(BF16)
    share_cot.start()
    take_qkv.hop()
    take_qkv.arrive()
    take_qkv.finish()
    for j in range(ns):
        rows = pl.ds(j * T, T)
        proj = mm(normed[rows, :], wqkv[...])
        projT[:, rows] = jnp.transpose(proj[:, : qw + kw])
        val = proj[:, qw + kw :]
        vT[:, rows] = jnp.transpose(val).astype(BF16)
        for i in range(hk):
            vrows[i, rows, :] = val[:, i * HD : (i + 1) * HD].astype(BF16)

    half = HD // 2

    def rope(row, gain, factor):
        u = projT[row, :]
        scale = lax.rsqrt(jnp.mean(u * u, axis=0, keepdims=True) + EPSILON)
        u = u * scale * gain
        a, b = u[:half], u[half:]
        return jnp.concatenate([a * cos[...] - b * sin[...], b * cos[...] + a * sin[...]], axis=0) * factor

    def rope_query(h, carry):
        row = block_of(h, HD)
        qT[row, :] = rope(row, gain_q, HD**-0.5).astype(BF16)
        return carry

    lax.fori_loop(0, hq, rope_query, 0)
    for i in range(hk):
        r = rope(pl.ds(qw + i * HD, HD), gain_k, 1.0)
        kT[i * HD : (i + 1) * HD, :] = r.astype(BF16)
        krows[i, :, :] = jnp.transpose(r).astype(BF16)

    share_x.drain()
    keep = lax.broadcasted_iota(jnp.int32, (T, T), 0) <= lax.broadcasted_iota(jnp.int32, (T, T), 1)
    block = block_of(s, qw)

    def mixed_out(rb):
        return remote(mixT.at[rb], mrowsT.at[block], ms.at[rb], mr.at[s], (d, rb))

    for rb in range(ns):
        cols = pl.ds(rb * T, T)
        span = rb * T

        def head(h, carry):
            kv = h // group
            row, vrow = block_of(h, HD), block_of(kv, HD)
            q = qT[row, cols]
            p = jnp.where(keep, jnp.exp(mm(krows[kv, cols, :], q)), 0.0)
            tot = jnp.sum(p, axis=0, keepdims=True)
            m = mm(vT[vrow, cols], p.astype(BF16))
            if span:
                p = jnp.exp(mm(krows[kv, 0:span, :], q))
                tot = tot + jnp.sum(p, axis=0, keepdims=True)
                m = m + mm(vT[vrow, 0:span], p.astype(BF16))
            one = 1.0 / tot
            inv[h, :, cols] = one
            mixT[rb, row, :] = (m * one).astype(BF16)
            return carry

        lax.fori_loop(0, hq, head, 0)
        pl.when(s != rb)(mixed_out(rb).start)
        if rb == 0:
            take_gate.start()
        if rb == ns - 1:
            take_out.hop()
            take_out.arrive()

    mrowsT[block, :] = mixT[s]
    for j in range(1, ns):
        src = at.seq_from(j)
        remote(mixT.at[0], mrowsT.at[block_of(src, qw)], ms.at[0], mr.at[src], (d, src)).wait_recv()
    take_out.finish()
    residual = x[...].astype(F32) + mm(jnp.transpose(mrowsT[...]), wout[...])
    resid[...] = residual
    scale_mid = lax.rsqrt(jnp.mean(residual * residual, axis=-1, keepdims=True) + EPSILON)
    xall[own, :] = (residual * scale_mid * gain_mid).astype(BF16)
    share_nm.start()
    share_cot.hop()
    take_gate.hop()
    take_up.start()
    take_gate.arrive()
    share_nm.hop()
    share_nm.finish()
    take_up.hop()
    take_dn.start()
    take_up.arrive()
    ft = 384 if n % 384 == 0 else 128
    nt = n // ft
    wt = 256

    def pre_part(base):
        def pre_block(j, carry):
            rows = block_of(j, T)
            for i in range(nt):
                f = pl.ds(base + i * ft, ft)
                gb[rows, f] = mm(xall[rows, :], gu[:, f]).astype(BF16)
            return carry

        lax.fori_loop(0, ns, pre_block, 0)

    take_gate.finish()
    pre_part(0)
    take_up.finish()
    pre_part(n)
    share_cot.finish()
    cot_local.wait()
    take_dn.hop()
    take_dn.arrive()
    take_dn.finish()
    sum_nm = SeqReduce(at, T, gsend, grecv, (ps, pr))
    for j in range(ns):
        rows = block_of(at.reduce_rank(j), T)
        stage = pl.ds((j - 1) * T, T)

        def hidden_tile(i, carry):
            f, f2 = block_of(i, ft), block_of(i + nt, ft)
            gate, up = gb[rows, f].astype(F32), gb[rows, f2].astype(F32)
            sig = 1.0 / (1.0 + jnp.exp(-gate))
            act = gate * sig
            back = mm_nt(cotall[rows, :], dn[f, :])
            hid = act * up
            hrow[:, f] = hid.astype(BF16)
            hT[f, rows] = jnp.transpose(hid).astype(BF16)
            gb[rows, f] = (back * up * sig * (1.0 + gate * (1.0 - sig))).astype(BF16)
            gb[rows, f2] = (back * act).astype(BF16)
            return carry

        lax.fori_loop(0, nt, hidden_tile, 0)

        def back_tile(i, carry):
            w = block_of(i, wt)
            part = mm_nt(gb[rows, :], gu[w, :])
            if j:
                gsend[stage, w] = part.astype(BF16)
            else:
                gown[:, w] = part
            return carry

        lax.fori_loop(0, width // wt, back_tile, 0)
        if j:
            sum_nm.push(j)

        def out_tile(i, carry):
            w = block_of(i, wt)
            part = mm(hrow[...], dn[:, w])
            if j:
                osend[stage, w] = part.astype(BF16)
            else:
                oown[:, w] = part + resid[:, w]
            return carry

        lax.fori_loop(0, width // wt, out_tile, 0)

    sum_nm.hop()
    share_nm.drain()
    share_cot.drain()
    take_gate.drain()
    take_up.drain()
    take_dn.drain()
    half_gu, half_dn = nz * R, nz * piece
    dns, dnown = dn.at[pl.ds(0, half_dn)], dn.at[pl.ds(half_dn, half_dn)]
    gus, gateown = (gu.at[pl.ds(i * half_gu, half_gu), pl.ds(0, n)] for i in range(2))
    uus, upown = (gu.at[pl.ds(i * half_gu, half_gu), pl.ds(n, n)] for i in range(2))
    dn_sum = Scatter(at, dnown, dnz, dnf, dnall, sems[24:31])
    gate_sum = Scatter(at, gateown, gaz, gaf, gateall, sems[31:38])
    up_sum = Scatter(at, upown, upz, upf, upall, sems[38:45])
    qkv_sum = Scatter(at, qkown, qkz, qkf, qkvall, sems[45:52])
    out_sum = Scatter(at, goown, goz, gof, outall, sems[52:59])
    for k in range(nd):
        nmT[k % 2, (k // 2) * R : (k // 2 + 1) * R, :] = jnp.transpose(xall[:, k * R : (k + 1) * R])

    def dn_rows(c, i):
        return hT[block_of(2 * i + c, piece), :]

    tiles = nt
    tw = n // tiles

    def other(buf, base):
        def tile(i, carry):
            f = block_of(i, tw)
            buf[:, f] = mm(nmT[1 - core], gb[:, pl.ds(pl.multiple_of(base + i * tw, 128), tw)]).astype(BF16)
            return carry

        lax.fori_loop(0, tiles, tile, 0)

    def summed(buf, got, base):
        def tile(i, carry):
            f = block_of(i, tw)
            part = mm(nmT[core], gb[:, pl.ds(pl.multiple_of(base + i * tw, 128), tw)])
            buf[:, f] = (part + got[:, f].astype(F32)).astype(BF16)
            return carry

        lax.fori_loop(0, tiles, tile, 0)

    dn_copy = remote(dns, dnr, ss.at[0], sr.at[0], at.sib)
    gate_copy = remote(gus, gur, ss.at[1], sr.at[1], at.sib)
    up_copy = remote(uus, uur, ss.at[2], sr.at[2], at.sib)

    def dn_other(i, carry):
        dns[block_of(i, piece), :] = mm(dn_rows(1 - core, i), cotall[...]).astype(BF16)
        return carry

    lax.fori_loop(0, nz, dn_other, 0)
    dn_copy.start()
    other(gus, 0)
    gate_copy.start()
    other(uus, n)
    up_copy.start()
    dn_copy.wait_recv()

    def dn_mine_sum(i, carry):
        r = block_of(i, piece)
        dnown[r, :] = (mm(dn_rows(core, i), cotall[...]) + dnr[r, :].astype(F32)).astype(BF16)
        return carry

    lax.fori_loop(0, nz, dn_mine_sum, 0)
    dn_sum.start()
    gate_copy.wait_recv()
    summed(gateown, gur, 0)
    up_copy.wait_recv()
    summed(upown, uur, n)
    gate_sum.start()

    gnm = sum_nm.total(gown[...])
    sum_nm.drain()
    residual = resid[...]
    scale_mid = lax.rsqrt(jnp.mean(residual * residual, axis=-1, keepdims=True) + EPSILON)
    gsecond[...] = jnp.broadcast_to(jnp.sum(gnm * residual * scale_mid, axis=0, keepdims=True), (8, width))
    weighted = gnm * gain_mid
    gown[...] = (
        cotall[own, :].astype(F32)
        + scale_mid * weighted
        - residual * (scale_mid * scale_mid * scale_mid) * jnp.mean(weighted * residual, axis=-1, keepdims=True)
    )
    rback = gown[...].astype(BF16)

    def mixed_back(p):
        return remote(gmr.at[p], grows.at[own], bs.at[p], br.at[s], (d, p))

    for p in range(ns):
        gmr[p] = mm_nt(rback, wout[p * qw : (p + 1) * qw, :]).astype(BF16)
        pl.when(s != p)(mixed_back(p).start)
    grows[own, :] = gmr[s]

    dn_sum.relay()
    for k in range(nd):
        nmT[k % 2, (k // 2) * R : (k // 2 + 1) * R, :] = mm(mrowsT[k * R : (k + 1) * R, :], rback).astype(BF16)
    go_copy = remote(nmT.at[1 - core], gor, ss2.at[0], sr2.at[0], at.sib)
    go_copy.start()
    for i in range(hk):
        qrows[i, :, :] = jnp.transpose(qT[i * group * HD : (i + 1) * group * HD, :])
    go_copy.wait_recv()
    gate_copy.wait_send()
    up_copy.wait_send()
    for p in range(ns):
        c = pl.ds(p * cw, cw)
        gu[0:half_gu, c] = (nmT[core, :, c].astype(F32) + gor[:, c].astype(F32)).astype(BF16)

    for j in range(1, ns):
        src = at.seq_from(j)
        remote(gmr.at[0], grows.at[block_of(src, T)], bs.at[0], br.at[src], (d, src)).wait_recv()
    for i in range(ns):
        rows = pl.ds(i * T, T)
        hT[pw : pw + qw, rows] = jnp.transpose(grows[rows, :])

    def gout_copy(j):
        return remote(gu.at[pl.ds(0, half_gu), block_of(at.seq_to(j)[1], cw)], gorecv.at[j - 1], gos.at[j], gorc.at[j], at.seq_to(j))

    sum_outputs = SeqReduce(at, T, osend, xall, (os_, or_))
    for j in range(1, ns):
        sum_outputs.push(j)
    for j in range(1, ns):
        gout_copy(j).start()

    causal = lax.broadcasted_iota(jnp.int32, (T, T), 0) <= lax.broadcasted_iota(jnp.int32, (T, T), 1)
    causal = jnp.concatenate([causal] * group, axis=1)
    gk[...] = jnp.zeros_like(gk)
    gv[...] = jnp.zeros_like(gv)

    def key_head(kv, carry):
        krow = block_of(kv, HD)
        lanes = block_of(kv, group * HD)
        for rb in range(ns):
            cols = pl.ds(rb * T, T)

            def side(ref, base):
                return jnp.concatenate(
                    [ref[pl.ds(pl.multiple_of(base + (kv * group + u) * HD, HD), HD), cols] for u in range(group)],
                    axis=1,
                )

            q, g = side(qT, 0), side(hT, pw)
            one = jnp.concatenate([inv[kv * group + u, :, cols] for u in range(group)], axis=1)
            m = jnp.concatenate(
                [mixT[rb, block_of(kv * group + u, HD), :] for u in range(group)], axis=1
            )
            delta = jnp.sum(g.astype(F32) * m.astype(F32), axis=0, keepdims=True)
            gr, qr = grows[cols, lanes], qrows[kv, cols, :]
            gr = jnp.concatenate([gr[:, u * HD : (u + 1) * HD] for u in range(group)], axis=0)
            qr = jnp.concatenate([qr[:, u * HD : (u + 1) * HD] for u in range(group)], axis=0)
            gq = jnp.zeros((HD, group * T), F32)
            for part, masked in ((pl.ds(0, rb * T), False), (cols, True)):
                if rb == 0 and not masked:
                    continue
                p = jnp.exp(mm(krows[kv, part, :], q)) * one
                if masked:
                    p = jnp.where(causal, p, 0.0)
                gp = mm(vrows[kv, part, :], g)
                ds = (p * (gp - delta)).astype(BF16)
                gv[kv, part, :] += mm(p.astype(BF16), gr)
                gk[kv, part, :] += mm(ds, qr)
                gq = gq + mm(kT[krow, part], ds)
            gq = gq * HD**-0.5
            for u in range(group):
                gqT[block_of(kv * group + u, HD), cols] = gq[:, u * T : (u + 1) * T]
        return carry

    lax.fori_loop(0, hk, key_head, 0)

    sum_outputs.hop()
    columns = jnp.transpose(gsum[:, : 2 * HD])
    gain_q, gain_k = columns[:HD, 2:3], columns[HD:, 2:3]

    def norm_column(row, g, gain):
        a, b = g[:half], g[half:]
        g = jnp.concatenate([a * cos[...] + b * sin[...], b * cos[...] - a * sin[...]], axis=0)
        u = projT[row, :]
        scale = lax.rsqrt(jnp.mean(u * u, axis=0, keepdims=True) + EPSILON)
        us = u * scale
        weighted = g * gain
        inner = jnp.mean(weighted * us, axis=0, keepdims=True)
        hT[row, :] = (scale * (weighted - us * inner)).astype(BF16)
        return jnp.sum(g * us, axis=1, keepdims=True)

    def query_back(h, acc):
        row = block_of(h, HD)
        return acc + norm_column(row, gqT[row, :], gain_q)

    gain_grad_q = lax.fori_loop(0, hq, query_back, jnp.zeros((HD, 1), F32))
    gain_grad_k = jnp.zeros((HD, 1), F32)
    for i in range(hk):
        gain_grad_k = gain_grad_k + norm_column(pl.ds(qw + i * HD, HD), jnp.transpose(gk[i]), gain_k)
        hT[qw + kw + i * HD : qw + kw + (i + 1) * HD, :] = jnp.transpose(gv[i]).astype(BF16)

    gate_sum.relay()
    up_sum.start()

    sum_ni = SeqReduce(at, T, gsend, grecv, (nis, nir))
    for i in range(ns):
        rows = pl.ds(i * T, T)
        cotall[rows, 0:pw] = jnp.transpose(hT[0:pw, rows])
    for j in list(range(1, ns)) + [0]:
        part = mm_nt(cotall[block_of(at.reduce_rank(j), T), 0:pw], wqkv[...])
        if j:
            gsend[pl.ds((j - 1) * T, T), :] = part.astype(BF16)
            sum_ni.push(j)
        else:
            resid[...] = part
    for k in range(nd):
        part = mm(hT[0:pw, :], normed[:, k * R : (k + 1) * R])
        gb[((k % 2) * nz + k // 2) * R : ((k % 2) * nz + k // 2 + 1) * R, 0:pw] = jnp.transpose(part).astype(BF16)
    qk_copy = remote(gb.at[block_of(1 - core, nz * R), pl.ds(0, pw)], qkr, ss2.at[1], sr2.at[1], at.sib)
    qk_copy.start()
    sum_ni.hop()
    dn_sum.total()
    for j in range(1, ns):
        gout_copy(j).wait_recv()
    acc = gu[0:half_gu, block_of(s, cw)].astype(F32)
    for j in range(1, ns):
        acc = acc + gorecv[j - 1].astype(F32)
    goown[...] = acc.astype(BF16)
    out_sum.start()
    qk_copy.wait_recv()
    qkown[...] = (gb[block_of(core, nz * R), pl.ds(0, pw)].astype(F32) + qkr[...].astype(F32)).astype(BF16)
    qkv_sum.start()
    up_sum.relay()
    out_sum.relay()
    gate_sum.total()
    qkv_sum.relay()

    gni = sum_ni.total(resid[...])
    dn_sum.share.hop()
    stream = x[...].astype(F32)
    scale = lax.rsqrt(jnp.mean(stream * stream, axis=-1, keepdims=True) + EPSILON)
    unit = stream * scale
    weighted = gni * gsum[0:1, :]
    gown[...] = gown[...] + scale * (weighted - unit * jnp.mean(weighted * unit, axis=-1, keepdims=True))
    stream_store = pltpu.make_async_copy(gown, gstream, loc.at[2])
    stream_store.start()
    first = jnp.sum(gni * unit, axis=0, keepdims=True)
    qk = jnp.broadcast_to(jnp.concatenate([gain_grad_q, gain_grad_k], axis=0), (2 * HD, 128))
    sm0[0:1, :] = first
    sm0[1:2, :] = gsecond[0:1, :]
    sm0[2:8, :] = jnp.zeros((6, width), F32)
    sm0[2:3, : 2 * HD] = jnp.transpose(qk)[0:1, :]

    def small_seq(j):
        return remote(sm0, sm1.at[j - 1], s1.at[j], r1.at[j], at.seq_to(j))

    def small_dp(j):
        return remote(sm2, sm3.at[j - 1], s2.at[j], r2.at[j], at.dp_to(j))

    for j in range(1, ns):
        small_seq(j).start()
    gate_sum.share.hop()
    up_sum.total()
    acc = sum_outputs.total(oown[...])
    last = pl.ds((ns - 1) * T, T)
    xall[last, :] = acc.astype(BF16)
    out_store = pltpu.make_async_copy(xall.at[last], outputs, loc.at[1])
    out_store.start()
    for j in range(1, ns):
        small_seq(j).wait_recv()
    acc = sm0[...]
    for j in range(1, ns):
        acc = acc + sm1[j - 1]
    sm2[...] = acc
    for j in range(1, nd):
        small_dp(j).start()
    out_sum.total()
    qkv_sum.total()
    up_sum.share.hop()
    out_sum.share.hop()
    qkv_sum.share.hop()
    for j in range(1, nd):
        small_dp(j).wait_recv()
    for j in range(1, nd):
        acc = acc + sm3[j - 1]
    small[...] = acc

    for p in range(ns):
        pl.when(s != p)(mixed_back(p).wait_send)
    go_copy.wait_send()
    qk_copy.wait_send()
    for j in range(1, ns):
        gout_copy(j).wait_send()
        small_seq(j).wait_send()
    for j in range(1, nd):
        small_dp(j).wait_send()
    for rb in range(ns):
        pl.when(s != rb)(mixed_out(rb).wait_send)
    for t in (sum_outputs, sum_ni):
        t.drain()
    for c in g_copies + [dn_copy]:
        c.wait_send()
    for t in (take_qkv, take_out):
        t.drain()
    for t in (dn_sum, out_sum, qkv_sum, gate_sum, up_sum):
        t.drain()
    out_store.wait()
    stream_store.wait()


def vmem(n):
    return [pl.BlockSpec(memory_space=pltpu.VMEM)] * n


def block(ns, nd, piece, x, gain1, gain2, gainqk, w_qkv, w_out, cot, w_gate, w_up, w_down):
    T, width = x.shape
    L = ns * T
    R = w_qkv.shape[0]
    n = nd * piece
    n2 = 2 * n
    nz = nd // 2
    hq, hk = H // ns, KV // ns
    qw, kw = hq * HD, hk * HD
    pw = qw + 2 * kw
    cw = width // ns
    cos, sin = rope_columns(L)
    sh, vm = jax.ShapeDtypeStruct, pltpu.VMEM
    outs = (
        sh((T, width), BF16), sh((T, width), F32), sh((ns, R, n), BF16), sh((ns, R, n), BF16),
        sh((ns, piece, width), BF16), sh((ns, R, pw), BF16), sh((ns, R, cw), BF16), sh((8, width), F32),
    )
    hbm = pl.BlockSpec(memory_space=pl.ANY)
    scratch = [
        vm((L, width), BF16), vm((qw + kw, L), F32), vm((qw, L), BF16), vm((kw, L), BF16),
        vm((hk, L, HD), BF16), vm((hk, L, HD), BF16), vm((hq, 1, L), F32), vm((ns, qw, T), BF16),
        vm((H * HD, T), BF16), vm((H * HD, width), BF16), vm((width, pw), BF16), vm((8, width), F32),
        vm(((ns - 1) * T, width), BF16), vm((T, width), F32), vm((8, width), F32),
        vm((kw, L), BF16), vm((T, width), F32), vm((L, width), BF16), vm((L, width), BF16), vm((8, 128), F32),
        vm((nd, 8, 128), F32), vm((R, pw), BF16), vm((R, n2), BF16), vm((nd * R, n2), BF16), vm((n, width), BF16),
        vm((T, n), BF16), vm((n, L), BF16), vm((L, n2), BF16), vm(((ns - 1) * T, width), BF16),
        vm(((ns - 1) * T, width), BF16), vm((T, width), F32), vm((2, nz * R, L), BF16),
        vm((nz * R, n), BF16), vm((nz * R, n), BF16), vm((nz * piece, width), BF16),
        vm((nz, R, n), BF16), vm((R, n), BF16), vm((nz, R, n), BF16), vm((R, n), BF16),
        vm((nz, piece, width), BF16), vm((piece, width), BF16), vm((ns, T, qw), BF16), vm((L, qw), BF16),
        vm((hk, L, qw // hk), BF16), vm((hk, L, HD), F32), vm((hk, L, HD), F32), vm((qw, L), F32),
        vm((nz * R, pw), BF16), vm((nz * R, pw), BF16), vm((nz, R, pw), BF16), vm((R, pw), BF16),
        vm((nz * R, width), BF16), vm((ns - 1, nz * R, cw), BF16), vm((nz * R, cw), BF16),
        vm((nz, R, cw), BF16), vm((R, cw), BF16),
        vm((8, width), F32), vm((ns - 1, 8, width), F32), vm((8, width), F32), vm((nd - 1, 8, width), F32),
    ]
    sems = seq_sems(ns) + [DMA((nd,)), DMA((nd,))] + seq_sems(ns) + [DMA((ns,))] * 2 + seq_sems(ns) * 2
    sems += [DMA((3,)), DMA((3,))]
    sems += [DMA((3,)), DMA((2, 8))]
    sems += seq_sems(ns) + [DMA((ns,))] * 2 + seq_sems(ns) + [DMA((2,)), DMA((2,))] + [DMA((ns,))] * 4 + [DMA((nd,)), DMA((nd,))]
    return pl.pallas_call(
        functools.partial(block_kernel, ns, nd),
        out_shape=outs,
        in_specs=vmem(5) + [hbm] * 5 + vmem(2),
        out_specs=[hbm] * 7 + vmem(1),
        scratch_shapes=scratch + sems + gather_sems(nz) * 4 + scatter_sems(ns, nz) * 5 + gather_sems(nz),
        compiler_params=pltpu.CompilerParams(
            collective_id=0, has_side_effects=True, vmem_limit_bytes=VMEM_LIMIT
        ),
        cost_estimate=pl.CostEstimate(flops=38_000_000_000, bytes_accessed=40_000_000, transcendentals=12_000_000),
    )(x, gain1, gain2, gainqk, w_qkv, w_out, cot, w_gate, w_up, w_down, cos, sin)


def finish_kernel(
    ns, nd, piece, gateall, upall, qkvall, outall, dnall, got, stream, sums,
    gate, up, qkv, out, down, outputs, gstream, first, second, qk,
):
    outputs[...] = got[...]
    gstream[...] = stream[...]
    d = lax.axis_index("dp")
    for k in range(nd):

        @pl.when(d == k)
        def _():
            for i, ref in enumerate((first, second, qk)):
                w = ref.shape[1]
                ref[...] = sums[i : i + 1, k * w : (k + 1) * w]

    hq, hk = H // ns, KV // ns
    qw, kw = hq * HD, hk * HD
    pad = gateall.shape[2] // nd
    for ref, got in ((gate, gateall), (up, upall)):
        parts = [got[i].astype(F32) for i in range(ns)]
        ref[...] = jnp.concatenate(
            [parts[i][:, k * pad : k * pad + piece] for k in range(nd) for i in range(ns)], axis=1
        )
    parts = [qkvall[i].astype(F32) for i in range(ns)]
    qkv[...] = jnp.concatenate(
        [p[:, :qw] for p in parts] + [p[:, qw : qw + kw] for p in parts] + [p[:, qw + kw :] for p in parts], axis=1
    )
    out[...] = jnp.concatenate([outall[i].astype(F32) for i in range(ns)], axis=1)
    down[...] = jnp.concatenate([dnall[i].astype(F32)[:piece] for i in range(dnall.shape[0])], axis=0)


def finish(ns, nd, piece, gateall, upall, qkvall, outall, dnall, got, stream, sums):
    R = gateall.shape[1]
    T, width = got.shape
    steps = 4
    rows = R // steps
    ff = ns * nd * piece
    widths = (ff, ff, ns * qkvall.shape[2], ns * outall.shape[2])
    many = ns // steps
    lines = (R, R, 2 * HD // nd)
    ins = [pl.BlockSpec((ns, rows, a.shape[2]), lambda i: (0, i, 0)) for a in (gateall, upall, qkvall, outall)]
    ins.append(pl.BlockSpec((many,) + dnall.shape[1:], lambda i: (i, 0, 0)))
    tokens = pl.BlockSpec((T // steps, width), lambda i: (i, 0))
    ins += [tokens, tokens, pl.BlockSpec((8, width), lambda i: (0, 0))]
    outs = [pl.BlockSpec((rows, w), lambda i: (i, 0)) for w in widths]
    outs += [pl.BlockSpec((many * piece, width), lambda i: (i, 0)), tokens, tokens]
    outs += [pl.BlockSpec((1, w), lambda i: (0, 0)) for w in lines]
    sh = jax.ShapeDtypeStruct
    return pl.pallas_call(
        functools.partial(finish_kernel, ns, nd, piece),
        grid=(steps,),
        out_shape=[sh((R, w), F32) for w in widths]
        + [sh((ns * piece, width), F32), sh((T, width), BF16), sh((T, width), F32)]
        + [sh((1, w), F32) for w in lines],
        in_specs=ins,
        out_specs=outs,
        compiler_params=pltpu.CompilerParams(vmem_limit_bytes=VMEM_LIMIT),
    )(gateall, upall, qkvall, outall, dnall, got, stream, sums)


def shards(inputs, cotangent, first_gain, w_qkv, qk_gain, w_out, second_gain, w_gate, w_up, w_down):
    ns, nd = lax.axis_size("seq"), lax.axis_size("dp")
    s, d = lax.axis_index("seq"), lax.axis_index("dp")
    piece = w_down.shape[0] // ns
    pad = -piece % 16
    down_rows = w_down
    if pad:
        down_rows = jnp.pad(lax.dynamic_slice_in_dim(w_down, s * piece, piece, 0), ((0, pad), (0, 0)))
    x = inputs[0]
    outputs, gstream, gateall, upall, dnall, qkvall, outall, small = block(
        ns, nd, piece + pad, x, first_gain[None], second_gain[None], qk_gain[None], w_qkv, w_out, cotangent[0],
        w_gate, w_up, down_rows,
    )
    gate, up, qkv, out, down, outputs, gstream, first, second, qk = finish(
        ns, nd, piece, gateall, upall, qkvall, outall, dnall, outputs, gstream, small
    )
    return (outputs[None], gstream[None], first[0], qkv, qk[0], out, second[0], gate, up, down)


def solution(mesh):
    act = P("dp", "seq", None)
    vec, mat = P("dp"), P("dp", None)
    in_specs = (act, act, vec, mat, vec, mat, vec, mat, mat, mat)
    out_specs = (act, act, vec, mat, vec, mat, vec, mat, mat, mat)
    return jax.shard_map(shards, mesh=mesh, in_specs=in_specs, out_specs=out_specs, check_vma=False)
```

```python
import functools

import jax
import jax.numpy as jnp
import numpy as np
from jax import lax
from jax.experimental import pallas as pl
from jax.experimental.pallas import tpu as pltpu
from jax.sharding import PartitionSpec as P

H = 16
KV = 8
HD = 64
EPSILON = 1e-06
THETA_BASE = 1000000.0
F32 = jnp.float32
BF16 = jnp.bfloat16
VMEM_LIMIT = 65000 << 10


def rope_columns(length):
    inverse = np.float32(THETA_BASE) ** (-np.arange(0, HD, 2).astype(np.float32) / np.float32(HD))
    angles = (np.arange(length, dtype=np.float32)[None, :] * inverse.astype(np.float32)[:, None]).astype(np.float32)
    angles = angles.astype(np.float64)
    return jnp.asarray(np.cos(angles), F32), jnp.asarray(np.sin(angles), F32)


MESH = pl.DeviceIdType.MESH
DMA = pltpu.SemaphoreType.DMA


def mm(a, b):
    return jnp.dot(a, b, preferred_element_type=F32)


def mm_nt(a, b):
    return lax.dot_general(a, b, (((1,), (1,)), ((), ())), preferred_element_type=F32)


def remote(src, dst, send, recv, device):
    return pltpu.make_async_remote_copy(
        src_ref=src, dst_ref=dst, send_sem=send, recv_sem=recv, device_id=device, device_id_type=MESH
    )


def block_of(index, size):
    return pl.ds(pl.multiple_of(index * size, size), size)


class Place:
    def __init__(self, ns, nd):
        self.ns, self.nd, self.nz = ns, nd, nd // 2
        self.d, self.s = lax.axis_index("dp"), lax.axis_index("seq")
        self.zz, self.core = self.d // 2, lax.rem(self.d, 2)
        self.sib = (self.d + 1 - 2 * self.core, self.s)

    def seq_to(self, j):
        return (self.d, lax.rem(self.s + j, self.ns))

    def seq_from(self, j):
        return lax.rem(self.s + self.ns - j, self.ns)

    def across(self):
        return (self.s + 1 - 2 * lax.rem(self.s, 2), lax.rem(self.s + 2, 4), 3 - self.s)

    def gather_rank(self, j):
        if j == 0:
            return self.s
        return self.across()[j - 1] if self.ns == 4 else self.seq_from(j)

    def reduce_rank(self, j):
        if j == 0:
            return self.s
        x, y, o = self.across()
        return (o, x, y)[j - 1] if self.ns == 4 else lax.rem(self.s + j, self.ns)

    def dp_to(self, j):
        return (lax.rem(self.d + j, self.nd), self.s)

    def z_index(self, j):
        return lax.rem(self.zz + j, self.nz)

    def z_from(self, j):
        return lax.rem(self.zz + self.nz - j, self.nz)

    def z_device(self, z):
        return (2 * z + self.core, self.s)

    def greet(self):
        bar = pltpu.get_barrier_semaphore()
        for j in range(1, self.nd):
            pl.semaphore_signal(bar, inc=1, device_id=self.dp_to(j), device_id_type=MESH)
        for j in range(1, self.ns):
            pl.semaphore_signal(bar, inc=1, device_id=self.seq_to(j), device_id_type=MESH)
        pl.semaphore_wait(bar, self.nd + self.ns - 2)


class SeqGather:
    def __init__(self, at, src, dst, sems):
        self.at, self.src, self.dst = at, src, dst
        self.send, self.recv = sems
        self.half = src.shape[0] // 2

    def direct(self, j):
        at = self.at
        to = at.across()[j - 1] if at.ns == 4 else at.seq_to(j)[1]
        return remote(self.src, self.dst(at.s), self.send.at[j], self.recv.at[j], (at.d, to))

    def forward(self, i):
        at = self.at
        part = self.dst(at.across()[i]).at[pl.ds(i * self.half, self.half)]
        return remote(part, part, self.send.at[3 + i], self.recv.at[3 + i], (at.d, at.across()[1 - i]))

    def near(self):
        return range(1, 3 if self.at.ns == 4 else self.at.ns)

    def start(self):
        for j in self.near():
            self.direct(j).start()

    def hop(self):
        if self.at.ns == 4:
            for i in range(2):
                self.direct(i + 1).wait_recv()
                self.forward(i).start()

    def wait(self, j):
        if self.at.ns != 4:
            self.direct(j).wait_recv()
        elif j == 3:
            for i in range(2):
                self.forward(i).wait_recv()

    def finish(self):
        for j in range(1, self.at.ns):
            self.wait(j)

    def drain(self):
        for j in self.near():
            self.direct(j).wait_send()
        if self.at.ns == 4:
            for i in range(2):
                self.forward(i).wait_send()


def seq_sems(ns):
    return [DMA((max(ns, 6),)), DMA((max(ns, 6),))]


class SeqReduce:
    def __init__(self, at, rows, stage, inbox, sems):
        self.at, self.rows, self.stage, self.inbox = at, rows, stage, inbox
        self.send, self.recv = sems

    def part(self, ref, block, half=None):
        if half is None:
            return ref.at[pl.ds(block * self.rows, self.rows)]
        h = self.rows // 2
        return ref.at[pl.ds(block * self.rows + half * h, h)]

    def leg(self, k):
        at = self.at
        if at.ns != 4:
            src, dst, to = self.part(self.stage, k - 1), self.part(self.inbox, k - 1), at.seq_to(k)[1]
        else:
            b, h, i, n = ((0, 0, 2, 0), (0, 1, 2, 1), (1, 0, 0, 0), (2, 1, 1, 1), (2, 0, 1, 1), (1, 1, 0, 0))[k]
            src, dst, to = self.part(self.stage, b, h), self.part(self.inbox, i, h), at.across()[n]
        return remote(src, dst, self.send.at[k], self.recv.at[k], (at.d, to))

    def push(self, j):
        for k in (j,) if self.at.ns != 4 else ((), (0, 1), (2,), (3,))[j]:
            self.leg(k).start()

    def hop(self):
        if self.at.ns != 4:
            return
        h = self.rows // 2
        for k, b in ((0, 2), (1, 1)):
            self.leg(k).wait_recv()
            mine, came = pl.ds(b * self.rows + k * h, h), pl.ds(2 * self.rows + k * h, h)
            self.stage[mine, :] = (self.stage[mine, :].astype(F32) + self.inbox[came, :].astype(F32)).astype(BF16)
            self.leg(4 + k).start()

    def total(self, acc):
        four = self.at.ns == 4
        for k in range(2, 6) if four else range(1, self.at.ns):
            self.leg(k).wait_recv()
        for b in range(2 if four else self.at.ns - 1):
            acc = acc + self.inbox[b * self.rows : (b + 1) * self.rows, :].astype(F32)
        return acc

    def drain(self):
        for k in range(6) if self.at.ns == 4 else range(1, self.at.ns):
            self.leg(k).wait_send()


class Gather:
    def __init__(self, at, src, dst, sems):
        self.at, self.src, self.dst = at, src, dst
        self.send, self.recv, self.fsend, self.frecv, self.rsend, self.local = sems
        self.rows = src.shape[0]
        nz = at.nz
        self.order = [1, nz - 1] + list(range(2, nz - 1))

    def piece(self, z):
        return self.dst.at[block_of(2 * z + self.at.core, self.rows)]

    def direct(self, j):
        at = self.at
        return remote(self.src, self.piece(at.zz), self.send.at[j], self.recv.at[j], at.z_device(at.z_index(j)))

    def near(self, j):
        at = self.at
        z = at.z_index(j)
        away = z - at.zz
        return ((z > 0) & (z < at.nz - 1)) | (away == 1) | (away == -1)

    def across(self, j):
        piece = self.src if j == 0 else self.piece(self.at.z_from(j))
        return remote(piece, self.piece(self.at.z_from(j)), self.fsend.at[j], self.frecv.at[j], self.at.sib)

    def relay(self, j):
        nz = self.at.nz
        out = []
        for k, (here, end) in enumerate(((1, 0), (nz - 2, nz - 1))):
            origin = (here - j) % nz
            if origin != end:
                piece = self.piece(origin)
                index = (end - origin) % nz
                copy = remote(piece, piece, self.rsend.at[k, j], self.recv.at[index], self.at.z_device(end))
                out.append((self.at.zz == here, copy))
        return out

    def mine(self):
        return pltpu.make_async_copy(self.src, self.dst.at[block_of(self.at.d, self.rows)], self.local.at[0])

    def start(self):
        for j in self.order[2:] + self.order[:2]:
            pl.when(self.near(j))(self.direct(j).start)
        self.across(0).start()
        self.mine().start()

    def hop(self):
        at = self.at

        @pl.when((at.zz == 1) | (at.zz == at.nz - 2))
        def _():
            for j in self.order:
                self.direct(j).wait_recv()
                for here, copy in self.relay(j):
                    pl.when(here)(copy.start)
                self.across(j).start()

    def arrive(self):
        at = self.at

        @pl.when((at.zz != 1) & (at.zz != at.nz - 2))
        def _():
            for j in self.order:
                self.direct(j).wait_recv()
                self.across(j).start()

    def finish(self):
        for j in range(self.at.nz):
            self.across(j).wait_recv()
        self.mine().wait()

    def drain_own(self):
        self.across(0).wait_send()
        for j in range(1, self.at.nz):
            pl.when(self.near(j))(self.direct(j).wait_send)

    def drain_rest(self):
        for j in range(1, self.at.nz):
            self.across(j).wait_send()
            for here, copy in self.relay(j):
                pl.when(here)(copy.wait_send)

    def drain(self):
        self.drain_own()
        self.drain_rest()


def gather_sems(nz):
    return [DMA((nz,)), DMA((nz,)), DMA((nz,)), DMA((nz,)), DMA((2, nz)), DMA((1,))]


class Scatter:
    def __init__(self, at, pieces, inbox, final, out, sems):
        self.at, self.pieces, self.inbox, self.final, self.out = at, pieces, inbox, final, out
        self.send, self.recv, osend, orecv, self.local, self.rsend, self.rrecv = sems
        self.rows = final.shape[0]
        self.share = SeqGather(at, final, lambda r: out.at[r], (osend, orecv))

    def piece(self, z):
        return self.pieces.at[block_of(z, self.rows)]

    def copy(self, j):
        at = self.at
        z = at.z_index(j)
        return remote(self.piece(z), self.inbox.at[j - 1], self.send.at[j], self.recv.at[j], at.z_device(z))

    def far_copy(self, target, via):
        slot = self.inbox.at[self.at.nz - 1]
        return remote(self.piece(target), slot, self.rsend.at[0], self.rrecv.at[0], self.at.z_device(via))

    def far(self):
        nz = self.at.nz
        return ((0, nz - 1, 1, nz - 2), (nz - 1, 0, nz - 2, 2))

    def near(self, away):
        return (away < self.at.nz - 1) & (away > 1 - self.at.nz)

    def free(self, j):
        go = self.near(self.at.z_index(j) - self.at.zz)
        for _, _, via, k in self.far():
            if k == j:
                go = go & (self.at.zz != via)
        return go

    def start(self):
        at = self.at
        for origin, target, via, _ in self.far():
            pl.when(at.zz == origin)(self.far_copy(target, via).start)
        for j in range(1, at.nz):
            pl.when(self.free(j))(self.copy(j).start)
            away = at.z_from(j) - at.zz

            @pl.when((away >= at.nz - 1) | (away <= 1 - at.nz))
            def _():
                self.inbox[j - 1] = jnp.zeros_like(self.inbox[j - 1])

    def relay(self):
        at = self.at
        for _, target, via, j in self.far():

            @pl.when(at.zz == via)
            def _():
                self.far_copy(target, via).wait_recv()
                rows = block_of(target, self.rows)
                both = self.pieces[rows, :].astype(F32) + self.inbox[at.nz - 1].astype(F32)
                self.pieces[rows, :] = both.astype(BF16)
                self.copy(j).start()

    def keep(self):
        return pltpu.make_async_copy(self.final, self.out.at[self.at.s], self.local.at[0])

    def total(self):
        at = self.at
        for j in range(1, at.nz):
            pl.when(self.near(at.z_from(j) - at.zz))(self.copy(j).wait_recv)
        acc = self.pieces[block_of(self.at.zz, self.rows), :].astype(F32)
        for j in range(1, self.at.nz):
            acc = acc + self.inbox[j - 1].astype(F32)
        self.final[...] = acc.astype(BF16)
        self.keep().start()
        self.share.start()

    def drain(self):
        self.keep().wait()
        self.share.finish()
        self.share.drain()
        at = self.at
        for j in range(1, at.nz):
            pl.when(self.near(at.z_index(j) - at.zz))(self.copy(j).wait_send)
        for origin, target, via, _ in self.far():
            pl.when(at.zz == origin)(self.far_copy(target, via).wait_send)


def scatter_sems(ns, nz):
    return [DMA((nz,)), DMA((nz,))] + seq_sems(ns) + [DMA((1,)), DMA((1,)), DMA((1,))]


def block_kernel(
    ns, nd, x, gain1, gain2, gainqk, wqkv_rows, wout_mine, cot, wgate, wup, wdown, cos, sin,
    outputs, gstream, gateall, upall, dnall, qkvall, outall, small,
    normed, projT, qT, kT, krows, vrows, inv, mixT, mrowsT, wout, wqkv, gsum, osend, oown, gsecond,
    vT, resid, cotall, xall, gains, gbuf, wqkv_mine, gu, dn, hrow, hT, gb, gsend, grecv, gown, nmT,
    gur, uur, dnr,
    gaz, gaf, upz, upf, dnz, dnf, grows, qrows, gk, gv, gqT, qkr, qkown, qkz, qkf,
    gor, gostage, gorecv, goown, goz, gof, sm0, sm1, sm2, sm3,
    xs, xr, gs, gr, cs, cr, ms, mr, ns_, nr, ps, pr, ss, sr, loc, wl,
    os_, or_, bs, br, nis, nir, ss2, sr2, gos, gorc, s1, r1, s2, r2, wos, wor, wok, cs2, cr2, *sems,
):
    at = Place(ns, nd)
    s, d, nz, core = at.s, at.d, at.nz, at.core
    T, width = x.shape
    L = ns * T
    R = wqkv_mine.shape[0]
    cw = width // ns
    n = dn.shape[0]
    piece = n // nd
    gl, ql = gain1.shape[1], gainqk.shape[1]
    dn_mine = wdown.at[block_of(s, piece)] if wdown.shape[0] == ns * piece else wdown
    hq, hk = H // ns, KV // ns
    group = hq // hk
    qw, kw = hq * HD, hk * HD
    own = block_of(s, T)
    pw = qw + 2 * kw
    gains[...] = jnp.zeros_like(gains)
    gains[0:1, :gl] = gain1[...]
    gains[1:2, :gl] = gain2[...]
    gains[2:3, :ql] = gainqk[...]
    for i in range(ns):

        @pl.when(s == i)
        def _():
            cuts = ((i * qw, qw), (H * HD + i * kw, kw), ((H + KV) * HD + i * kw, kw))
            wqkv_mine[...] = jnp.concatenate([wqkv_rows[:, a : a + b] for a, b in cuts], axis=1)

    at.greet()

    share_x = SeqGather(at, x, lambda r: xall.at[block_of(r, T)], (xs, xr))
    g_copies = [remote(gains, gbuf.at[d], gs.at[j], gr.at[j], at.dp_to(j)) for j in range(1, nd)]
    hw = width // 2

    def share_half(i, sem):
        c = pl.ds(i * hw, hw)
        return SeqGather(at, cot.at[:, c], lambda r: cotall.at[block_of(r, T), c], sem)

    share_cot = [share_half(0, (cs, cr)), share_half(1, (cs2, cr2))]
    share_nm = SeqGather(at, xall.at[own], lambda r: xall.at[block_of(r, T)], (ns_, nr))
    take_qkv = Gather(at, wqkv_mine, wqkv, sems[0:6])
    wo, mycols = nmT.at[0], block_of(s, cw)

    def out_z(j):
        rows = wo.at[block_of(at.zz, R), mycols]
        return remote(wout_mine.at[:, mycols], rows, sems[6].at[j], sems[7].at[j], at.z_device(at.z_index(j)))

    out_local = pltpu.make_async_copy(wout_mine.at[:, mycols], wo.at[block_of(at.zz, R), mycols], sems[11].at[0])
    share_out = SeqGather(at, wo.at[:, mycols], lambda r: wo.at[:, block_of(r, cw)], (wos, wor))

    def out_across(z):
        rows = wout.at[block_of(2 * z + core, R)]
        return remote(wo.at[pl.ds(z * R, R)], rows, sems[8].at[z], sems[9].at[z], at.sib)

    def out_keep(z):
        return pltpu.make_async_copy(wo.at[pl.ds(z * R, R)], wout.at[block_of(2 * z + core, R)], wok.at[z])

    base = L // 2
    take_gate = Gather(at, gb.at[pl.ds(base, R), pl.ds(0, n)], gu.at[:, pl.ds(0, n)], sems[12:18])
    take_up = Gather(at, gb.at[pl.ds(base, R), pl.ds(n, n)], gu.at[:, pl.ds(n, n)], sems[59:65])
    take_dn = Gather(at, dn_mine, dn, sems[18:24])
    for c in g_copies:
        c.start()
    share_x.start()
    take_qkv.start()
    for j in range(1, nz):
        out_z(j).start()
    out_local.start()
    xall[own, :] = x[...]
    gbuf[d] = gains[...]
    cot_local = pltpu.make_async_copy(cot, cotall.at[own], loc.at[0])
    cot_local.start()
    ff = wgate.shape[1]
    parts = max(1, -(-ff // (2 * n)))
    while nd % parts:
        parts += 1
    span = ff // parts
    stage = []
    for i, w in enumerate((wgate, wup)):
        for k in range(parts):
            row = pl.ds((i * parts + k) * R, R)
            stage.append(
                pltpu.make_async_copy(w.at[:, pl.ds(k * span, span)], gb.at[row, pl.ds(0, span)], wl.at[i, k])
            )
    for c in stage:
        c.start()
    for c in stage:
        c.wait()
    real = wgate.shape[1] // nd // ns
    gap = [jnp.zeros((R, piece - real), BF16)] if piece > real else []
    for i in range(ns):

        @pl.when(s == i)
        def _():
            cuts = []
            for w in range(2):
                for k in range(nd):
                    a = (k * ns + i) * real
                    row = (w * parts + a // span) * R
                    cuts += [gb[row : row + R, a % span : a % span + real]] + gap
            gb[base : base + R, :] = jnp.concatenate(cuts, axis=1)


    for c in g_copies:
        c.wait_recv()
    gain_in = jnp.concatenate([gbuf[k][0:1, :gl] for k in range(nd)], axis=1)
    gain_mid = jnp.concatenate([gbuf[k][1:2, :gl] for k in range(nd)], axis=1)
    gain_qk = jnp.concatenate([gbuf[k][2:3, :ql] for k in range(nd)], axis=1)
    gsum[...] = jnp.zeros_like(gsum)
    gsum[0:1, :] = gain_in
    gsum[1:2, :] = gain_mid
    gsum[2:3, : 2 * HD] = gain_qk
    columns = jnp.transpose(jnp.broadcast_to(gain_qk, (8, 2 * HD)))
    gain_q, gain_k = columns[:HD, 0:1], columns[HD:, 0:1]
    take_qkv.hop()
    take_gate.start()
    take_up.start()
    take_dn.start()
    for j in range(ns):
        rows = block_of(at.gather_rank(j), T)
        if j == 1:
            share_x.hop()
        if j:
            share_x.wait(j)
        xc = xall[rows, :].astype(F32)
        scale = lax.rsqrt(jnp.mean(xc * xc, axis=-1, keepdims=True) + EPSILON)
        normed[rows, :] = (xc * scale * gain_in).astype(BF16)
    for j in range(1, nz):
        out_z(j).wait_recv()
    out_local.wait()
    share_out.start()
    take_qkv.arrive()
    take_qkv.finish()
    for j in range(ns):
        rows = pl.ds(j * T, T)
        proj = mm(normed[rows, :], wqkv[...])
        projT[:, rows] = jnp.transpose(proj[:, : qw + kw])
        val = proj[:, qw + kw :]
        vT[:, rows] = jnp.transpose(val).astype(BF16)
        for i in range(hk):
            vrows[i, rows, :] = val[:, i * HD : (i + 1) * HD].astype(BF16)

    half = HD // 2

    def rope(row, gain, factor):
        u = projT[row, :]
        scale = lax.rsqrt(jnp.mean(u * u, axis=0, keepdims=True) + EPSILON)
        u = u * scale * gain
        a, b = u[:half], u[half:]
        return jnp.concatenate([a * cos[...] - b * sin[...], b * cos[...] + a * sin[...]], axis=0) * factor

    def rope_query(h, carry):
        row = block_of(h, HD)
        qT[row, :] = rope(row, gain_q, HD**-0.5).astype(BF16)
        return carry

    lax.fori_loop(0, hq, rope_query, 0)
    for i in range(hk):
        r = rope(pl.ds(qw + i * HD, HD), gain_k, 1.0)
        kT[i * HD : (i + 1) * HD, :] = r.astype(BF16)
        krows[i, :, :] = jnp.transpose(r).astype(BF16)

    share_x.drain()
    share_out.hop()
    take_gate.hop()
    keep = lax.broadcasted_iota(jnp.int32, (T, T), 0) <= lax.broadcasted_iota(jnp.int32, (T, T), 1)
    block = block_of(s, qw)

    def mixed_out(rb):
        return remote(mixT.at[rb], mrowsT.at[block], ms.at[rb], mr.at[s], (d, rb))

    for rb in range(ns):
        cols = pl.ds(rb * T, T)
        span = rb * T

        def head(h, carry):
            kv = h // group
            row, vrow = block_of(h, HD), block_of(kv, HD)
            q = qT[row, cols]
            p = jnp.where(keep, jnp.exp(mm(krows[kv, cols, :], q)), 0.0)
            tot = jnp.sum(p, axis=0, keepdims=True)
            m = mm(vT[vrow, cols], p.astype(BF16))
            if span:
                p = jnp.exp(mm(krows[kv, 0:span, :], q))
                tot = tot + jnp.sum(p, axis=0, keepdims=True)
                m = m + mm(vT[vrow, 0:span], p.astype(BF16))
            one = 1.0 / tot
            inv[h, :, cols] = one
            mixT[rb, row, :] = (m * one).astype(BF16)
            return carry

        lax.fori_loop(0, hq, head, 0)
        pl.when(s != rb)(mixed_out(rb).start)
        if rb == ns - 1:
            share_out.finish()
            for z in range(nz):
                out_across(z).start()
                out_keep(z).start()

    share_cot[0].start()
    mrowsT[block, :] = mixT[s]
    for j in range(1, ns):
        src = at.seq_from(j)
        remote(mixT.at[0], mrowsT.at[block_of(src, qw)], ms.at[0], mr.at[src], (d, src)).wait_recv()
    for z in range(nz):
        out_across(z).wait_recv()
        out_keep(z).wait()
    residual = x[...].astype(F32) + mm(jnp.transpose(mrowsT[...]), wout[...])
    resid[...] = residual
    scale_mid = lax.rsqrt(jnp.mean(residual * residual, axis=-1, keepdims=True) + EPSILON)
    xall[own, :] = (residual * scale_mid * gain_mid).astype(BF16)
    share_nm.start()
    take_up.hop()
    share_nm.hop()
    share_cot[0].hop()
    share_cot[1].start()
    take_dn.hop()
    take_gate.arrive()
    take_up.arrive()
    share_nm.finish()
    ft, nt, wt = n, 1, width

    def pre_part(base):
        def pre_block(j, carry):
            rows = block_of(j, T)
            for i in range(nt):
                f = pl.ds(base + i * ft, ft)
                gb[rows, f] = mm(xall[rows, :], gu[:, f]).astype(BF16)
            return carry

        lax.fori_loop(0, ns, pre_block, 0)

    take_gate.drain_own()
    take_up.drain_own()
    take_gate.finish()
    take_up.finish()
    pre_part(0)
    pre_part(n)
    share_nm.drain()
    share_out.drain()
    for z in range(nz):
        out_across(z).wait_send()
    for k in range(nd):
        nmT[k % 2, (k // 2) * R : (k // 2 + 1) * R, :] = jnp.transpose(xall[:, k * R : (k + 1) * R])
    share_cot[1].hop()
    take_dn.arrive()
    take_dn.finish()
    share_cot[0].finish()
    share_cot[1].finish()
    cot_local.wait()
    sum_nm = SeqReduce(at, T, gsend, grecv, (ps, pr))
    for j in list(range(1, ns)) + [0]:
        if j == 0:
            sum_nm.hop()
        rows = block_of(at.reduce_rank(j), T)
        stage = pl.ds((j - 1) * T, T)

        def hidden_tile(i, carry):
            f, f2 = block_of(i, ft), block_of(i + nt, ft)
            gate, up = gb[rows, f].astype(F32), gb[rows, f2].astype(F32)
            sig = 1.0 / (1.0 + jnp.exp(-gate))
            act = gate * sig
            back = mm_nt(cotall[rows, :], dn[f, :])
            hid = act * up
            hrow[:, f] = hid.astype(BF16)
            hid = jnp.transpose(hid.astype(BF16))
            for k in range(nd):
                first = (k % 2) * nz * piece + (k // 2) * piece
                hT[first : first + piece, rows] = hid[k * piece : (k + 1) * piece]
            gb[rows, f] = (back * up * sig * (1.0 + gate * (1.0 - sig))).astype(BF16)
            gb[rows, f2] = (back * act).astype(BF16)
            return carry

        lax.fori_loop(0, nt, hidden_tile, 0)

        def back_tile(i, carry):
            w = block_of(i, wt)
            part = mm_nt(gb[rows, :], gu[w, :])
            if j:
                gsend[stage, w] = part.astype(BF16)
            else:
                gown[:, w] = part
            return carry

        lax.fori_loop(0, width // wt, back_tile, 0)
        if j:
            sum_nm.push(j)

        def out_tile(i, carry):
            w = block_of(i, wt)
            part = mm(hrow[...], dn[:, w])
            if j:
                osend[stage, w] = part.astype(BF16)
            else:
                oown[:, w] = part + resid[:, w]
            return carry

        lax.fori_loop(0, width // wt, out_tile, 0)

    share_cot[0].drain()
    share_cot[1].drain()
    take_gate.drain_rest()
    take_up.drain_rest()
    take_dn.drain()
    half_gu, half_dn = nz * R, nz * piece
    dns, dnown = dn.at[pl.ds(0, half_dn)], dn.at[pl.ds(half_dn, half_dn)]
    gus, gateown = (gu.at[pl.ds(i * half_gu, half_gu), pl.ds(0, n)] for i in range(2))
    uus, upown = (gu.at[pl.ds(i * half_gu, half_gu), pl.ds(n, n)] for i in range(2))
    dn_sum = Scatter(at, dnown, dnz, dnf, dnall, sems[24:31])
    gate_sum = Scatter(at, gateown, gaz, gaf, gateall, sems[31:38])
    up_sum = Scatter(at, upown, upz, upf, upall, sems[38:45])
    qkv_sum = Scatter(at, qkown, qkz, qkf, qkvall, sems[45:52])
    out_sum = Scatter(at, goown, goz, gof, outall, sems[52:59])

    def dn_part(c, i):
        return mm(hT[block_of(c, nz * piece), :], cotall[:, block_of(i, 512)])

    tiles = n // 384
    tw = n // tiles

    def other(buf, base):
        def tile(i, carry):
            f = block_of(i, tw)
            buf[:, f] = mm(nmT[1 - core], gb[:, pl.ds(pl.multiple_of(base + i * tw, 128), tw)]).astype(BF16)
            return carry

        lax.fori_loop(0, tiles, tile, 0)

    def summed(buf, got, base):
        def tile(i, carry):
            f = block_of(i, tw)
            part = mm(nmT[core], gb[:, pl.ds(pl.multiple_of(base + i * tw, 128), tw)])
            buf[:, f] = (part + got[:, f].astype(F32)).astype(BF16)
            return carry

        lax.fori_loop(0, tiles, tile, 0)

    dn_copy = remote(dns, dnr, ss.at[0], sr.at[0], at.sib)
    gate_copy = remote(gus, gur, ss.at[1], sr.at[1], at.sib)
    up_copy = remote(uus, uur, ss.at[2], sr.at[2], at.sib)

    def dn_other(i, carry):
        dns[:, block_of(i, 512)] = dn_part(1 - core, i).astype(BF16)
        return carry

    def dn_mine(i, carry):
        dnown[:, block_of(i, 512)] = dn_part(core, i).astype(BF16)
        return carry

    lax.fori_loop(0, width // 512, dn_other, 0)
    dn_copy.start()
    lax.fori_loop(0, width // 512, dn_mine, 0)
    dn_copy.wait_recv()
    dnown[...] = (dnown[...].astype(F32) + dnr[...].astype(F32)).astype(BF16)
    dn_sum.start()
    other(gus, 0)
    gate_copy.start()
    gnm = sum_nm.total(gown[...])
    sum_nm.drain()
    residual = resid[...]
    scale_mid = lax.rsqrt(jnp.mean(residual * residual, axis=-1, keepdims=True) + EPSILON)
    gsecond[...] = jnp.broadcast_to(jnp.sum(gnm * residual * scale_mid, axis=0, keepdims=True), (8, width))
    weighted = gnm * gain_mid
    gown[...] = (
        cotall[own, :].astype(F32)
        + scale_mid * weighted
        - residual * (scale_mid * scale_mid * scale_mid) * jnp.mean(weighted * residual, axis=-1, keepdims=True)
    )
    rback = gown[...].astype(BF16)

    def mixed_back(p):
        return remote(gsend.at[pl.ds(0, T), pl.ds(p * qw, qw)], grows.at[own], bs.at[p], br.at[s], (d, p))

    for p in range(ns):
        gsend[0:T, p * qw : (p + 1) * qw] = mm_nt(rback, wout[p * qw : (p + 1) * qw, :]).astype(BF16)
        pl.when(s != p)(mixed_back(p).start)
    grows[own, :] = gsend[0:T, block_of(s, qw)]

    sum_outputs = SeqReduce(at, T, osend, xall, (os_, or_))
    for j in range(1, ns):
        sum_outputs.push(j)
    other(uus, n)
    up_copy.start()
    gate_copy.wait_recv()
    summed(gateown, gur, 0)
    gate_sum.start()
    up_copy.wait_recv()
    summed(upown, uur, n)
    up_sum.start()
    for k in range(nd):
        nmT[k % 2, (k // 2) * R : (k // 2 + 1) * R, :] = mm(mrowsT[k * R : (k + 1) * R, :], rback).astype(BF16)
    go_copy = remote(nmT.at[1 - core], gor, ss2.at[0], sr2.at[0], at.sib)
    go_copy.start()
    for i in range(hk):
        qrows[i, :, :] = jnp.transpose(qT[i * group * HD : (i + 1) * group * HD, :])
    go_copy.wait_recv()
    gate_copy.wait_send()
    up_copy.wait_send()
    sum_gout = SeqReduce(at, nz * R, gostage, gorecv, (gos, gorc))

    def gout_columns(r):
        c = block_of(r, cw)
        return nmT[core, :, c].astype(F32) + gor[:, c].astype(F32)

    for j in range(1, ns):
        gostage[pl.ds((j - 1) * nz * R, nz * R), :] = gout_columns(at.reduce_rank(j)).astype(BF16)
    for j in range(1, ns):
        src = at.seq_from(j)
        remote(gsend.at[pl.ds(0, T), pl.ds(0, qw)], grows.at[block_of(src, T)], bs.at[0], br.at[src], (d, src)).wait_recv()
    for i in range(ns):
        rows = pl.ds(i * T, T)
        hT[pw : pw + qw, rows] = jnp.transpose(grows[rows, :])

    for j in range(1, ns):
        sum_gout.push(j)
    dn_sum.relay()

    causal = lax.broadcasted_iota(jnp.int32, (T, T), 0) <= lax.broadcasted_iota(jnp.int32, (T, T), 1)
    causal = jnp.concatenate([causal] * group, axis=1)
    gk[...] = jnp.zeros_like(gk)
    gv[...] = jnp.zeros_like(gv)

    def key_head(kv, carry):
        krow = block_of(kv, HD)
        lanes = block_of(kv, group * HD)
        for rb in range(ns):
            cols = pl.ds(rb * T, T)

            def side(ref, base):
                return jnp.concatenate(
                    [ref[pl.ds(pl.multiple_of(base + (kv * group + u) * HD, HD), HD), cols] for u in range(group)],
                    axis=1,
                )

            q, g = side(qT, 0), side(hT, pw)
            one = jnp.concatenate([inv[kv * group + u, :, cols] for u in range(group)], axis=1)
            m = jnp.concatenate(
                [mixT[rb, block_of(kv * group + u, HD), :] for u in range(group)], axis=1
            )
            delta = jnp.sum(g.astype(F32) * m.astype(F32), axis=0, keepdims=True)
            gr, qr = grows[cols, lanes], qrows[kv, cols, :]
            gr = jnp.concatenate([gr[:, u * HD : (u + 1) * HD] for u in range(group)], axis=0)
            qr = jnp.concatenate([qr[:, u * HD : (u + 1) * HD] for u in range(group)], axis=0)
            gq = jnp.zeros((HD, group * T), F32)
            for part, masked in ((pl.ds(0, rb * T), False), (cols, True)):
                if rb == 0 and not masked:
                    continue
                p = jnp.exp(mm(krows[kv, part, :], q)) * one
                if masked:
                    p = jnp.where(causal, p, 0.0)
                gp = mm(vrows[kv, part, :], g)
                ds = (p * (gp - delta)).astype(BF16)
                gv[kv, part, :] += mm(p.astype(BF16), gr)
                gk[kv, part, :] += mm(ds, qr)
                gq = gq + mm(kT[krow, part], ds)
            gq = gq * HD**-0.5
            for u in range(group):
                gqT[block_of(kv * group + u, HD), cols] = gq[:, u * T : (u + 1) * T]
        return carry

    lax.fori_loop(0, hk, key_head, 0)

    sum_outputs.hop()
    columns = jnp.transpose(gsum[:, : 2 * HD])
    gain_q, gain_k = columns[:HD, 2:3], columns[HD:, 2:3]

    def norm_column(row, g, gain):
        a, b = g[:half], g[half:]
        g = jnp.concatenate([a * cos[...] + b * sin[...], b * cos[...] - a * sin[...]], axis=0)
        u = projT[row, :]
        scale = lax.rsqrt(jnp.mean(u * u, axis=0, keepdims=True) + EPSILON)
        us = u * scale
        weighted = g * gain
        inner = jnp.mean(weighted * us, axis=0, keepdims=True)
        hT[row, :] = (scale * (weighted - us * inner)).astype(BF16)
        return jnp.sum(g * us, axis=1, keepdims=True)

    def query_back(h, acc):
        row = block_of(h, HD)
        return acc + norm_column(row, gqT[row, :], gain_q)

    gain_grad_q = lax.fori_loop(0, hq, query_back, jnp.zeros((HD, 1), F32))
    gain_grad_k = jnp.zeros((HD, 1), F32)
    for i in range(hk):
        gain_grad_k = gain_grad_k + norm_column(pl.ds(qw + i * HD, HD), jnp.transpose(gk[i]), gain_k)
        hT[qw + kw + i * HD : qw + kw + (i + 1) * HD, :] = jnp.transpose(gv[i]).astype(BF16)

    sum_gout.hop()
    gate_sum.relay()

    sum_ni = SeqReduce(at, T, gsend, grecv, (nis, nir))
    for p in range(ns):
        pl.when(s != p)(mixed_back(p).wait_send)
    for i in range(ns):
        rows = pl.ds(i * T, T)
        cotall[rows, 0:pw] = jnp.transpose(hT[0:pw, rows])
    for j in list(range(1, ns)) + [0]:
        part = mm_nt(cotall[block_of(at.reduce_rank(j), T), 0:pw], wqkv[...])
        if j:
            gsend[pl.ds((j - 1) * T, T), :] = part.astype(BF16)
            sum_ni.push(j)
        else:
            resid[...] = part
    for k in range(nd):
        part = mm(hT[0:pw, :], normed[:, k * R : (k + 1) * R])
        gb[((k % 2) * nz + k // 2) * R : ((k % 2) * nz + k // 2 + 1) * R, 0:pw] = jnp.transpose(part).astype(BF16)
    qk_copy = remote(gb.at[block_of(1 - core, nz * R), pl.ds(0, pw)], qkr, ss2.at[1], sr2.at[1], at.sib)
    qk_copy.start()
    sum_ni.hop()
    dn_sum.total()
    goown[...] = sum_gout.total(gout_columns(s)).astype(BF16)
    out_sum.start()
    qk_copy.wait_recv()
    qkown[...] = (gb[block_of(core, nz * R), pl.ds(0, pw)].astype(F32) + qkr[...].astype(F32)).astype(BF16)
    qkv_sum.start()
    up_sum.relay()
    out_sum.relay()
    gate_sum.total()
    qkv_sum.relay()

    gni = sum_ni.total(resid[...])
    dn_sum.share.hop()
    stream = x[...].astype(F32)
    scale = lax.rsqrt(jnp.mean(stream * stream, axis=-1, keepdims=True) + EPSILON)
    unit = stream * scale
    weighted = gni * gsum[0:1, :]
    gown[...] = gown[...] + scale * (weighted - unit * jnp.mean(weighted * unit, axis=-1, keepdims=True))
    stream_store = pltpu.make_async_copy(gown, gstream, loc.at[2])
    stream_store.start()
    first = jnp.sum(gni * unit, axis=0, keepdims=True)
    qk = jnp.broadcast_to(jnp.concatenate([gain_grad_q, gain_grad_k], axis=0), (2 * HD, 128))
    sm0[0:1, :] = first
    sm0[1:2, :] = gsecond[0:1, :]
    sm0[2:8, :] = jnp.zeros((6, width), F32)
    sm0[2:3, : 2 * HD] = jnp.transpose(qk)[0:1, :]

    def small_seq(j):
        return remote(sm0, sm1.at[j - 1], s1.at[j], r1.at[j], at.seq_to(j))

    def small_dp(j):
        return remote(sm2.at[at.dp_to(j)[0]], sm3.at[j - 1], s2.at[j], r2.at[j], at.dp_to(j))

    for j in range(1, ns):
        small_seq(j).start()
    gate_sum.share.hop()
    up_sum.total()
    acc = sum_outputs.total(oown[...])
    last = pl.ds((ns - 1) * T, T)
    xall[last, :] = acc.astype(BF16)
    out_store = pltpu.make_async_copy(xall.at[last], outputs, loc.at[1])
    out_store.start()
    for j in range(1, ns):
        small_seq(j).wait_recv()
    acc = sm0[...]
    for j in range(1, ns):
        acc = acc + sm1[j - 1]
    sm2[...] = jnp.zeros_like(sm2)
    for k in range(nd):
        sm2[k, 0:2, :gl] = acc[0:2, k * gl : (k + 1) * gl]
        sm2[k, 2:3, :ql] = acc[2:3, k * ql : (k + 1) * ql]
    for j in range(1, nd):
        small_dp(j).start()
    out_sum.total()
    qkv_sum.total()
    up_sum.share.hop()
    out_sum.share.hop()
    qkv_sum.share.hop()
    for j in range(1, nd):
        small_dp(j).wait_recv()
    acc = sm2[d]
    for j in range(1, nd):
        acc = acc + sm3[j - 1]
    small[...] = acc

    go_copy.wait_send()
    qk_copy.wait_send()
    for j in range(1, ns):
        small_seq(j).wait_send()
    for j in range(1, nd):
        small_dp(j).wait_send()
    for rb in range(ns):
        pl.when(s != rb)(mixed_out(rb).wait_send)
    for t in (sum_outputs, sum_ni, sum_gout):
        t.drain()
    for c in g_copies + [dn_copy]:
        c.wait_send()
    take_qkv.drain()
    for j in range(1, nz):
        out_z(j).wait_send()
    for t in (dn_sum, out_sum, qkv_sum, gate_sum, up_sum):
        t.drain()
    out_store.wait()
    stream_store.wait()


def vmem(n):
    return [pl.BlockSpec(memory_space=pltpu.VMEM)] * n


def block(ns, nd, piece, x, gain1, gain2, gainqk, w_qkv, w_out, cot, w_gate, w_up, w_down):
    T, width = x.shape
    L = ns * T
    R = w_qkv.shape[0]
    n = nd * piece
    n2 = 2 * n
    nz = nd // 2
    hq, hk = H // ns, KV // ns
    qw, kw = hq * HD, hk * HD
    pw = qw + 2 * kw
    cw = width // ns
    cos, sin = rope_columns(L)
    sh, vm = jax.ShapeDtypeStruct, pltpu.VMEM
    outs = (
        sh((T, width), BF16), sh((T, width), F32), sh((ns, R, n), BF16), sh((ns, R, n), BF16),
        sh((ns, piece, width), BF16), sh((ns, R, pw), BF16), sh((ns, R, cw), BF16), sh((8, 128), F32),
    )
    hbm = pl.BlockSpec(memory_space=pl.ANY)
    scratch = [
        vm((L, width), BF16), vm((qw + kw, L), F32), vm((qw, L), BF16), vm((kw, L), BF16),
        vm((hk, L, HD), BF16), vm((hk, L, HD), BF16), vm((hq, 1, L), F32), vm((ns, qw, T), BF16),
        vm((H * HD, T), BF16), vm((H * HD, width), BF16), vm((width, pw), BF16), vm((8, width), F32),
        vm(((ns - 1) * T, width), BF16), vm((T, width), F32), vm((8, width), F32),
        vm((kw, L), BF16), vm((T, width), F32), vm((L, width), BF16), vm((L, width), BF16), vm((8, 128), F32),
        vm((nd, 8, 128), F32), vm((R, pw), BF16), vm((nd * R, n2), BF16), vm((n, width), BF16),
        vm((T, n), BF16), vm((n, L), BF16), vm((L, n2), BF16), vm(((ns - 1) * T, width), BF16),
        vm(((ns - 1) * T, width), BF16), vm((T, width), F32), vm((2, nz * R, L), BF16),
        vm((nz * R, n), BF16), vm((nz * R, n), BF16), vm((nz * piece, width), BF16),
        vm((nz, R, n), BF16), vm((R, n), BF16), vm((nz, R, n), BF16), vm((R, n), BF16),
        vm((nz, piece, width), BF16), vm((piece, width), BF16), vm((L, qw), BF16),
        vm((hk, L, qw // hk), BF16), vm((hk, L, HD), F32), vm((hk, L, HD), F32), vm((qw, L), F32),
        vm((nz * R, pw), BF16), vm((nz * R, pw), BF16), vm((nz, R, pw), BF16), vm((R, pw), BF16),
        vm((nz * R, width), BF16), vm(((ns - 1) * nz * R, cw), BF16), vm(((ns - 1) * nz * R, cw), BF16), vm((nz * R, cw), BF16),
        vm((nz, R, cw), BF16), vm((R, cw), BF16),
        vm((8, width), F32), vm((ns - 1, 8, width), F32), vm((nd, 8, 128), F32), vm((nd - 1, 8, 128), F32),
    ]
    sems = seq_sems(ns) + [DMA((nd,)), DMA((nd,))] + seq_sems(ns) + [DMA((ns,))] * 2 + seq_sems(ns) * 2
    sems += [DMA((3,)), DMA((3,))]
    sems += [DMA((3,)), DMA((2, 8))]
    sems += seq_sems(ns) + [DMA((ns,))] * 2 + seq_sems(ns) + [DMA((2,)), DMA((2,))] + seq_sems(ns) + [DMA((ns,))] * 2 + [DMA((nd,)), DMA((nd,))]
    sems += seq_sems(ns) + [DMA((nz,))] + seq_sems(ns)
    return pl.pallas_call(
        functools.partial(block_kernel, ns, nd),
        out_shape=outs,
        in_specs=vmem(5) + [hbm] * 5 + vmem(2),
        out_specs=[hbm] * 7 + vmem(1),
        scratch_shapes=scratch + sems + gather_sems(nz) * 4 + scatter_sems(ns, nz) * 5 + gather_sems(nz),
        compiler_params=pltpu.CompilerParams(
            collective_id=0, has_side_effects=True, vmem_limit_bytes=VMEM_LIMIT
        ),
        cost_estimate=pl.CostEstimate(flops=38_000_000_000, bytes_accessed=40_000_000, transcendentals=12_000_000),
    )(x, gain1, gain2, gainqk, w_qkv, w_out, cot, w_gate, w_up, w_down, cos, sin)


def finish_kernel(
    ns, nd, piece, gateall, upall, qkvall, outall, dnall, got, stream, sums,
    gate, up, qkv, out, down, outputs, gstream, first, second, qk,
):
    outputs[...] = got[...]
    gstream[...] = stream[...]
    for i, ref in enumerate((first, second, qk)):
        ref[...] = sums[i : i + 1, : ref.shape[1]]
    hq, hk = H // ns, KV // ns
    qw, kw = hq * HD, hk * HD
    pad = gateall.shape[2] // nd
    for ref, got in ((gate, gateall), (up, upall)):
        parts = [got[i].astype(F32) for i in range(ns)]
        ref[...] = jnp.concatenate(
            [parts[i][:, k * pad : k * pad + piece] for k in range(nd) for i in range(ns)], axis=1
        )
    parts = [qkvall[i].astype(F32) for i in range(ns)]
    qkv[...] = jnp.concatenate(
        [p[:, :qw] for p in parts] + [p[:, qw : qw + kw] for p in parts] + [p[:, qw + kw :] for p in parts], axis=1
    )
    out[...] = jnp.concatenate([outall[i].astype(F32) for i in range(ns)], axis=1)
    down[...] = jnp.concatenate([dnall[i].astype(F32)[:piece] for i in range(dnall.shape[0])], axis=0)


def finish(ns, nd, piece, gateall, upall, qkvall, outall, dnall, got, stream, sums):
    R = gateall.shape[1]
    T, width = got.shape
    steps = 4
    rows = R // steps
    ff = ns * nd * piece
    widths = (ff, ff, ns * qkvall.shape[2], ns * outall.shape[2])
    many = ns // steps
    lines = (R, R, 2 * HD // nd)
    ins = [pl.BlockSpec((ns, rows, a.shape[2]), lambda i: (0, i, 0)) for a in (gateall, upall, qkvall, outall)]
    ins.append(pl.BlockSpec((many,) + dnall.shape[1:], lambda i: (i, 0, 0)))
    tokens = pl.BlockSpec((T // steps, width), lambda i: (i, 0))
    ins += [tokens, tokens, pl.BlockSpec((8, 128), lambda i: (0, 0))]
    outs = [pl.BlockSpec((rows, w), lambda i: (i, 0)) for w in widths]
    outs += [pl.BlockSpec((many * piece, width), lambda i: (i, 0)), tokens, tokens]
    outs += [pl.BlockSpec((1, w), lambda i: (0, 0)) for w in lines]
    sh = jax.ShapeDtypeStruct
    return pl.pallas_call(
        functools.partial(finish_kernel, ns, nd, piece),
        grid=(steps,),
        out_shape=[sh((R, w), F32) for w in widths]
        + [sh((ns * piece, width), F32), sh((T, width), BF16), sh((T, width), F32)]
        + [sh((1, w), F32) for w in lines],
        in_specs=ins,
        out_specs=outs,
        compiler_params=pltpu.CompilerParams(vmem_limit_bytes=VMEM_LIMIT),
    )(gateall, upall, qkvall, outall, dnall, got, stream, sums)


def shards(inputs, cotangent, first_gain, w_qkv, qk_gain, w_out, second_gain, w_gate, w_up, w_down):
    ns, nd = lax.axis_size("seq"), lax.axis_size("dp")
    s, d = lax.axis_index("seq"), lax.axis_index("dp")
    piece = w_down.shape[0] // ns
    pad = -piece % 16
    down_rows = w_down
    if pad:
        down_rows = jnp.pad(lax.dynamic_slice_in_dim(w_down, s * piece, piece, 0), ((0, pad), (0, 0)))
    x = inputs[0]
    outputs, gstream, gateall, upall, dnall, qkvall, outall, small = block(
        ns, nd, piece + pad, x, first_gain[None], second_gain[None], qk_gain[None], w_qkv, w_out, cotangent[0],
        w_gate, w_up, down_rows,
    )
    gate, up, qkv, out, down, outputs, gstream, first, second, qk = finish(
        ns, nd, piece, gateall, upall, qkvall, outall, dnall, outputs, gstream, small
    )
    return (outputs[None], gstream[None], first[0], qkv, qk[0], out, second[0], gate, up, down)


def solution(mesh):
    act = P("dp", "seq", None)
    vec, mat = P("dp"), P("dp", None)
    in_specs = (act, act, vec, mat, vec, mat, vec, mat, mat, mat)
    out_specs = (act, act, vec, mat, vec, mat, vec, mat, mat, mat)
    return jax.shard_map(shards, mesh=mesh, in_specs=in_specs, out_specs=out_specs, check_vma=False)
```

```python
import functools

import jax
import jax.numpy as jnp
import numpy as np
from jax import lax
from jax.experimental import pallas as pl
from jax.experimental.pallas import tpu as pltpu
from jax.sharding import PartitionSpec as P

H = 16
KV = 8
HD = 64
EPSILON = 1e-06
THETA_BASE = 1000000.0
F32 = jnp.float32
BF16 = jnp.bfloat16
VMEM_LIMIT = 65000 << 10


def rope_columns(length):
    inverse = np.float32(THETA_BASE) ** (-np.arange(0, HD, 2).astype(np.float32) / np.float32(HD))
    angles = (np.arange(length, dtype=np.float32)[None, :] * inverse.astype(np.float32)[:, None]).astype(np.float32)
    angles = angles.astype(np.float64)
    return jnp.asarray(np.cos(angles), F32), jnp.asarray(np.sin(angles), F32)


MESH = pl.DeviceIdType.MESH
DMA = pltpu.SemaphoreType.DMA


def mm(a, b):
    return jnp.dot(a, b, preferred_element_type=F32)


def mm_nt(a, b):
    return lax.dot_general(a, b, (((1,), (1,)), ((), ())), preferred_element_type=F32)


def remote(src, dst, send, recv, device):
    return pltpu.make_async_remote_copy(
        src_ref=src, dst_ref=dst, send_sem=send, recv_sem=recv, device_id=device, device_id_type=MESH
    )


def block_of(index, size):
    return pl.ds(pl.multiple_of(index * size, size), size)


class Place:
    def __init__(self, ns, nd):
        self.ns, self.nd, self.nz = ns, nd, nd // 2
        self.d, self.s = lax.axis_index("dp"), lax.axis_index("seq")
        self.zz, self.core = self.d // 2, lax.rem(self.d, 2)
        self.sib = (self.d + 1 - 2 * self.core, self.s)

    def seq_to(self, j):
        return (self.d, lax.rem(self.s + j, self.ns))

    def seq_from(self, j):
        return lax.rem(self.s + self.ns - j, self.ns)

    def across(self):
        return (self.s + 1 - 2 * lax.rem(self.s, 2), lax.rem(self.s + 2, 4), 3 - self.s)

    def gather_rank(self, j):
        if j == 0:
            return self.s
        return self.across()[j - 1] if self.ns == 4 else self.seq_from(j)

    def reduce_rank(self, j):
        if j == 0:
            return self.s
        x, y, o = self.across()
        return (o, x, y)[j - 1] if self.ns == 4 else lax.rem(self.s + j, self.ns)

    def dp_to(self, j):
        return (lax.rem(self.d + j, self.nd), self.s)

    def z_index(self, j):
        return lax.rem(self.zz + j, self.nz)

    def z_from(self, j):
        return lax.rem(self.zz + self.nz - j, self.nz)

    def z_device(self, z):
        return (2 * z + self.core, self.s)

    def greet(self):
        bar = pltpu.get_barrier_semaphore()
        for j in range(1, self.nd):
            pl.semaphore_signal(bar, inc=1, device_id=self.dp_to(j), device_id_type=MESH)
        for j in range(1, self.ns):
            pl.semaphore_signal(bar, inc=1, device_id=self.seq_to(j), device_id_type=MESH)
        pl.semaphore_wait(bar, self.nd + self.ns - 2)


class SeqGather:
    def __init__(self, at, src, dst, sems):
        self.at, self.src, self.dst = at, src, dst
        self.send, self.recv = sems
        self.half = src.shape[0] // 2

    def direct(self, j):
        at = self.at
        to = at.across()[j - 1] if at.ns == 4 else at.seq_to(j)[1]
        return remote(self.src, self.dst(at.s), self.send.at[j], self.recv.at[j], (at.d, to))

    def forward(self, i):
        at = self.at
        part = self.dst(at.across()[i]).at[pl.ds(i * self.half, self.half)]
        return remote(part, part, self.send.at[3 + i], self.recv.at[3 + i], (at.d, at.across()[1 - i]))

    def near(self):
        return range(1, 3 if self.at.ns == 4 else self.at.ns)

    def start(self):
        for j in self.near():
            self.direct(j).start()

    def hop(self):
        if self.at.ns == 4:
            for i in range(2):
                self.direct(i + 1).wait_recv()
                self.forward(i).start()

    def wait(self, j):
        if self.at.ns != 4:
            self.direct(j).wait_recv()
        elif j == 3:
            for i in range(2):
                self.forward(i).wait_recv()

    def finish(self):
        for j in range(1, self.at.ns):
            self.wait(j)

    def drain(self):
        for j in self.near():
            self.direct(j).wait_send()
        if self.at.ns == 4:
            for i in range(2):
                self.forward(i).wait_send()


def seq_sems(ns):
    return [DMA((max(ns, 6),)), DMA((max(ns, 6),))]


class SeqReduce:
    def __init__(self, at, rows, stage, inbox, sems):
        self.at, self.rows, self.stage, self.inbox = at, rows, stage, inbox
        self.send, self.recv = sems

    def part(self, ref, block, half=None):
        if half is None:
            return ref.at[pl.ds(block * self.rows, self.rows)]
        h = self.rows // 2
        return ref.at[pl.ds(block * self.rows + half * h, h)]

    def leg(self, k):
        at = self.at
        if at.ns != 4:
            src, dst, to = self.part(self.stage, k - 1), self.part(self.inbox, k - 1), at.seq_to(k)[1]
        else:
            b, h, i, n = ((0, 0, 2, 0), (0, 1, 2, 1), (1, 0, 0, 0), (2, 1, 1, 1), (2, 0, 1, 1), (1, 1, 0, 0))[k]
            src, dst, to = self.part(self.stage, b, h), self.part(self.inbox, i, h), at.across()[n]
        return remote(src, dst, self.send.at[k], self.recv.at[k], (at.d, to))

    def push(self, j):
        for k in (j,) if self.at.ns != 4 else ((), (0, 1), (2,), (3,))[j]:
            self.leg(k).start()

    def hop(self):
        if self.at.ns != 4:
            return
        h = self.rows // 2
        for k, b in ((0, 2), (1, 1)):
            self.leg(k).wait_recv()
            mine, came = pl.ds(b * self.rows + k * h, h), pl.ds(2 * self.rows + k * h, h)
            self.stage[mine, :] = (self.stage[mine, :].astype(F32) + self.inbox[came, :].astype(F32)).astype(BF16)
            self.leg(4 + k).start()

    def total(self, acc):
        four = self.at.ns == 4
        for k in range(2, 6) if four else range(1, self.at.ns):
            self.leg(k).wait_recv()
        for b in range(2 if four else self.at.ns - 1):
            acc = acc + self.inbox[b * self.rows : (b + 1) * self.rows, :].astype(F32)
        return acc

    def drain(self):
        for k in range(6) if self.at.ns == 4 else range(1, self.at.ns):
            self.leg(k).wait_send()


class Gather:
    def __init__(self, at, src, dst, sems):
        self.at, self.src, self.dst = at, src, dst
        self.send, self.recv, self.fsend, self.frecv, self.rsend, self.local = sems
        self.rows = src.shape[0]
        nz = at.nz
        self.order = [1, nz - 1] + list(range(2, nz - 1))

    def piece(self, z):
        return self.dst.at[block_of(2 * z + self.at.core, self.rows)]

    def direct(self, j):
        at = self.at
        return remote(self.src, self.piece(at.zz), self.send.at[j], self.recv.at[j], at.z_device(at.z_index(j)))

    def near(self, j):
        at = self.at
        z = at.z_index(j)
        away = z - at.zz
        return ((z > 0) & (z < at.nz - 1)) | (away == 1) | (away == -1)

    def across(self, j):
        piece = self.src if j == 0 else self.piece(self.at.z_from(j))
        return remote(piece, self.piece(self.at.z_from(j)), self.fsend.at[j], self.frecv.at[j], self.at.sib)

    def relay(self, j):
        nz = self.at.nz
        out = []
        for k, (here, end) in enumerate(((1, 0), (nz - 2, nz - 1))):
            origin = (here - j) % nz
            if origin != end:
                piece = self.piece(origin)
                index = (end - origin) % nz
                copy = remote(piece, piece, self.rsend.at[k, j], self.recv.at[index], self.at.z_device(end))
                out.append((self.at.zz == here, copy))
        return out

    def mine(self):
        return pltpu.make_async_copy(self.src, self.dst.at[block_of(self.at.d, self.rows)], self.local.at[0])

    def start(self):
        for j in self.order[2:] + self.order[:2]:
            pl.when(self.near(j))(self.direct(j).start)
        self.across(0).start()
        self.mine().start()

    def hop(self):
        at = self.at

        @pl.when((at.zz == 1) | (at.zz == at.nz - 2))
        def _():
            for j in self.order:
                self.direct(j).wait_recv()
                for here, copy in self.relay(j):
                    pl.when(here)(copy.start)
                self.across(j).start()

    def arrive(self):
        at = self.at

        @pl.when((at.zz != 1) & (at.zz != at.nz - 2))
        def _():
            for j in self.order:
                self.direct(j).wait_recv()
                self.across(j).start()

    def finish(self):
        for j in range(self.at.nz):
            self.across(j).wait_recv()
        self.mine().wait()

    def drain_own(self):
        self.across(0).wait_send()
        for j in range(1, self.at.nz):
            pl.when(self.near(j))(self.direct(j).wait_send)

    def drain_rest(self):
        for j in range(1, self.at.nz):
            self.across(j).wait_send()
            for here, copy in self.relay(j):
                pl.when(here)(copy.wait_send)

    def drain(self):
        self.drain_own()
        self.drain_rest()


def gather_sems(nz):
    return [DMA((nz,)), DMA((nz,)), DMA((nz,)), DMA((nz,)), DMA((2, nz)), DMA((1,))]


class Scatter:
    def __init__(self, at, pieces, inbox, final, out, sems):
        self.at, self.pieces, self.inbox, self.final, self.out = at, pieces, inbox, final, out
        self.send, self.recv, osend, orecv, self.local, self.rsend, self.rrecv = sems
        self.rows = final.shape[0]
        self.share = SeqGather(at, final, lambda r: out.at[r], (osend, orecv))

    def piece(self, z):
        return self.pieces.at[block_of(z, self.rows)]

    def copy(self, j):
        at = self.at
        z = at.z_index(j)
        return remote(self.piece(z), self.inbox.at[j - 1], self.send.at[j], self.recv.at[j], at.z_device(z))

    def far_copy(self, target, via):
        slot = self.inbox.at[self.at.nz - 1]
        return remote(self.piece(target), slot, self.rsend.at[0], self.rrecv.at[0], self.at.z_device(via))

    def far(self):
        nz = self.at.nz
        return ((0, nz - 1, 1, nz - 2), (nz - 1, 0, nz - 2, 2))

    def near(self, away):
        return (away < self.at.nz - 1) & (away > 1 - self.at.nz)

    def free(self, j):
        go = self.near(self.at.z_index(j) - self.at.zz)
        for _, _, via, k in self.far():
            if k == j:
                go = go & (self.at.zz != via)
        return go

    def start(self):
        at = self.at
        for origin, target, via, _ in self.far():
            pl.when(at.zz == origin)(self.far_copy(target, via).start)
        for j in range(1, at.nz):
            pl.when(self.free(j))(self.copy(j).start)
            away = at.z_from(j) - at.zz

            @pl.when((away >= at.nz - 1) | (away <= 1 - at.nz))
            def _():
                self.inbox[j - 1] = jnp.zeros_like(self.inbox[j - 1])

    def relay(self):
        at = self.at
        for _, target, via, j in self.far():

            @pl.when(at.zz == via)
            def _():
                self.far_copy(target, via).wait_recv()
                rows = block_of(target, self.rows)
                both = self.pieces[rows, :].astype(F32) + self.inbox[at.nz - 1].astype(F32)
                self.pieces[rows, :] = both.astype(BF16)
                self.copy(j).start()

    def keep(self):
        return pltpu.make_async_copy(self.final, self.out.at[self.at.s], self.local.at[0])

    def total(self):
        at = self.at
        for j in range(1, at.nz):
            pl.when(self.near(at.z_from(j) - at.zz))(self.copy(j).wait_recv)
        acc = self.pieces[block_of(self.at.zz, self.rows), :].astype(F32)
        for j in range(1, self.at.nz):
            acc = acc + self.inbox[j - 1].astype(F32)
        self.final[...] = acc.astype(BF16)
        self.keep().start()
        self.share.start()

    def drain(self):
        self.keep().wait()
        self.share.finish()
        self.share.drain()
        at = self.at
        for j in range(1, at.nz):
            pl.when(self.near(at.z_index(j) - at.zz))(self.copy(j).wait_send)
        for origin, target, via, _ in self.far():
            pl.when(at.zz == origin)(self.far_copy(target, via).wait_send)


def scatter_sems(ns, nz):
    return [DMA((nz,)), DMA((nz,))] + seq_sems(ns) + [DMA((1,)), DMA((1,)), DMA((1,))]


def block_kernel(
    ns, nd, x, gain1, gain2, gainqk, wqkv_rows, wout_mine, cot, wgate, wup, wdown, cos, sin,
    outputs, gstream, gateall, upall, dnall, qkvall, outall, small,
    normed, projT, qT, kT, krows, vrows, inv, mixT, mrowsT, wout, wqkv, gsum, osend, oown, gsecond,
    vT, resid, cotall, xall, gains, gbuf, wqkv_mine, gu, dn, hrow, hT, gb, gsend, grecv, gown, nmT,
    gur, uur, dnr,
    gaz, gaf, upz, upf, dnz, dnf, grows, qrows, gk, gv, gqT, qkr, qkown, qkz, qkf,
    gor, gostage, gorecv, goown, goz, gof, sm0, sm1, sm2, sm3,
    xs, xr, gs, gr, cs, cr, ms, mr, ns_, nr, ps, pr, ss, sr, loc, wl,
    os_, or_, bs, br, nis, nir, ss2, sr2, gos, gorc, s1, r1, s2, r2, wos, wor, wok, cs2, cr2, *sems,
):
    at = Place(ns, nd)
    s, d, nz, core = at.s, at.d, at.nz, at.core
    T, width = x.shape
    L = ns * T
    R = wqkv_mine.shape[0]
    cw = width // ns
    n = dn.shape[0]
    piece = n // nd
    gl, ql = gain1.shape[1], gainqk.shape[1]
    dn_mine = wdown.at[block_of(s, piece)] if wdown.shape[0] == ns * piece else wdown
    hq, hk = H // ns, KV // ns
    group = hq // hk
    qw, kw = hq * HD, hk * HD
    own = block_of(s, T)
    pw = qw + 2 * kw
    gains[...] = jnp.zeros_like(gains)
    gains[0:1, :gl] = gain1[...]
    gains[1:2, :gl] = gain2[...]
    gains[2:3, :ql] = gainqk[...]
    for i in range(ns):

        @pl.when(s == i)
        def _():
            cuts = ((i * qw, qw), (H * HD + i * kw, kw), ((H + KV) * HD + i * kw, kw))
            wqkv_mine[...] = jnp.concatenate([wqkv_rows[:, a : a + b] for a, b in cuts], axis=1)

    at.greet()

    share_x = SeqGather(at, x, lambda r: xall.at[block_of(r, T)], (xs, xr))
    g_copies = [remote(gains, gbuf.at[d], gs.at[j], gr.at[j], at.dp_to(j)) for j in range(1, nd)]
    hw = width // 2

    def share_half(i, sem):
        c = pl.ds(i * hw, hw)
        return SeqGather(at, cot.at[:, c], lambda r: cotall.at[block_of(r, T), c], sem)

    share_cot = [share_half(0, (cs, cr)), share_half(1, (cs2, cr2))]
    share_nm = SeqGather(at, xall.at[own], lambda r: xall.at[block_of(r, T)], (ns_, nr))
    take_qkv = Gather(at, wqkv_mine, wqkv, sems[0:6])
    wo, mycols = nmT.at[0], block_of(s, cw)

    def out_z(j):
        rows = wo.at[block_of(at.zz, R), mycols]
        return remote(wout_mine.at[:, mycols], rows, sems[6].at[j], sems[7].at[j], at.z_device(at.z_index(j)))

    out_local = pltpu.make_async_copy(wout_mine.at[:, mycols], wo.at[block_of(at.zz, R), mycols], sems[11].at[0])
    share_out = SeqGather(at, wo.at[:, mycols], lambda r: wo.at[:, block_of(r, cw)], (wos, wor))

    def out_across(z):
        rows = wout.at[block_of(2 * z + core, R)]
        return remote(wo.at[pl.ds(z * R, R)], rows, sems[8].at[z], sems[9].at[z], at.sib)

    def out_keep(z):
        return pltpu.make_async_copy(wo.at[pl.ds(z * R, R)], wout.at[block_of(2 * z + core, R)], wok.at[z])

    base = L // 2
    take_gate = Gather(at, gb.at[pl.ds(base, R), pl.ds(0, n)], gu.at[:, pl.ds(0, n)], sems[12:18])
    take_up = Gather(at, gb.at[pl.ds(base, R), pl.ds(n, n)], gu.at[:, pl.ds(n, n)], sems[59:65])
    take_dn = Gather(at, dn_mine, dn, sems[18:24])
    for c in g_copies:
        c.start()
    share_x.start()
    take_qkv.start()
    for j in range(1, nz):
        out_z(j).start()
    out_local.start()
    xall[own, :] = x[...]
    gbuf[d] = gains[...]
    cot_local = pltpu.make_async_copy(cot, cotall.at[own], loc.at[0])
    cot_local.start()
    ff = wgate.shape[1]
    parts = max(1, -(-ff // (2 * n)))
    while nd % parts:
        parts += 1
    span = ff // parts
    stage = []
    for i, w in enumerate((wgate, wup)):
        for k in range(parts):
            row = pl.ds((i * parts + k) * R, R)
            stage.append(
                pltpu.make_async_copy(w.at[:, pl.ds(k * span, span)], gb.at[row, pl.ds(0, span)], wl.at[i, k])
            )
    for c in stage:
        c.start()
    for c in stage:
        c.wait()
    real = wgate.shape[1] // nd // ns
    gap = [jnp.zeros((R, piece - real), BF16)] if piece > real else []
    for i in range(ns):

        @pl.when(s == i)
        def _():
            cuts = []
            for w in range(2):
                for k in range(nd):
                    a = (k * ns + i) * real
                    row = (w * parts + a // span) * R
                    cuts += [gb[row : row + R, a % span : a % span + real]] + gap
            gb[base : base + R, :] = jnp.concatenate(cuts, axis=1)


    for c in g_copies:
        c.wait_recv()
    gain_in = jnp.concatenate([gbuf[k][0:1, :gl] for k in range(nd)], axis=1)
    gain_mid = jnp.concatenate([gbuf[k][1:2, :gl] for k in range(nd)], axis=1)
    gain_qk = jnp.concatenate([gbuf[k][2:3, :ql] for k in range(nd)], axis=1)
    gsum[...] = jnp.zeros_like(gsum)
    gsum[0:1, :] = gain_in
    gsum[1:2, :] = gain_mid
    gsum[2:3, : 2 * HD] = gain_qk
    columns = jnp.transpose(jnp.broadcast_to(gain_qk, (8, 2 * HD)))
    gain_q, gain_k = columns[:HD, 0:1], columns[HD:, 0:1]
    take_qkv.hop()
    take_gate.start()
    take_up.start()
    take_dn.start()
    for j in range(ns):
        rows = block_of(at.gather_rank(j), T)
        if j == 1:
            share_x.hop()
        if j:
            share_x.wait(j)
        xc = xall[rows, :].astype(F32)
        scale = lax.rsqrt(jnp.mean(xc * xc, axis=-1, keepdims=True) + EPSILON)
        normed[rows, :] = (xc * scale * gain_in).astype(BF16)
    for j in range(1, nz):
        out_z(j).wait_recv()
    out_local.wait()
    share_out.start()
    take_qkv.arrive()
    take_qkv.finish()
    for j in range(ns):
        rows = pl.ds(j * T, T)
        proj = mm(normed[rows, :], wqkv[...])
        projT[:, rows] = jnp.transpose(proj[:, : qw + kw])
        val = proj[:, qw + kw :]
        vT[:, rows] = jnp.transpose(val).astype(BF16)
        for i in range(hk):
            vrows[i, rows, :] = val[:, i * HD : (i + 1) * HD].astype(BF16)

    half = HD // 2

    def rope(row, gain, factor):
        u = projT[row, :]
        scale = lax.rsqrt(jnp.mean(u * u, axis=0, keepdims=True) + EPSILON)
        u = u * scale * gain
        a, b = u[:half], u[half:]
        return jnp.concatenate([a * cos[...] - b * sin[...], b * cos[...] + a * sin[...]], axis=0) * factor

    def rope_query(h, carry):
        row = block_of(h, HD)
        qT[row, :] = rope(row, gain_q, HD**-0.5).astype(BF16)
        return carry

    lax.fori_loop(0, hq, rope_query, 0)
    for i in range(hk):
        r = rope(pl.ds(qw + i * HD, HD), gain_k, 1.0)
        kT[i * HD : (i + 1) * HD, :] = r.astype(BF16)
        krows[i, :, :] = jnp.transpose(r).astype(BF16)

    share_x.drain()
    share_out.hop()
    take_gate.hop()
    keep = lax.broadcasted_iota(jnp.int32, (T, T), 0) <= lax.broadcasted_iota(jnp.int32, (T, T), 1)
    block = block_of(s, qw)

    def mixed_out(rb):
        return remote(mixT.at[rb], mrowsT.at[block], ms.at[rb], mr.at[s], (d, rb))

    for rb in range(ns):
        cols = pl.ds(rb * T, T)
        span = rb * T

        def head(h, carry):
            kv = h // group
            row, vrow = block_of(h, HD), block_of(kv, HD)
            q = qT[row, cols]
            p = jnp.where(keep, jnp.exp(mm(krows[kv, cols, :], q)), 0.0)
            tot = jnp.sum(p, axis=0, keepdims=True)
            m = mm(vT[vrow, cols], p.astype(BF16))
            if span:
                p = jnp.exp(mm(krows[kv, 0:span, :], q))
                tot = tot + jnp.sum(p, axis=0, keepdims=True)
                m = m + mm(vT[vrow, 0:span], p.astype(BF16))
            one = 1.0 / tot
            inv[h, :, cols] = one
            mixT[rb, row, :] = (m * one).astype(BF16)
            return carry

        lax.fori_loop(0, hq, head, 0)
        pl.when(s != rb)(mixed_out(rb).start)
        if rb == ns - 1:
            share_out.finish()
            for z in range(nz):
                out_across(z).start()
                out_keep(z).start()

    share_cot[0].start()
    mrowsT[block, :] = mixT[s]
    for j in range(1, ns):
        src = at.seq_from(j)
        remote(mixT.at[0], mrowsT.at[block_of(src, qw)], ms.at[0], mr.at[src], (d, src)).wait_recv()
    for z in range(nz):
        out_across(z).wait_recv()
        out_keep(z).wait()
    residual = x[...].astype(F32) + mm(jnp.transpose(mrowsT[...]), wout[...])
    resid[...] = residual
    scale_mid = lax.rsqrt(jnp.mean(residual * residual, axis=-1, keepdims=True) + EPSILON)
    xall[own, :] = (residual * scale_mid * gain_mid).astype(BF16)
    share_nm.start()
    take_up.hop()
    share_nm.hop()
    share_cot[0].hop()
    share_cot[1].start()
    take_dn.hop()
    take_gate.arrive()
    take_up.arrive()
    ft, nt, wt = n, 1, width

    take_gate.drain_own()
    take_up.drain_own()
    take_gate.finish()
    take_up.finish()
    for j in range(ns):
        if j == ns - 1:
            share_cot[1].hop()
        if j:
            share_nm.wait(j)
        rows = block_of(at.gather_rank(j), T)
        for i in range(2):
            f = pl.ds(i * n, n)
            gb[rows, f] = mm(xall[rows, :], gu[:, f]).astype(BF16)
    share_nm.drain()
    share_out.drain()
    for z in range(nz):
        out_across(z).wait_send()
    for k in range(nd):
        nmT[k % 2, (k // 2) * R : (k // 2 + 1) * R, :] = jnp.transpose(xall[:, k * R : (k + 1) * R])
    take_dn.arrive()
    take_dn.finish()
    share_cot[0].finish()
    share_cot[1].finish()
    cot_local.wait()
    sum_nm = SeqReduce(at, T, gsend, grecv, (ps, pr))
    for j in list(range(1, ns)) + [0]:
        if j == 0:
            sum_nm.hop()
        rows = block_of(at.reduce_rank(j), T)
        stage = pl.ds((j - 1) * T, T)

        def hidden_tile(i, carry):
            f, f2 = block_of(i, ft), block_of(i + nt, ft)
            gate, up = gb[rows, f].astype(F32), gb[rows, f2].astype(F32)
            sig = 1.0 / (1.0 + jnp.exp(-gate))
            act = gate * sig
            back = mm_nt(cotall[rows, :], dn[f, :])
            hid = act * up
            hrow[:, f] = hid.astype(BF16)
            hid = jnp.transpose(hid.astype(BF16))
            for k in range(nd):
                first = (k % 2) * nz * piece + (k // 2) * piece
                hT[first : first + piece, rows] = hid[k * piece : (k + 1) * piece]
            gb[rows, f] = (back * up * sig * (1.0 + gate * (1.0 - sig))).astype(BF16)
            gb[rows, f2] = (back * act).astype(BF16)
            return carry

        lax.fori_loop(0, nt, hidden_tile, 0)

        def back_tile(i, carry):
            w = block_of(i, wt)
            part = mm_nt(gb[rows, :], gu[w, :])
            if j:
                gsend[stage, w] = part.astype(BF16)
            else:
                gown[:, w] = part
            return carry

        lax.fori_loop(0, width // wt, back_tile, 0)
        if j:
            sum_nm.push(j)

        def out_tile(i, carry):
            w = block_of(i, wt)
            part = mm(hrow[...], dn[:, w])
            if j:
                osend[stage, w] = part.astype(BF16)
            else:
                oown[:, w] = part + resid[:, w]
            return carry

        lax.fori_loop(0, width // wt, out_tile, 0)

    share_cot[0].drain()
    share_cot[1].drain()
    take_gate.drain_rest()
    take_up.drain_rest()
    take_dn.drain()
    half_gu, half_dn = nz * R, nz * piece
    dns, dnown = dn.at[pl.ds(0, half_dn)], dn.at[pl.ds(half_dn, half_dn)]
    gus, gateown = (gu.at[pl.ds(i * half_gu, half_gu), pl.ds(0, n)] for i in range(2))
    uus, upown = (gu.at[pl.ds(i * half_gu, half_gu), pl.ds(n, n)] for i in range(2))
    dn_sum = Scatter(at, dnown, dnz, dnf, dnall, sems[24:31])
    gate_sum = Scatter(at, gateown, gaz, gaf, gateall, sems[31:38])
    up_sum = Scatter(at, upown, upz, upf, upall, sems[38:45])
    qkv_sum = Scatter(at, qkown, qkz, qkf, qkvall, sems[45:52])
    out_sum = Scatter(at, goown, goz, gof, outall, sems[52:59])

    def dn_part(c, i):
        return mm(hT[block_of(c, nz * piece), :], cotall[:, block_of(i, 512)])

    tiles = n // 384
    tw = n // tiles

    def other(buf, base):
        def tile(i, carry):
            f = block_of(i, tw)
            buf[:, f] = mm(nmT[1 - core], gb[:, pl.ds(pl.multiple_of(base + i * tw, 128), tw)]).astype(BF16)
            return carry

        lax.fori_loop(0, tiles, tile, 0)

    def summed(buf, got, base):
        def tile(i, carry):
            f = block_of(i, tw)
            part = mm(nmT[core], gb[:, pl.ds(pl.multiple_of(base + i * tw, 128), tw)])
            buf[:, f] = (part + got[:, f].astype(F32)).astype(BF16)
            return carry

        lax.fori_loop(0, tiles, tile, 0)

    dn_copy = remote(dns, dnr, ss.at[0], sr.at[0], at.sib)
    gate_copy = remote(gus, gur, ss.at[1], sr.at[1], at.sib)
    up_copy = remote(uus, uur, ss.at[2], sr.at[2], at.sib)

    def dn_other(i, carry):
        dns[:, block_of(i, 512)] = dn_part(1 - core, i).astype(BF16)
        return carry

    def dn_mine(i, carry):
        dnown[:, block_of(i, 512)] = dn_part(core, i).astype(BF16)
        return carry

    lax.fori_loop(0, width // 512, dn_other, 0)
    dn_copy.start()
    lax.fori_loop(0, width // 512, dn_mine, 0)
    dn_copy.wait_recv()
    dnown[...] = (dnown[...].astype(F32) + dnr[...].astype(F32)).astype(BF16)
    dn_sum.start()
    other(gus, 0)
    gate_copy.start()
    gnm = sum_nm.total(gown[...])
    sum_nm.drain()
    residual = resid[...]
    scale_mid = lax.rsqrt(jnp.mean(residual * residual, axis=-1, keepdims=True) + EPSILON)
    gsecond[...] = jnp.broadcast_to(jnp.sum(gnm * residual * scale_mid, axis=0, keepdims=True), (8, width))
    weighted = gnm * gain_mid
    gown[...] = (
        cotall[own, :].astype(F32)
        + scale_mid * weighted
        - residual * (scale_mid * scale_mid * scale_mid) * jnp.mean(weighted * residual, axis=-1, keepdims=True)
    )
    rback = gown[...].astype(BF16)

    def mixed_back(p):
        return remote(gsend.at[pl.ds(0, T), pl.ds(p * qw, qw)], grows.at[own], bs.at[p], br.at[s], (d, p))

    for p in range(ns):
        gsend[0:T, p * qw : (p + 1) * qw] = mm_nt(rback, wout[p * qw : (p + 1) * qw, :]).astype(BF16)
        pl.when(s != p)(mixed_back(p).start)
    grows[own, :] = gsend[0:T, block_of(s, qw)]

    sum_outputs = SeqReduce(at, T, osend, xall, (os_, or_))
    for j in range(1, ns):
        sum_outputs.push(j)
    other(uus, n)
    up_copy.start()
    gate_copy.wait_recv()
    summed(gateown, gur, 0)
    gate_sum.start()
    up_copy.wait_recv()
    summed(upown, uur, n)
    up_sum.start()
    for k in range(nd):
        nmT[k % 2, (k // 2) * R : (k // 2 + 1) * R, :] = mm(mrowsT[k * R : (k + 1) * R, :], rback).astype(BF16)
    go_copy = remote(nmT.at[1 - core], gor, ss2.at[0], sr2.at[0], at.sib)
    go_copy.start()
    for i in range(hk):
        qrows[i, :, :] = jnp.transpose(qT[i * group * HD : (i + 1) * group * HD, :])
    go_copy.wait_recv()
    gate_copy.wait_send()
    up_copy.wait_send()
    sum_gout = SeqReduce(at, nz * R, gostage, gorecv, (gos, gorc))

    def gout_columns(r):
        c = block_of(r, cw)
        return nmT[core, :, c].astype(F32) + gor[:, c].astype(F32)

    for j in range(1, ns):
        gostage[pl.ds((j - 1) * nz * R, nz * R), :] = gout_columns(at.reduce_rank(j)).astype(BF16)
    for j in range(1, ns):
        src = at.seq_from(j)
        remote(gsend.at[pl.ds(0, T), pl.ds(0, qw)], grows.at[block_of(src, T)], bs.at[0], br.at[src], (d, src)).wait_recv()
    for i in range(ns):
        rows = pl.ds(i * T, T)
        hT[pw : pw + qw, rows] = jnp.transpose(grows[rows, :])

    for j in range(1, ns):
        sum_gout.push(j)
    dn_sum.relay()

    causal = lax.broadcasted_iota(jnp.int32, (T, T), 0) <= lax.broadcasted_iota(jnp.int32, (T, T), 1)
    causal = jnp.concatenate([causal] * group, axis=1)
    gk[...] = jnp.zeros_like(gk)
    gv[...] = jnp.zeros_like(gv)

    def key_head(kv, carry):
        krow = block_of(kv, HD)
        lanes = block_of(kv, group * HD)
        for rb in range(ns):
            cols = pl.ds(rb * T, T)

            def side(ref, base):
                return jnp.concatenate(
                    [ref[pl.ds(pl.multiple_of(base + (kv * group + u) * HD, HD), HD), cols] for u in range(group)],
                    axis=1,
                )

            q, g = side(qT, 0), side(hT, pw)
            one = jnp.concatenate([inv[kv * group + u, :, cols] for u in range(group)], axis=1)
            m = jnp.concatenate(
                [mixT[rb, block_of(kv * group + u, HD), :] for u in range(group)], axis=1
            )
            delta = jnp.sum(g.astype(F32) * m.astype(F32), axis=0, keepdims=True)
            gr, qr = grows[cols, lanes], qrows[kv, cols, :]
            gr = jnp.concatenate([gr[:, u * HD : (u + 1) * HD] for u in range(group)], axis=0)
            qr = jnp.concatenate([qr[:, u * HD : (u + 1) * HD] for u in range(group)], axis=0)
            gq = jnp.zeros((HD, group * T), F32)
            for part, masked in ((pl.ds(0, rb * T), False), (cols, True)):
                if rb == 0 and not masked:
                    continue
                p = jnp.exp(mm(krows[kv, part, :], q)) * one
                if masked:
                    p = jnp.where(causal, p, 0.0)
                gp = mm(vrows[kv, part, :], g)
                ds = (p * (gp - delta)).astype(BF16)
                gv[kv, part, :] += mm(p.astype(BF16), gr)
                gk[kv, part, :] += mm(ds, qr)
                gq = gq + mm(kT[krow, part], ds)
            gq = gq * HD**-0.5
            for u in range(group):
                gqT[block_of(kv * group + u, HD), cols] = gq[:, u * T : (u + 1) * T]
        return carry

    lax.fori_loop(0, hk, key_head, 0)

    sum_outputs.hop()
    columns = jnp.transpose(gsum[:, : 2 * HD])
    gain_q, gain_k = columns[:HD, 2:3], columns[HD:, 2:3]

    def norm_column(row, g, gain):
        a, b = g[:half], g[half:]
        g = jnp.concatenate([a * cos[...] + b * sin[...], b * cos[...] - a * sin[...]], axis=0)
        u = projT[row, :]
        scale = lax.rsqrt(jnp.mean(u * u, axis=0, keepdims=True) + EPSILON)
        us = u * scale
        weighted = g * gain
        inner = jnp.mean(weighted * us, axis=0, keepdims=True)
        hT[row, :] = (scale * (weighted - us * inner)).astype(BF16)
        return jnp.sum(g * us, axis=1, keepdims=True)

    def query_back(h, acc):
        row = block_of(h, HD)
        return acc + norm_column(row, gqT[row, :], gain_q)

    gain_grad_q = lax.fori_loop(0, hq, query_back, jnp.zeros((HD, 1), F32))
    gain_grad_k = jnp.zeros((HD, 1), F32)
    for i in range(hk):
        gain_grad_k = gain_grad_k + norm_column(pl.ds(qw + i * HD, HD), jnp.transpose(gk[i]), gain_k)
        hT[qw + kw + i * HD : qw + kw + (i + 1) * HD, :] = jnp.transpose(gv[i]).astype(BF16)

    sum_gout.hop()
    gate_sum.relay()

    sum_ni = SeqReduce(at, T, gsend, grecv, (nis, nir))
    for p in range(ns):
        pl.when(s != p)(mixed_back(p).wait_send)
    for i in range(ns):
        rows = pl.ds(i * T, T)
        cotall[rows, 0:pw] = jnp.transpose(hT[0:pw, rows])
    for j in list(range(1, ns)) + [0]:
        part = mm_nt(cotall[block_of(at.reduce_rank(j), T), 0:pw], wqkv[...])
        if j:
            gsend[pl.ds((j - 1) * T, T), :] = part.astype(BF16)
            sum_ni.push(j)
        else:
            resid[...] = part
    for k in range(nd):
        part = mm(hT[0:pw, :], normed[:, k * R : (k + 1) * R])
        gb[((k % 2) * nz + k // 2) * R : ((k % 2) * nz + k // 2 + 1) * R, 0:pw] = jnp.transpose(part).astype(BF16)
    qk_copy = remote(gb.at[block_of(1 - core, nz * R), pl.ds(0, pw)], qkr, ss2.at[1], sr2.at[1], at.sib)
    qk_copy.start()
    sum_ni.hop()
    dn_sum.total()
    goown[...] = sum_gout.total(gout_columns(s)).astype(BF16)
    out_sum.start()
    qk_copy.wait_recv()
    qkown[...] = (gb[block_of(core, nz * R), pl.ds(0, pw)].astype(F32) + qkr[...].astype(F32)).astype(BF16)
    qkv_sum.start()
    up_sum.relay()
    out_sum.relay()
    gate_sum.total()
    qkv_sum.relay()

    gni = sum_ni.total(resid[...])
    dn_sum.share.hop()
    stream = x[...].astype(F32)
    scale = lax.rsqrt(jnp.mean(stream * stream, axis=-1, keepdims=True) + EPSILON)
    unit = stream * scale
    weighted = gni * gsum[0:1, :]
    gown[...] = gown[...] + scale * (weighted - unit * jnp.mean(weighted * unit, axis=-1, keepdims=True))
    stream_store = pltpu.make_async_copy(gown, gstream, loc.at[2])
    stream_store.start()
    first = jnp.sum(gni * unit, axis=0, keepdims=True)
    qk = jnp.broadcast_to(jnp.concatenate([gain_grad_q, gain_grad_k], axis=0), (2 * HD, 128))
    sm0[0:1, :] = first
    sm0[1:2, :] = gsecond[0:1, :]
    sm0[2:8, :] = jnp.zeros((6, width), F32)
    sm0[2:3, : 2 * HD] = jnp.transpose(qk)[0:1, :]

    def small_seq(j):
        return remote(sm0, sm1.at[j - 1], s1.at[j], r1.at[j], at.seq_to(j))

    def small_dp(j):
        return remote(sm2.at[at.dp_to(j)[0]], sm3.at[j - 1], s2.at[j], r2.at[j], at.dp_to(j))

    for j in range(1, ns):
        small_seq(j).start()
    gate_sum.share.hop()
    up_sum.total()
    acc = sum_outputs.total(oown[...])
    last = pl.ds((ns - 1) * T, T)
    xall[last, :] = acc.astype(BF16)
    out_store = pltpu.make_async_copy(xall.at[last], outputs, loc.at[1])
    out_store.start()
    for j in range(1, ns):
        small_seq(j).wait_recv()
    acc = sm0[...]
    for j in range(1, ns):
        acc = acc + sm1[j - 1]
    sm2[...] = jnp.zeros_like(sm2)
    for k in range(nd):
        sm2[k, 0:2, :gl] = acc[0:2, k * gl : (k + 1) * gl]
        sm2[k, 2:3, :ql] = acc[2:3, k * ql : (k + 1) * ql]
    for j in range(1, nd):
        small_dp(j).start()
    out_sum.total()
    qkv_sum.total()
    up_sum.share.hop()
    out_sum.share.hop()
    qkv_sum.share.hop()
    for j in range(1, nd):
        small_dp(j).wait_recv()
    acc = sm2[d]
    for j in range(1, nd):
        acc = acc + sm3[j - 1]
    small[...] = acc

    go_copy.wait_send()
    qk_copy.wait_send()
    for j in range(1, ns):
        small_seq(j).wait_send()
    for j in range(1, nd):
        small_dp(j).wait_send()
    for rb in range(ns):
        pl.when(s != rb)(mixed_out(rb).wait_send)
    for t in (sum_outputs, sum_ni, sum_gout):
        t.drain()
    for c in g_copies + [dn_copy]:
        c.wait_send()
    take_qkv.drain()
    for j in range(1, nz):
        out_z(j).wait_send()
    for t in (dn_sum, out_sum, qkv_sum, gate_sum, up_sum):
        t.drain()
    out_store.wait()
    stream_store.wait()


def vmem(n):
    return [pl.BlockSpec(memory_space=pltpu.VMEM)] * n


def block(ns, nd, piece, x, gain1, gain2, gainqk, w_qkv, w_out, cot, w_gate, w_up, w_down):
    T, width = x.shape
    L = ns * T
    R = w_qkv.shape[0]
    n = nd * piece
    n2 = 2 * n
    nz = nd // 2
    hq, hk = H // ns, KV // ns
    qw, kw = hq * HD, hk * HD
    pw = qw + 2 * kw
    cw = width // ns
    cos, sin = rope_columns(L)
    sh, vm = jax.ShapeDtypeStruct, pltpu.VMEM
    outs = (
        sh((T, width), BF16), sh((T, width), F32), sh((ns, R, n), BF16), sh((ns, R, n), BF16),
        sh((ns, piece, width), BF16), sh((ns, R, pw), BF16), sh((ns, R, cw), BF16), sh((8, 128), F32),
    )
    hbm = pl.BlockSpec(memory_space=pl.ANY)
    scratch = [
        vm((L, width), BF16), vm((qw + kw, L), F32), vm((qw, L), BF16), vm((kw, L), BF16),
        vm((hk, L, HD), BF16), vm((hk, L, HD), BF16), vm((hq, 1, L), F32), vm((ns, qw, T), BF16),
        vm((H * HD, T), BF16), vm((H * HD, width), BF16), vm((width, pw), BF16), vm((8, width), F32),
        vm(((ns - 1) * T, width), BF16), vm((T, width), F32), vm((8, width), F32),
        vm((kw, L), BF16), vm((T, width), F32), vm((L, width), BF16), vm((L, width), BF16), vm((8, 128), F32),
        vm((nd, 8, 128), F32), vm((R, pw), BF16), vm((nd * R, n2), BF16), vm((n, width), BF16),
        vm((T, n), BF16), vm((n, L), BF16), vm((L, n2), BF16), vm(((ns - 1) * T, width), BF16),
        vm(((ns - 1) * T, width), BF16), vm((T, width), F32), vm((2, nz * R, L), BF16),
        vm((nz * R, n), BF16), vm((nz * R, n), BF16), vm((nz * piece, width), BF16),
        vm((nz, R, n), BF16), vm((R, n), BF16), vm((nz, R, n), BF16), vm((R, n), BF16),
        vm((nz, piece, width), BF16), vm((piece, width), BF16), vm((L, qw), BF16),
        vm((hk, L, qw // hk), BF16), vm((hk, L, HD), F32), vm((hk, L, HD), F32), vm((qw, L), F32),
        vm((nz * R, pw), BF16), vm((nz * R, pw), BF16), vm((nz, R, pw), BF16), vm((R, pw), BF16),
        vm((nz * R, width), BF16), vm(((ns - 1) * nz * R, cw), BF16), vm(((ns - 1) * nz * R, cw), BF16), vm((nz * R, cw), BF16),
        vm((nz, R, cw), BF16), vm((R, cw), BF16),
        vm((8, width), F32), vm((ns - 1, 8, width), F32), vm((nd, 8, 128), F32), vm((nd - 1, 8, 128), F32),
    ]
    sems = seq_sems(ns) + [DMA((nd,)), DMA((nd,))] + seq_sems(ns) + [DMA((ns,))] * 2 + seq_sems(ns) * 2
    sems += [DMA((3,)), DMA((3,))]
    sems += [DMA((3,)), DMA((2, 8))]
    sems += seq_sems(ns) + [DMA((ns,))] * 2 + seq_sems(ns) + [DMA((2,)), DMA((2,))] + seq_sems(ns) + [DMA((ns,))] * 2 + [DMA((nd,)), DMA((nd,))]
    sems += seq_sems(ns) + [DMA((nz,))] + seq_sems(ns)
    return pl.pallas_call(
        functools.partial(block_kernel, ns, nd),
        out_shape=outs,
        in_specs=vmem(5) + [hbm] * 5 + vmem(2),
        out_specs=[hbm] * 7 + vmem(1),
        scratch_shapes=scratch + sems + gather_sems(nz) * 4 + scatter_sems(ns, nz) * 5 + gather_sems(nz),
        compiler_params=pltpu.CompilerParams(
            collective_id=0, has_side_effects=True, vmem_limit_bytes=VMEM_LIMIT
        ),
        cost_estimate=pl.CostEstimate(flops=38_000_000_000, bytes_accessed=40_000_000, transcendentals=12_000_000),
    )(x, gain1, gain2, gainqk, w_qkv, w_out, cot, w_gate, w_up, w_down, cos, sin)


def finish_kernel(
    ns, nd, piece, gateall, upall, qkvall, outall, dnall, got, stream, sums,
    gate, up, qkv, out, down, outputs, gstream, first, second, qk,
):
    outputs[...] = got[...]
    gstream[...] = stream[...]
    for i, ref in enumerate((first, second, qk)):
        ref[...] = sums[i : i + 1, : ref.shape[1]]
    hq, hk = H // ns, KV // ns
    qw, kw = hq * HD, hk * HD
    pad = gateall.shape[2] // nd
    for ref, got in ((gate, gateall), (up, upall)):
        parts = [got[i].astype(F32) for i in range(ns)]
        ref[...] = jnp.concatenate(
            [parts[i][:, k * pad : k * pad + piece] for k in range(nd) for i in range(ns)], axis=1
        )
    parts = [qkvall[i].astype(F32) for i in range(ns)]
    qkv[...] = jnp.concatenate(
        [p[:, :qw] for p in parts] + [p[:, qw : qw + kw] for p in parts] + [p[:, qw + kw :] for p in parts], axis=1
    )
    out[...] = jnp.concatenate([outall[i].astype(F32) for i in range(ns)], axis=1)
    down[...] = jnp.concatenate([dnall[i].astype(F32)[:piece] for i in range(dnall.shape[0])], axis=0)


def finish(ns, nd, piece, gateall, upall, qkvall, outall, dnall, got, stream, sums):
    R = gateall.shape[1]
    T, width = got.shape
    steps = 4
    rows = R // steps
    ff = ns * nd * piece
    widths = (ff, ff, ns * qkvall.shape[2], ns * outall.shape[2])
    many = ns // steps
    lines = (R, R, 2 * HD // nd)
    ins = [pl.BlockSpec((ns, rows, a.shape[2]), lambda i: (0, i, 0)) for a in (gateall, upall, qkvall, outall)]
    ins.append(pl.BlockSpec((many,) + dnall.shape[1:], lambda i: (i, 0, 0)))
    tokens = pl.BlockSpec((T // steps, width), lambda i: (i, 0))
    ins += [tokens, tokens, pl.BlockSpec((8, 128), lambda i: (0, 0))]
    outs = [pl.BlockSpec((rows, w), lambda i: (i, 0)) for w in widths]
    outs += [pl.BlockSpec((many * piece, width), lambda i: (i, 0)), tokens, tokens]
    outs += [pl.BlockSpec((1, w), lambda i: (0, 0)) for w in lines]
    sh = jax.ShapeDtypeStruct
    return pl.pallas_call(
        functools.partial(finish_kernel, ns, nd, piece),
        grid=(steps,),
        out_shape=[sh((R, w), F32) for w in widths]
        + [sh((ns * piece, width), F32), sh((T, width), BF16), sh((T, width), F32)]
        + [sh((1, w), F32) for w in lines],
        in_specs=ins,
        out_specs=outs,
        compiler_params=pltpu.CompilerParams(vmem_limit_bytes=VMEM_LIMIT),
    )(gateall, upall, qkvall, outall, dnall, got, stream, sums)


def shards(inputs, cotangent, first_gain, w_qkv, qk_gain, w_out, second_gain, w_gate, w_up, w_down):
    ns, nd = lax.axis_size("seq"), lax.axis_size("dp")
    s, d = lax.axis_index("seq"), lax.axis_index("dp")
    piece = w_down.shape[0] // ns
    pad = -piece % 16
    down_rows = w_down
    if pad:
        down_rows = jnp.pad(lax.dynamic_slice_in_dim(w_down, s * piece, piece, 0), ((0, pad), (0, 0)))
    x = inputs[0]
    outputs, gstream, gateall, upall, dnall, qkvall, outall, small = block(
        ns, nd, piece + pad, x, first_gain[None], second_gain[None], qk_gain[None], w_qkv, w_out, cotangent[0],
        w_gate, w_up, down_rows,
    )
    gate, up, qkv, out, down, outputs, gstream, first, second, qk = finish(
        ns, nd, piece, gateall, upall, qkvall, outall, dnall, outputs, gstream, small
    )
    return (outputs[None], gstream[None], first[0], qkv, qk[0], out, second[0], gate, up, down)


def solution(mesh):
    act = P("dp", "seq", None)
    vec, mat = P("dp"), P("dp", None)
    in_specs = (act, act, vec, mat, vec, mat, vec, mat, mat, mat)
    out_specs = (act, act, vec, mat, vec, mat, vec, mat, mat, mat)
    return jax.shard_map(shards, mesh=mesh, in_specs=in_specs, out_specs=out_specs, check_vma=False)
```

```python
import functools

import jax
import jax.numpy as jnp
import numpy as np
from jax import lax
from jax.experimental import pallas as pl
from jax.experimental.pallas import tpu as pltpu
from jax.sharding import PartitionSpec as P

H = 16
KV = 8
HD = 64
EPSILON = 1e-06
THETA_BASE = 1000000.0
F32 = jnp.float32
BF16 = jnp.bfloat16
VMEM_LIMIT = 65000 << 10


def rope_columns(length):
    inverse = np.float32(THETA_BASE) ** (-np.arange(0, HD, 2).astype(np.float32) / np.float32(HD))
    angles = (np.arange(length, dtype=np.float32)[None, :] * inverse.astype(np.float32)[:, None]).astype(np.float32)
    angles = angles.astype(np.float64)
    return jnp.asarray(np.cos(angles), F32), jnp.asarray(np.sin(angles), F32)


MESH = pl.DeviceIdType.MESH
DMA = pltpu.SemaphoreType.DMA


def mm(a, b):
    return jnp.dot(a, b, preferred_element_type=F32)


def mm_nt(a, b):
    return lax.dot_general(a, b, (((1,), (1,)), ((), ())), preferred_element_type=F32)


def remote(src, dst, send, recv, device):
    return pltpu.make_async_remote_copy(
        src_ref=src, dst_ref=dst, send_sem=send, recv_sem=recv, device_id=device, device_id_type=MESH
    )


def block_of(index, size):
    return pl.ds(pl.multiple_of(index * size, size), size)


class Place:
    def __init__(self, ns, nd):
        self.ns, self.nd, self.nz = ns, nd, nd // 2
        self.d, self.s = lax.axis_index("dp"), lax.axis_index("seq")
        self.zz, self.core = self.d // 2, lax.rem(self.d, 2)
        self.sib = (self.d + 1 - 2 * self.core, self.s)

    def seq_to(self, j):
        return (self.d, lax.rem(self.s + j, self.ns))

    def seq_from(self, j):
        return lax.rem(self.s + self.ns - j, self.ns)

    def across(self):
        return (self.s + 1 - 2 * lax.rem(self.s, 2), lax.rem(self.s + 2, 4), 3 - self.s)

    def gather_rank(self, j):
        if j == 0:
            return self.s
        return self.across()[j - 1] if self.ns == 4 else self.seq_from(j)

    def reduce_rank(self, j):
        if j == 0:
            return self.s
        x, y, o = self.across()
        return (o, x, y)[j - 1] if self.ns == 4 else lax.rem(self.s + j, self.ns)

    def dp_to(self, j):
        return (lax.rem(self.d + j, self.nd), self.s)

    def z_index(self, j):
        return lax.rem(self.zz + j, self.nz)

    def z_from(self, j):
        return lax.rem(self.zz + self.nz - j, self.nz)

    def z_device(self, z):
        return (2 * z + self.core, self.s)

    def greet(self):
        bar = pltpu.get_barrier_semaphore()
        for j in range(1, self.nd):
            pl.semaphore_signal(bar, inc=1, device_id=self.dp_to(j), device_id_type=MESH)
        for j in range(1, self.ns):
            pl.semaphore_signal(bar, inc=1, device_id=self.seq_to(j), device_id_type=MESH)
        pl.semaphore_wait(bar, self.nd + self.ns - 2)


class SeqGather:
    def __init__(self, at, src, dst, sems):
        self.at, self.src, self.dst = at, src, dst
        self.send, self.recv = sems
        self.half = src.shape[0] // 2

    def direct(self, j):
        at = self.at
        to = at.across()[j - 1] if at.ns == 4 else at.seq_to(j)[1]
        return remote(self.src, self.dst(at.s), self.send.at[j], self.recv.at[j], (at.d, to))

    def forward(self, i):
        at = self.at
        part = self.dst(at.across()[i]).at[pl.ds(i * self.half, self.half)]
        return remote(part, part, self.send.at[3 + i], self.recv.at[3 + i], (at.d, at.across()[1 - i]))

    def near(self):
        return range(1, 3 if self.at.ns == 4 else self.at.ns)

    def start(self):
        for j in self.near():
            self.direct(j).start()

    def hop(self):
        if self.at.ns == 4:
            for i in range(2):
                self.direct(i + 1).wait_recv()
                self.forward(i).start()

    def wait(self, j):
        if self.at.ns != 4:
            self.direct(j).wait_recv()
        elif j == 3:
            for i in range(2):
                self.forward(i).wait_recv()

    def finish(self):
        for j in range(1, self.at.ns):
            self.wait(j)

    def drain(self):
        for j in self.near():
            self.direct(j).wait_send()
        if self.at.ns == 4:
            for i in range(2):
                self.forward(i).wait_send()


def seq_sems(ns):
    return [DMA((max(ns, 6),)), DMA((max(ns, 6),))]


class SeqReduce:
    def __init__(self, at, rows, stage, inbox, sems):
        self.at, self.rows, self.stage, self.inbox = at, rows, stage, inbox
        self.send, self.recv = sems

    def part(self, ref, block, half=None):
        if half is None:
            return ref.at[pl.ds(block * self.rows, self.rows)]
        h = self.rows // 2
        return ref.at[pl.ds(block * self.rows + half * h, h)]

    def leg(self, k):
        at = self.at
        if at.ns != 4:
            src, dst, to = self.part(self.stage, k - 1), self.part(self.inbox, k - 1), at.seq_to(k)[1]
        else:
            b, h, i, n = ((0, 0, 2, 0), (0, 1, 2, 1), (1, 0, 0, 0), (2, 1, 1, 1), (2, 0, 1, 1), (1, 1, 0, 0))[k]
            src, dst, to = self.part(self.stage, b, h), self.part(self.inbox, i, h), at.across()[n]
        return remote(src, dst, self.send.at[k], self.recv.at[k], (at.d, to))

    def push(self, j):
        for k in (j,) if self.at.ns != 4 else ((), (0, 1), (2,), (3,))[j]:
            self.leg(k).start()

    def hop(self):
        if self.at.ns != 4:
            return
        h = self.rows // 2
        for k, b in ((0, 2), (1, 1)):
            self.leg(k).wait_recv()
            mine, came = pl.ds(b * self.rows + k * h, h), pl.ds(2 * self.rows + k * h, h)
            self.stage[mine, :] = (self.stage[mine, :].astype(F32) + self.inbox[came, :].astype(F32)).astype(BF16)
            self.leg(4 + k).start()

    def total(self, acc):
        four = self.at.ns == 4
        for k in range(2, 6) if four else range(1, self.at.ns):
            self.leg(k).wait_recv()
        for b in range(2 if four else self.at.ns - 1):
            acc = acc + self.inbox[b * self.rows : (b + 1) * self.rows, :].astype(F32)
        return acc

    def drain(self):
        for k in range(6) if self.at.ns == 4 else range(1, self.at.ns):
            self.leg(k).wait_send()


class Gather:
    def __init__(self, at, src, dst, sems):
        self.at, self.src, self.dst = at, src, dst
        self.send, self.recv, self.fsend, self.frecv, self.rsend, self.local = sems
        self.rows = src.shape[0]
        nz = at.nz
        self.order = [1, nz - 1] + list(range(2, nz - 1))

    def piece(self, z):
        return self.dst.at[block_of(2 * z + self.at.core, self.rows)]

    def direct(self, j):
        at = self.at
        return remote(self.src, self.piece(at.zz), self.send.at[j], self.recv.at[j], at.z_device(at.z_index(j)))

    def near(self, j):
        at = self.at
        z = at.z_index(j)
        away = z - at.zz
        return ((z > 0) & (z < at.nz - 1)) | (away == 1) | (away == -1)

    def across(self, j):
        piece = self.src if j == 0 else self.piece(self.at.z_from(j))
        return remote(piece, self.piece(self.at.z_from(j)), self.fsend.at[j], self.frecv.at[j], self.at.sib)

    def relay(self, j):
        nz = self.at.nz
        out = []
        for k, (here, end) in enumerate(((1, 0), (nz - 2, nz - 1))):
            origin = (here - j) % nz
            if origin != end:
                piece = self.piece(origin)
                index = (end - origin) % nz
                copy = remote(piece, piece, self.rsend.at[k, j], self.recv.at[index], self.at.z_device(end))
                out.append((self.at.zz == here, copy))
        return out

    def mine(self):
        return pltpu.make_async_copy(self.src, self.dst.at[block_of(self.at.d, self.rows)], self.local.at[0])

    def start(self):
        for j in self.order[2:] + self.order[:2]:
            pl.when(self.near(j))(self.direct(j).start)
        self.across(0).start()
        self.mine().start()

    def hop(self):
        at = self.at

        @pl.when((at.zz == 1) | (at.zz == at.nz - 2))
        def _():
            for j in self.order:
                self.direct(j).wait_recv()
                for here, copy in self.relay(j):
                    pl.when(here)(copy.start)
                self.across(j).start()

    def arrive(self):
        at = self.at

        @pl.when((at.zz != 1) & (at.zz != at.nz - 2))
        def _():
            for j in self.order:
                self.direct(j).wait_recv()
                self.across(j).start()

    def finish(self):
        for j in range(self.at.nz):
            self.across(j).wait_recv()
        self.mine().wait()

    def drain_own(self):
        self.across(0).wait_send()
        for j in range(1, self.at.nz):
            pl.when(self.near(j))(self.direct(j).wait_send)

    def drain_rest(self):
        for j in range(1, self.at.nz):
            self.across(j).wait_send()
            for here, copy in self.relay(j):
                pl.when(here)(copy.wait_send)

    def drain(self):
        self.drain_own()
        self.drain_rest()


def gather_sems(nz):
    return [DMA((nz,)), DMA((nz,)), DMA((nz,)), DMA((nz,)), DMA((2, nz)), DMA((1,))]


class Scatter:
    def __init__(self, at, pieces, inbox, final, out, sems):
        self.at, self.pieces, self.inbox, self.final, self.out = at, pieces, inbox, final, out
        self.send, self.recv, osend, orecv, self.local, self.rsend, self.rrecv = sems
        self.rows = final.shape[0]
        self.share = SeqGather(at, final, lambda r: out.at[r], (osend, orecv))

    def piece(self, z):
        return self.pieces.at[block_of(z, self.rows)]

    def copy(self, j):
        at = self.at
        z = at.z_index(j)
        return remote(self.piece(z), self.inbox.at[j - 1], self.send.at[j], self.recv.at[j], at.z_device(z))

    def far_copy(self, target, via):
        slot = self.inbox.at[self.at.nz - 1]
        return remote(self.piece(target), slot, self.rsend.at[0], self.rrecv.at[0], self.at.z_device(via))

    def far(self):
        nz = self.at.nz
        return ((0, nz - 1, 1, nz - 2), (nz - 1, 0, nz - 2, 2))

    def near(self, away):
        return (away < self.at.nz - 1) & (away > 1 - self.at.nz)

    def free(self, j):
        go = self.near(self.at.z_index(j) - self.at.zz)
        for _, _, via, k in self.far():
            if k == j:
                go = go & (self.at.zz != via)
        return go

    def start(self):
        at = self.at
        for origin, target, via, _ in self.far():
            pl.when(at.zz == origin)(self.far_copy(target, via).start)
        for j in range(1, at.nz):
            pl.when(self.free(j))(self.copy(j).start)
            away = at.z_from(j) - at.zz

            @pl.when((away >= at.nz - 1) | (away <= 1 - at.nz))
            def _():
                self.inbox[j - 1] = jnp.zeros_like(self.inbox[j - 1])

    def relay(self):
        at = self.at
        for _, target, via, j in self.far():

            @pl.when(at.zz == via)
            def _():
                self.far_copy(target, via).wait_recv()
                rows = block_of(target, self.rows)
                both = self.pieces[rows, :].astype(F32) + self.inbox[at.nz - 1].astype(F32)
                self.pieces[rows, :] = both.astype(BF16)
                self.copy(j).start()

    def keep(self):
        return pltpu.make_async_copy(self.final, self.out.at[self.at.s], self.local.at[0])

    def total(self):
        at = self.at
        for j in range(1, at.nz):
            pl.when(self.near(at.z_from(j) - at.zz))(self.copy(j).wait_recv)
        acc = self.pieces[block_of(self.at.zz, self.rows), :].astype(F32)
        for j in range(1, self.at.nz):
            acc = acc + self.inbox[j - 1].astype(F32)
        self.final[...] = acc.astype(BF16)
        self.keep().start()
        self.share.start()

    def drain(self):
        self.keep().wait()
        self.share.finish()
        self.share.drain()
        at = self.at
        for j in range(1, at.nz):
            pl.when(self.near(at.z_index(j) - at.zz))(self.copy(j).wait_send)
        for origin, target, via, _ in self.far():
            pl.when(at.zz == origin)(self.far_copy(target, via).wait_send)


def scatter_sems(ns, nz):
    return [DMA((nz,)), DMA((nz,))] + seq_sems(ns) + [DMA((1,)), DMA((1,)), DMA((1,))]


def block_kernel(
    ns, nd, x, gain1, gain2, gainqk, wqkv_rows, wout_mine, cot, wgate, wup, wdown, cos, sin,
    outputs, gstream, gateall, upall, dnall, qkvall, outall, small,
    normed, projT, qT, kT, krows, vrows, inv, mixT, mrowsT, wout, wqkv, gsum, osend, oown, gsecond,
    vT, resid, cotall, xall, gains, gbuf, wqkv_mine, gu, dn, hrow, hT, gb, gsend, grecv, gown, nmT,
    gur, uur, dnr,
    gaz, gaf, upz, upf, dnz, dnf, grows, qrows, gk, gv, gqT, qkr, qkown, qkz, qkf,
    gor, gostage, gorecv, goown, goz, gof, sm0, sm1, sm2, sm3,
    xs, xr, gs, gr, cs, cr, ms, mr, ns_, nr, ps, pr, ss, sr, loc, wl,
    os_, or_, bs, br, nis, nir, ss2, sr2, gos, gorc, s1, r1, s2, r2, wos, wor, wok, cs2, cr2, *sems,
):
    at = Place(ns, nd)
    s, d, nz, core = at.s, at.d, at.nz, at.core
    T, width = x.shape
    L = ns * T
    R = wqkv_mine.shape[0]
    cw = width // ns
    n = dn.shape[0]
    piece = n // nd
    gl, ql = gain1.shape[1], gainqk.shape[1]
    dn_mine = wdown.at[block_of(s, piece)] if wdown.shape[0] == ns * piece else wdown
    hq, hk = H // ns, KV // ns
    group = hq // hk
    qw, kw = hq * HD, hk * HD
    own = block_of(s, T)
    pw = qw + 2 * kw
    gains[...] = jnp.zeros_like(gains)
    gains[0:1, :gl] = gain1[...]
    gains[1:2, :gl] = gain2[...]
    gains[2:3, :ql] = gainqk[...]
    for i in range(ns):

        @pl.when(s == i)
        def _():
            cuts = ((i * qw, qw), (H * HD + i * kw, kw), ((H + KV) * HD + i * kw, kw))
            wqkv_mine[...] = jnp.concatenate([wqkv_rows[:, a : a + b] for a, b in cuts], axis=1)

    at.greet()

    share_x = SeqGather(at, x, lambda r: xall.at[block_of(r, T)], (xs, xr))
    g_copies = [remote(gains, gbuf.at[d], gs.at[j], gr.at[j], at.dp_to(j)) for j in range(1, nd)]
    hw = width // 2

    def share_half(i, sem):
        c = pl.ds(i * hw, hw)
        return SeqGather(at, cot.at[:, c], lambda r: cotall.at[block_of(r, T), c], sem)

    share_cot = [share_half(0, (cs, cr)), share_half(1, (cs2, cr2))]
    share_nm = SeqGather(at, xall.at[own], lambda r: xall.at[block_of(r, T)], (ns_, nr))
    take_qkv = Gather(at, wqkv_mine, wqkv, sems[0:6])
    wo, mycols = nmT.at[0], block_of(s, cw)

    def out_z(j):
        rows = wo.at[block_of(at.zz, R), mycols]
        return remote(wout_mine.at[:, mycols], rows, sems[6].at[j], sems[7].at[j], at.z_device(at.z_index(j)))

    out_local = pltpu.make_async_copy(wout_mine.at[:, mycols], wo.at[block_of(at.zz, R), mycols], sems[11].at[0])
    share_out = SeqGather(at, wo.at[:, mycols], lambda r: wo.at[:, block_of(r, cw)], (wos, wor))

    def out_across(z):
        rows = wout.at[block_of(2 * z + core, R)]
        return remote(wo.at[pl.ds(z * R, R)], rows, sems[8].at[z], sems[9].at[z], at.sib)

    def out_keep(z):
        return pltpu.make_async_copy(wo.at[pl.ds(z * R, R)], wout.at[block_of(2 * z + core, R)], wok.at[z])

    base = L // 2
    take_gate = Gather(at, gb.at[pl.ds(base, R), pl.ds(0, n)], gu.at[:, pl.ds(0, n)], sems[12:18])
    take_up = Gather(at, gb.at[pl.ds(base, R), pl.ds(n, n)], gu.at[:, pl.ds(n, n)], sems[59:65])
    take_dn = Gather(at, dn_mine, dn, sems[18:24])
    for c in g_copies:
        c.start()
    share_x.start()
    take_qkv.start()
    for j in range(1, nz):
        out_z(j).start()
    out_local.start()
    xall[own, :] = x[...]
    gbuf[d] = gains[...]
    cot_local = pltpu.make_async_copy(cot, cotall.at[own], loc.at[0])
    cot_local.start()
    ff = wgate.shape[1]
    parts = max(1, -(-ff // (2 * n)))
    while nd % parts:
        parts += 1
    span = ff // parts
    stage = []
    for i, w in enumerate((wgate, wup)):
        for k in range(parts):
            row = pl.ds((i * parts + k) * R, R)
            stage.append(
                pltpu.make_async_copy(w.at[:, pl.ds(k * span, span)], gb.at[row, pl.ds(0, span)], wl.at[i, k])
            )
    for c in stage:
        c.start()
    for c in stage:
        c.wait()
    real = wgate.shape[1] // nd // ns
    gap = [jnp.zeros((R, piece - real), BF16)] if piece > real else []
    for i in range(ns):

        @pl.when(s == i)
        def _():
            cuts = []
            for w in range(2):
                for k in range(nd):
                    a = (k * ns + i) * real
                    row = (w * parts + a // span) * R
                    cuts += [gb[row : row + R, a % span : a % span + real]] + gap
            gb[base : base + R, :] = jnp.concatenate(cuts, axis=1)


    for c in g_copies:
        c.wait_recv()
    gain_in = jnp.concatenate([gbuf[k][0:1, :gl] for k in range(nd)], axis=1)
    gain_mid = jnp.concatenate([gbuf[k][1:2, :gl] for k in range(nd)], axis=1)
    gain_qk = jnp.concatenate([gbuf[k][2:3, :ql] for k in range(nd)], axis=1)
    gsum[...] = jnp.zeros_like(gsum)
    gsum[0:1, :] = gain_in
    gsum[1:2, :] = gain_mid
    gsum[2:3, : 2 * HD] = gain_qk
    columns = jnp.transpose(jnp.broadcast_to(gain_qk, (8, 2 * HD)))
    gain_q, gain_k = columns[:HD, 0:1], columns[HD:, 0:1]
    take_qkv.hop()
    take_gate.start()
    take_up.start()
    take_dn.start()
    for j in range(ns):
        rows = block_of(at.gather_rank(j), T)
        if j == 1:
            share_x.hop()
        if j:
            share_x.wait(j)
        xc = xall[rows, :].astype(F32)
        scale = lax.rsqrt(jnp.mean(xc * xc, axis=-1, keepdims=True) + EPSILON)
        normed[rows, :] = (xc * scale * gain_in).astype(BF16)
    for j in range(1, nz):
        out_z(j).wait_recv()
    out_local.wait()
    share_out.start()
    take_qkv.arrive()
    take_qkv.finish()
    for j in range(ns):
        rows = pl.ds(j * T, T)
        proj = mm(normed[rows, :], wqkv[...])
        projT[:, rows] = jnp.transpose(proj[:, : qw + kw])
        val = proj[:, qw + kw :]
        vT[:, rows] = jnp.transpose(val).astype(BF16)
        for i in range(hk):
            vrows[i, rows, :] = val[:, i * HD : (i + 1) * HD].astype(BF16)

    half = HD // 2

    def rope(row, gain, factor):
        u = projT[row, :]
        scale = lax.rsqrt(jnp.mean(u * u, axis=0, keepdims=True) + EPSILON)
        u = u * scale * gain
        a, b = u[:half], u[half:]
        return jnp.concatenate([a * cos[...] - b * sin[...], b * cos[...] + a * sin[...]], axis=0) * factor

    def rope_query(h, carry):
        row = block_of(h, HD)
        qT[row, :] = rope(row, gain_q, HD**-0.5).astype(BF16)
        return carry

    lax.fori_loop(0, hq, rope_query, 0)
    for i in range(hk):
        r = rope(pl.ds(qw + i * HD, HD), gain_k, 1.0)
        kT[i * HD : (i + 1) * HD, :] = r.astype(BF16)
        krows[i, :, :] = jnp.transpose(r).astype(BF16)

    share_x.drain()
    share_out.hop()
    take_gate.hop()
    keep = lax.broadcasted_iota(jnp.int32, (T, T), 0) <= lax.broadcasted_iota(jnp.int32, (T, T), 1)
    block = block_of(s, qw)

    def mixed_out(rb):
        return remote(mixT.at[rb], mrowsT.at[block], ms.at[rb], mr.at[s], (d, rb))

    for rb in range(ns):
        cols = pl.ds(rb * T, T)
        span = rb * T

        def head(h, carry):
            kv = h // group
            row, vrow = block_of(h, HD), block_of(kv, HD)
            q = qT[row, cols]
            p = jnp.where(keep, jnp.exp(mm(krows[kv, cols, :], q)), 0.0)
            tot = jnp.sum(p, axis=0, keepdims=True)
            m = mm(vT[vrow, cols], p.astype(BF16))
            if span:
                p = jnp.exp(mm(krows[kv, 0:span, :], q))
                tot = tot + jnp.sum(p, axis=0, keepdims=True)
                m = m + mm(vT[vrow, 0:span], p.astype(BF16))
            one = 1.0 / tot
            inv[h, :, cols] = one
            mixT[rb, row, :] = (m * one).astype(BF16)
            return carry

        lax.fori_loop(0, hq, head, 0)
        pl.when(s != rb)(mixed_out(rb).start)
        if rb == ns - 1:
            share_out.finish()
            for z in range(nz):
                out_across(z).start()
                out_keep(z).start()

    share_cot[0].start()
    mrowsT[block, :] = mixT[s]
    for j in range(1, ns):
        src = at.seq_from(j)
        remote(mixT.at[0], mrowsT.at[block_of(src, qw)], ms.at[0], mr.at[src], (d, src)).wait_recv()
    for z in range(nz):
        out_across(z).wait_recv()
        out_keep(z).wait()
    residual = x[...].astype(F32) + mm(jnp.transpose(mrowsT[...]), wout[...])
    resid[...] = residual
    scale_mid = lax.rsqrt(jnp.mean(residual * residual, axis=-1, keepdims=True) + EPSILON)
    xall[own, :] = (residual * scale_mid * gain_mid).astype(BF16)
    share_nm.start()
    take_up.hop()
    share_nm.hop()
    share_cot[0].hop()
    share_cot[1].start()
    take_dn.hop()
    take_gate.arrive()
    take_up.arrive()
    ft, nt, wt = n, 1, width

    take_gate.drain_own()
    take_up.drain_own()
    take_gate.finish()
    take_up.finish()
    for j in range(ns):
        if j == ns - 1:
            share_cot[1].hop()
        if j:
            share_nm.wait(j)
        rows = block_of(at.gather_rank(j), T)
        for i in range(2):
            f = pl.ds(i * n, n)
            gb[rows, f] = mm(xall[rows, :], gu[:, f]).astype(BF16)
    share_nm.drain()
    share_out.drain()
    for z in range(nz):
        out_across(z).wait_send()
    for k in range(nd):
        nmT[k % 2, (k // 2) * R : (k // 2 + 1) * R, :] = jnp.transpose(xall[:, k * R : (k + 1) * R])
    take_dn.arrive()
    take_dn.finish()
    share_cot[0].finish()
    share_cot[1].finish()
    cot_local.wait()
    sum_nm = SeqReduce(at, T, gsend, grecv, (ps, pr))
    for j in list(range(1, ns)) + [0]:
        if j == 0:
            sum_nm.hop()
        rows = block_of(at.reduce_rank(j), T)
        stage = pl.ds((j - 1) * T, T)

        def hidden_tile(i, carry):
            f, f2 = block_of(i, ft), block_of(i + nt, ft)
            gate, up = gb[rows, f].astype(F32), gb[rows, f2].astype(F32)
            sig = 1.0 / (1.0 + jnp.exp(-gate))
            act = gate * sig
            back = mm_nt(cotall[rows, :], dn[f, :])
            hid = act * up
            hrow[:, f] = hid.astype(BF16)
            hid = jnp.transpose(hid.astype(BF16))
            for k in range(nd):
                first = (k % 2) * nz * piece + (k // 2) * piece
                hT[first : first + piece, rows] = hid[k * piece : (k + 1) * piece]
            gb[rows, f] = (back * up * sig * (1.0 + gate * (1.0 - sig))).astype(BF16)
            gb[rows, f2] = (back * act).astype(BF16)
            return carry

        lax.fori_loop(0, nt, hidden_tile, 0)

        def back_tile(i, carry):
            w = block_of(i, wt)
            part = mm_nt(gb[rows, :], gu[w, :])
            if j:
                gsend[stage, w] = part.astype(BF16)
            else:
                gown[:, w] = part
            return carry

        lax.fori_loop(0, width // wt, back_tile, 0)
        if j:
            sum_nm.push(j)

        def out_tile(i, carry):
            w = block_of(i, wt)
            part = mm(hrow[...], dn[:, w])
            if j:
                osend[stage, w] = part.astype(BF16)
            else:
                oown[:, w] = part + resid[:, w]
            return carry

        lax.fori_loop(0, width // wt, out_tile, 0)

    share_cot[0].drain()
    share_cot[1].drain()
    take_gate.drain_rest()
    take_up.drain_rest()
    take_dn.drain()
    half_gu, half_dn = nz * R, nz * piece
    dns, dnown = dn.at[pl.ds(0, half_dn)], dn.at[pl.ds(half_dn, half_dn)]
    gus, gateown = (gu.at[pl.ds(i * half_gu, half_gu), pl.ds(0, n)] for i in range(2))
    uus, upown = (gu.at[pl.ds(i * half_gu, half_gu), pl.ds(n, n)] for i in range(2))
    dn_sum = Scatter(at, dnown, dnz, dnf, dnall, sems[24:31])
    gate_sum = Scatter(at, gateown, gaz, gaf, gateall, sems[31:38])
    up_sum = Scatter(at, upown, upz, upf, upall, sems[38:45])
    qkv_sum = Scatter(at, qkown, qkz, qkf, qkvall, sems[45:52])
    out_sum = Scatter(at, goown, goz, gof, outall, sems[52:59])

    def dn_part(c, i):
        return mm(hT[block_of(c, nz * piece), :], cotall[:, block_of(i, 512)])

    tiles = n // 384
    tw = n // tiles

    def other(buf, base):
        def tile(i, carry):
            f = block_of(i, tw)
            buf[:, f] = mm(nmT[1 - core], gb[:, pl.ds(pl.multiple_of(base + i * tw, 128), tw)]).astype(BF16)
            return carry

        lax.fori_loop(0, tiles, tile, 0)

    def summed(buf, got, base):
        def tile(i, carry):
            f = block_of(i, tw)
            part = mm(nmT[core], gb[:, pl.ds(pl.multiple_of(base + i * tw, 128), tw)])
            buf[:, f] = (part + got[:, f].astype(F32)).astype(BF16)
            return carry

        lax.fori_loop(0, tiles, tile, 0)

    dn_copy = remote(dns, dnr, ss.at[0], sr.at[0], at.sib)
    gate_copy = remote(gus, gur, ss.at[1], sr.at[1], at.sib)
    up_copy = remote(uus, uur, ss.at[2], sr.at[2], at.sib)

    def dn_other(i, carry):
        dns[:, block_of(i, 512)] = dn_part(1 - core, i).astype(BF16)
        return carry

    def dn_mine(i, carry):
        dnown[:, block_of(i, 512)] = dn_part(core, i).astype(BF16)
        return carry

    lax.fori_loop(0, width // 512, dn_other, 0)
    dn_copy.start()
    lax.fori_loop(0, width // 512, dn_mine, 0)
    dn_copy.wait_recv()
    dnown[...] = (dnown[...].astype(F32) + dnr[...].astype(F32)).astype(BF16)
    dn_sum.start()
    other(gus, 0)
    gate_copy.start()
    gnm = sum_nm.total(gown[...])
    sum_nm.drain()
    residual = resid[...]
    scale_mid = lax.rsqrt(jnp.mean(residual * residual, axis=-1, keepdims=True) + EPSILON)
    gsecond[...] = jnp.broadcast_to(jnp.sum(gnm * residual * scale_mid, axis=0, keepdims=True), (8, width))
    weighted = gnm * gain_mid
    gown[...] = (
        cotall[own, :].astype(F32)
        + scale_mid * weighted
        - residual * (scale_mid * scale_mid * scale_mid) * jnp.mean(weighted * residual, axis=-1, keepdims=True)
    )
    rback = gown[...].astype(BF16)

    def mixed_back(p):
        return remote(gsend.at[pl.ds(0, T), pl.ds(p * qw, qw)], grows.at[own], bs.at[p], br.at[s], (d, p))

    for p in range(ns):
        gsend[0:T, p * qw : (p + 1) * qw] = mm_nt(rback, wout[p * qw : (p + 1) * qw, :]).astype(BF16)
        pl.when(s != p)(mixed_back(p).start)
    grows[own, :] = gsend[0:T, block_of(s, qw)]

    sum_outputs = SeqReduce(at, T, osend, xall, (os_, or_))
    for j in range(1, ns):
        sum_outputs.push(j)
    other(uus, n)
    up_copy.start()
    gate_copy.wait_recv()
    summed(gateown, gur, 0)
    gate_sum.start()
    up_copy.wait_recv()
    summed(upown, uur, n)
    up_sum.start()
    for k in range(nd):
        nmT[k % 2, (k // 2) * R : (k // 2 + 1) * R, :] = mm(mrowsT[k * R : (k + 1) * R, :], rback).astype(BF16)
    go_copy = remote(nmT.at[1 - core], gor, ss2.at[0], sr2.at[0], at.sib)
    go_copy.start()
    for i in range(hk):
        qrows[i, :, :] = jnp.transpose(qT[i * group * HD : (i + 1) * group * HD, :])
    go_copy.wait_recv()
    gate_copy.wait_send()
    up_copy.wait_send()
    sum_gout = SeqReduce(at, nz * R, gostage, gorecv, (gos, gorc))

    def gout_columns(r):
        c = block_of(r, cw)
        return nmT[core, :, c].astype(F32) + gor[:, c].astype(F32)

    for j in range(1, ns):
        gostage[pl.ds((j - 1) * nz * R, nz * R), :] = gout_columns(at.reduce_rank(j)).astype(BF16)
    for j in range(1, ns):
        src = at.seq_from(j)
        remote(gsend.at[pl.ds(0, T), pl.ds(0, qw)], grows.at[block_of(src, T)], bs.at[0], br.at[src], (d, src)).wait_recv()
    for i in range(ns):
        rows = pl.ds(i * T, T)
        hT[pw : pw + qw, rows] = jnp.transpose(grows[rows, :])

    for j in range(1, ns):
        sum_gout.push(j)
    dn_sum.relay()

    causal = lax.broadcasted_iota(jnp.int32, (T, T), 0) <= lax.broadcasted_iota(jnp.int32, (T, T), 1)
    causal = jnp.concatenate([causal] * group, axis=1)
    gk[...] = jnp.zeros_like(gk)
    gv[...] = jnp.zeros_like(gv)

    def key_head(kv, carry):
        krow = block_of(kv, HD)
        lanes = block_of(kv, group * HD)
        for rb in range(ns):
            cols = pl.ds(rb * T, T)

            def side(ref, base):
                return jnp.concatenate(
                    [ref[pl.ds(pl.multiple_of(base + (kv * group + u) * HD, HD), HD), cols] for u in range(group)],
                    axis=1,
                )

            q, g = side(qT, 0), side(hT, pw)
            one = jnp.concatenate([inv[kv * group + u, :, cols] for u in range(group)], axis=1)
            m = jnp.concatenate(
                [mixT[rb, block_of(kv * group + u, HD), :] for u in range(group)], axis=1
            )
            delta = jnp.sum(g.astype(F32) * m.astype(F32), axis=0, keepdims=True)
            gr, qr = grows[cols, lanes], qrows[kv, cols, :]
            gr = jnp.concatenate([gr[:, u * HD : (u + 1) * HD] for u in range(group)], axis=0)
            qr = jnp.concatenate([qr[:, u * HD : (u + 1) * HD] for u in range(group)], axis=0)
            gq = jnp.zeros((HD, group * T), F32)
            for part, masked in ((pl.ds(0, rb * T), False), (cols, True)):
                if rb == 0 and not masked:
                    continue
                p = jnp.exp(mm(krows[kv, part, :], q)) * one
                if masked:
                    p = jnp.where(causal, p, 0.0)
                gp = mm(vrows[kv, part, :], g)
                ds = (p * (gp - delta)).astype(BF16)
                gv[kv, part, :] += mm(p.astype(BF16), gr)
                gk[kv, part, :] += mm(ds, qr)
                gq = gq + mm(kT[krow, part], ds)
            gq = gq * HD**-0.5
            for u in range(group):
                gqT[block_of(kv * group + u, HD), cols] = gq[:, u * T : (u + 1) * T]
        return carry

    lax.fori_loop(0, hk, key_head, 0)

    sum_outputs.hop()
    columns = jnp.transpose(gsum[:, : 2 * HD])
    gain_q, gain_k = columns[:HD, 2:3], columns[HD:, 2:3]

    def norm_column(row, g, gain):
        a, b = g[:half], g[half:]
        g = jnp.concatenate([a * cos[...] + b * sin[...], b * cos[...] - a * sin[...]], axis=0)
        u = projT[row, :]
        scale = lax.rsqrt(jnp.mean(u * u, axis=0, keepdims=True) + EPSILON)
        us = u * scale
        weighted = g * gain
        inner = jnp.mean(weighted * us, axis=0, keepdims=True)
        hT[row, :] = (scale * (weighted - us * inner)).astype(BF16)
        return jnp.sum(g * us, axis=1, keepdims=True)

    def query_back(h, acc):
        row = block_of(h, HD)
        return acc + norm_column(row, gqT[row, :], gain_q)

    gain_grad_q = lax.fori_loop(0, hq, query_back, jnp.zeros((HD, 1), F32))
    gain_grad_k = jnp.zeros((HD, 1), F32)
    for i in range(hk):
        gain_grad_k = gain_grad_k + norm_column(pl.ds(qw + i * HD, HD), jnp.transpose(gk[i]), gain_k)
        hT[qw + kw + i * HD : qw + kw + (i + 1) * HD, :] = jnp.transpose(gv[i]).astype(BF16)

    sum_gout.hop()
    gate_sum.relay()

    sum_ni = SeqReduce(at, T, gsend, grecv, (nis, nir))
    for p in range(ns):
        pl.when(s != p)(mixed_back(p).wait_send)
    for i in range(ns):
        rows = pl.ds(i * T, T)
        cotall[rows, 0:pw] = jnp.transpose(hT[0:pw, rows])
    for j in list(range(1, ns)) + [0]:
        part = mm_nt(cotall[block_of(at.reduce_rank(j), T), 0:pw], wqkv[...])
        if j:
            gsend[pl.ds((j - 1) * T, T), :] = part.astype(BF16)
            sum_ni.push(j)
        else:
            resid[...] = part
    for k in range(nd):
        part = mm(hT[0:pw, :], normed[:, k * R : (k + 1) * R])
        gb[((k % 2) * nz + k // 2) * R : ((k % 2) * nz + k // 2 + 1) * R, 0:pw] = jnp.transpose(part).astype(BF16)
    qk_copy = remote(gb.at[block_of(1 - core, nz * R), pl.ds(0, pw)], qkr, ss2.at[1], sr2.at[1], at.sib)
    qk_copy.start()
    sum_ni.hop()
    dn_sum.total()
    goown[...] = sum_gout.total(gout_columns(s)).astype(BF16)
    out_sum.start()
    qk_copy.wait_recv()
    qkown[...] = (gb[block_of(core, nz * R), pl.ds(0, pw)].astype(F32) + qkr[...].astype(F32)).astype(BF16)
    qkv_sum.start()
    up_sum.relay()
    out_sum.relay()
    gate_sum.total()
    qkv_sum.relay()

    gni = sum_ni.total(resid[...])
    dn_sum.share.hop()
    stream = x[...].astype(F32)
    scale = lax.rsqrt(jnp.mean(stream * stream, axis=-1, keepdims=True) + EPSILON)
    unit = stream * scale
    weighted = gni * gsum[0:1, :]
    gown[...] = gown[...] + scale * (weighted - unit * jnp.mean(weighted * unit, axis=-1, keepdims=True))
    stream_store = pltpu.make_async_copy(gown, gstream, loc.at[2])
    stream_store.start()
    first = jnp.sum(gni * unit, axis=0, keepdims=True)
    qk = jnp.broadcast_to(jnp.concatenate([gain_grad_q, gain_grad_k], axis=0), (2 * HD, 128))
    sm0[0:1, :] = first
    sm0[1:2, :] = gsecond[0:1, :]
    sm0[2:8, :] = jnp.zeros((6, width), F32)
    sm0[2:3, : 2 * HD] = jnp.transpose(qk)[0:1, :]

    def small_seq(j):
        return remote(sm0, sm1.at[j - 1], s1.at[j], r1.at[j], at.seq_to(j))

    def small_dp(j):
        return remote(sm2.at[at.dp_to(j)[0]], sm3.at[j - 1], s2.at[j], r2.at[j], at.dp_to(j))

    for j in range(1, ns):
        small_seq(j).start()
    gate_sum.share.hop()
    up_sum.total()
    acc = sum_outputs.total(oown[...])
    last = pl.ds((ns - 1) * T, T)
    xall[last, :] = acc.astype(BF16)
    out_store = pltpu.make_async_copy(xall.at[last], outputs, loc.at[1])
    out_store.start()
    for j in range(1, ns):
        small_seq(j).wait_recv()
    acc = sm0[...]
    for j in range(1, ns):
        acc = acc + sm1[j - 1]
    sm2[...] = jnp.zeros_like(sm2)
    for k in range(nd):
        sm2[k, 0:2, :gl] = acc[0:2, k * gl : (k + 1) * gl]
        sm2[k, 2:3, :ql] = acc[2:3, k * ql : (k + 1) * ql]
    for j in range(1, nd):
        small_dp(j).start()
    out_sum.total()
    qkv_sum.total()
    up_sum.share.hop()
    out_sum.share.hop()
    qkv_sum.share.hop()
    for j in range(1, nd):
        small_dp(j).wait_recv()
    acc = sm2[d]
    for j in range(1, nd):
        acc = acc + sm3[j - 1]
    small[...] = acc

    go_copy.wait_send()
    qk_copy.wait_send()
    for j in range(1, ns):
        small_seq(j).wait_send()
    for j in range(1, nd):
        small_dp(j).wait_send()
    for rb in range(ns):
        pl.when(s != rb)(mixed_out(rb).wait_send)
    for t in (sum_outputs, sum_ni, sum_gout):
        t.drain()
    for c in g_copies + [dn_copy]:
        c.wait_send()
    take_qkv.drain()
    for j in range(1, nz):
        out_z(j).wait_send()
    for t in (dn_sum, out_sum, qkv_sum, gate_sum, up_sum):
        t.drain()
    out_store.wait()
    stream_store.wait()


def vmem(n):
    return [pl.BlockSpec(memory_space=pltpu.VMEM)] * n


def block(ns, nd, piece, x, gain1, gain2, gainqk, w_qkv, w_out, cot, w_gate, w_up, w_down):
    T, width = x.shape
    L = ns * T
    R = w_qkv.shape[0]
    n = nd * piece
    n2 = 2 * n
    nz = nd // 2
    hq, hk = H // ns, KV // ns
    qw, kw = hq * HD, hk * HD
    pw = qw + 2 * kw
    cw = width // ns
    cos, sin = rope_columns(L)
    sh, vm = jax.ShapeDtypeStruct, pltpu.VMEM
    outs = (
        sh((T, width), BF16), sh((T, width), F32), sh((ns, R, n), BF16), sh((ns, R, n), BF16),
        sh((ns, piece, width), BF16), sh((ns, R, pw), BF16), sh((ns, R, cw), BF16), sh((8, 128), F32),
    )
    hbm = pl.BlockSpec(memory_space=pl.ANY)
    scratch = [
        vm((L, width), BF16), vm((qw + kw, L), F32), vm((qw, L), BF16), vm((kw, L), BF16),
        vm((hk, L, HD), BF16), vm((hk, L, HD), BF16), vm((hq, 1, L), F32), vm((ns, qw, T), BF16),
        vm((H * HD, T), BF16), vm((H * HD, width), BF16), vm((width, pw), BF16), vm((8, width), F32),
        vm(((ns - 1) * T, width), BF16), vm((T, width), F32), vm((8, width), F32),
        vm((kw, L), BF16), vm((T, width), F32), vm((L, width), BF16), vm((L, width), BF16), vm((8, 128), F32),
        vm((nd, 8, 128), F32), vm((R, pw), BF16), vm((nd * R, n2), BF16), vm((n, width), BF16),
        vm((T, n), BF16), vm((n, L), BF16), vm((L, n2), BF16), vm(((ns - 1) * T, width), BF16),
        vm(((ns - 1) * T, width), BF16), vm((T, width), F32), vm((2, nz * R, L), BF16),
        vm((nz * R, n), BF16), vm((nz * R, n), BF16), vm((nz * piece, width), BF16),
        vm((nz, R, n), BF16), vm((R, n), BF16), vm((nz, R, n), BF16), vm((R, n), BF16),
        vm((nz, piece, width), BF16), vm((piece, width), BF16), vm((L, qw), BF16),
        vm((hk, L, qw // hk), BF16), vm((hk, L, HD), F32), vm((hk, L, HD), F32), vm((qw, L), F32),
        vm((nz * R, pw), BF16), vm((nz * R, pw), BF16), vm((nz, R, pw), BF16), vm((R, pw), BF16),
        vm((nz * R, width), BF16), vm(((ns - 1) * nz * R, cw), BF16), vm(((ns - 1) * nz * R, cw), BF16), vm((nz * R, cw), BF16),
        vm((nz, R, cw), BF16), vm((R, cw), BF16),
        vm((8, width), F32), vm((ns - 1, 8, width), F32), vm((nd, 8, 128), F32), vm((nd - 1, 8, 128), F32),
    ]
    sems = seq_sems(ns) + [DMA((nd,)), DMA((nd,))] + seq_sems(ns) + [DMA((ns,))] * 2 + seq_sems(ns) * 2
    sems += [DMA((3,)), DMA((3,))]
    sems += [DMA((3,)), DMA((2, 8))]
    sems += seq_sems(ns) + [DMA((ns,))] * 2 + seq_sems(ns) + [DMA((2,)), DMA((2,))] + seq_sems(ns) + [DMA((ns,))] * 2 + [DMA((nd,)), DMA((nd,))]
    sems += seq_sems(ns) + [DMA((nz,))] + seq_sems(ns)
    return pl.pallas_call(
        functools.partial(block_kernel, ns, nd),
        out_shape=outs,
        in_specs=vmem(5) + [hbm] * 5 + vmem(2),
        out_specs=[hbm] * 7 + vmem(1),
        scratch_shapes=scratch + sems + gather_sems(nz) * 4 + scatter_sems(ns, nz) * 5 + gather_sems(nz),
        compiler_params=pltpu.CompilerParams(
            collective_id=0, has_side_effects=True, vmem_limit_bytes=VMEM_LIMIT
        ),
        cost_estimate=pl.CostEstimate(flops=38_000_000_000, bytes_accessed=40_000_000, transcendentals=12_000_000),
    )(x, gain1, gain2, gainqk, w_qkv, w_out, cot, w_gate, w_up, w_down, cos, sin)


def finish_kernel(
    ns, nd, piece, gateall, upall, qkvall, outall, dnall, got, stream, sums,
    gate, up, qkv, out, down, outputs, gstream, first, second, qk,
):
    outputs[...] = got[...]
    gstream[...] = stream[...]
    for i, ref in enumerate((first, second, qk)):
        ref[...] = sums[i : i + 1, : ref.shape[1]]
    hq, hk = H // ns, KV // ns
    qw, kw = hq * HD, hk * HD
    pad = gateall.shape[2] // nd
    for ref, got in ((gate, gateall), (up, upall)):
        parts = [got[i].astype(F32) for i in range(ns)]
        ref[...] = jnp.concatenate(
            [parts[i][:, k * pad : k * pad + piece] for k in range(nd) for i in range(ns)], axis=1
        )
    parts = [qkvall[i].astype(F32) for i in range(ns)]
    qkv[...] = jnp.concatenate(
        [p[:, :qw] for p in parts] + [p[:, qw : qw + kw] for p in parts] + [p[:, qw + kw :] for p in parts], axis=1
    )
    out[...] = jnp.concatenate([outall[i].astype(F32) for i in range(ns)], axis=1)
    down[...] = jnp.concatenate([dnall[i].astype(F32)[:piece] for i in range(dnall.shape[0])], axis=0)


def finish(ns, nd, piece, gateall, upall, qkvall, outall, dnall, got, stream, sums):
    R = gateall.shape[1]
    T, width = got.shape
    steps = 4
    rows = R // steps
    ff = ns * nd * piece
    widths = (ff, ff, ns * qkvall.shape[2], ns * outall.shape[2])
    many = ns // steps
    lines = (R, R, 2 * HD // nd)
    ins = [pl.BlockSpec((ns, rows, a.shape[2]), lambda i: (0, i, 0)) for a in (gateall, upall, qkvall, outall)]
    ins.append(pl.BlockSpec((many,) + dnall.shape[1:], lambda i: (i, 0, 0)))
    tokens = pl.BlockSpec((T // steps, width), lambda i: (i, 0))
    ins += [tokens, tokens, pl.BlockSpec((8, 128), lambda i: (0, 0))]
    outs = [pl.BlockSpec((rows, w), lambda i: (i, 0)) for w in widths]
    outs += [pl.BlockSpec((many * piece, width), lambda i: (i, 0)), tokens, tokens]
    outs += [pl.BlockSpec((1, w), lambda i: (0, 0)) for w in lines]
    sh = jax.ShapeDtypeStruct
    return pl.pallas_call(
        functools.partial(finish_kernel, ns, nd, piece),
        grid=(steps,),
        out_shape=[sh((R, w), F32) for w in widths]
        + [sh((ns * piece, width), F32), sh((T, width), BF16), sh((T, width), F32)]
        + [sh((1, w), F32) for w in lines],
        in_specs=ins,
        out_specs=outs,
        compiler_params=pltpu.CompilerParams(vmem_limit_bytes=60 << 20),
    )(gateall, upall, qkvall, outall, dnall, got, stream, sums)


def shards(inputs, cotangent, first_gain, w_qkv, qk_gain, w_out, second_gain, w_gate, w_up, w_down):
    ns, nd = lax.axis_size("seq"), lax.axis_size("dp")
    s, d = lax.axis_index("seq"), lax.axis_index("dp")
    piece = w_down.shape[0] // ns
    pad = -piece % 16
    down_rows = w_down
    if pad:
        down_rows = jnp.pad(lax.dynamic_slice_in_dim(w_down, s * piece, piece, 0), ((0, pad), (0, 0)))
    x = inputs[0]
    outputs, gstream, gateall, upall, dnall, qkvall, outall, small = block(
        ns, nd, piece + pad, x, first_gain[None], second_gain[None], qk_gain[None], w_qkv, w_out, cotangent[0],
        w_gate, w_up, down_rows,
    )
    gate, up, qkv, out, down, outputs, gstream, first, second, qk = finish(
        ns, nd, piece, gateall, upall, qkvall, outall, dnall, outputs, gstream, small
    )
    return (outputs[None], gstream[None], first[0], qkv, qk[0], out, second[0], gate, up, down)


def solution(mesh):
    act = P("dp", "seq", None)
    vec, mat = P("dp"), P("dp", None)
    in_specs = (act, act, vec, mat, vec, mat, vec, mat, mat, mat)
    out_specs = (act, act, vec, mat, vec, mat, vec, mat, mat, mat)
    return jax.shard_map(shards, mesh=mesh, in_specs=in_specs, out_specs=out_specs, check_vma=False)
```

```python
import functools

import jax
import jax.numpy as jnp
import numpy as np
from jax import lax
from jax.experimental import pallas as pl
from jax.experimental.pallas import tpu as pltpu
from jax.sharding import PartitionSpec as P

H = 16
KV = 8
HD = 64
EPSILON = 1e-06
THETA_BASE = 1000000.0
F32 = jnp.float32
BF16 = jnp.bfloat16
VMEM_LIMIT = 65000 << 10


def rope_columns(length):
    inverse = np.float32(THETA_BASE) ** (-np.arange(0, HD, 2).astype(np.float32) / np.float32(HD))
    angles = (np.arange(length, dtype=np.float32)[None, :] * inverse.astype(np.float32)[:, None]).astype(np.float32)
    angles = angles.astype(np.float64)
    return jnp.asarray(np.cos(angles), F32), jnp.asarray(np.sin(angles), F32)


MESH = pl.DeviceIdType.MESH
DMA = pltpu.SemaphoreType.DMA


def mm(a, b):
    return jnp.dot(a, b, preferred_element_type=F32)


def mm_nt(a, b):
    return lax.dot_general(a, b, (((1,), (1,)), ((), ())), preferred_element_type=F32)


def remote(src, dst, send, recv, device):
    return pltpu.make_async_remote_copy(
        src_ref=src, dst_ref=dst, send_sem=send, recv_sem=recv, device_id=device, device_id_type=MESH
    )


def block_of(index, size):
    return pl.ds(pl.multiple_of(index * size, size), size)


class Place:
    def __init__(self, ns, nd):
        self.ns, self.nd, self.nz = ns, nd, nd // 2
        self.d, self.s = lax.axis_index("dp"), lax.axis_index("seq")
        self.zz, self.core = self.d // 2, lax.rem(self.d, 2)
        self.sib = (self.d + 1 - 2 * self.core, self.s)

    def seq_to(self, j):
        return (self.d, lax.rem(self.s + j, self.ns))

    def seq_from(self, j):
        return lax.rem(self.s + self.ns - j, self.ns)

    def across(self):
        return (self.s + 1 - 2 * lax.rem(self.s, 2), lax.rem(self.s + 2, 4), 3 - self.s)

    def gather_rank(self, j):
        if j == 0:
            return self.s
        return self.across()[j - 1] if self.ns == 4 else self.seq_from(j)

    def reduce_rank(self, j):
        if j == 0:
            return self.s
        x, y, o = self.across()
        return (o, x, y)[j - 1] if self.ns == 4 else lax.rem(self.s + j, self.ns)

    def dp_to(self, j):
        return (lax.rem(self.d + j, self.nd), self.s)

    def z_index(self, j):
        return lax.rem(self.zz + j, self.nz)

    def z_from(self, j):
        return lax.rem(self.zz + self.nz - j, self.nz)

    def z_device(self, z):
        return (2 * z + self.core, self.s)

    def greet(self):
        bar = pltpu.get_barrier_semaphore()
        for j in range(1, self.nd):
            pl.semaphore_signal(bar, inc=1, device_id=self.dp_to(j), device_id_type=MESH)
        for j in range(1, self.ns):
            pl.semaphore_signal(bar, inc=1, device_id=self.seq_to(j), device_id_type=MESH)
        pl.semaphore_wait(bar, self.nd + self.ns - 2)


class SeqGather:
    def __init__(self, at, src, dst, sems):
        self.at, self.src, self.dst = at, src, dst
        self.send, self.recv = sems
        self.half = src.shape[0] // 2

    def direct(self, j):
        at = self.at
        to = at.across()[j - 1] if at.ns == 4 else at.seq_to(j)[1]
        return remote(self.src, self.dst(at.s), self.send.at[j], self.recv.at[j], (at.d, to))

    def forward(self, i):
        at = self.at
        part = self.dst(at.across()[i]).at[pl.ds(i * self.half, self.half)]
        return remote(part, part, self.send.at[3 + i], self.recv.at[3 + i], (at.d, at.across()[1 - i]))

    def near(self):
        return range(1, 3 if self.at.ns == 4 else self.at.ns)

    def start(self):
        for j in self.near():
            self.direct(j).start()

    def hop(self):
        if self.at.ns == 4:
            for i in range(2):
                self.direct(i + 1).wait_recv()
                self.forward(i).start()

    def wait(self, j):
        if self.at.ns != 4:
            self.direct(j).wait_recv()
        elif j == 3:
            for i in range(2):
                self.forward(i).wait_recv()

    def finish(self):
        for j in range(1, self.at.ns):
            self.wait(j)

    def drain(self):
        for j in self.near():
            self.direct(j).wait_send()
        if self.at.ns == 4:
            for i in range(2):
                self.forward(i).wait_send()


def seq_sems(ns):
    return [DMA((max(ns, 6),)), DMA((max(ns, 6),))]


class SeqReduce:
    def __init__(self, at, rows, stage, inbox, sems):
        self.at, self.rows, self.stage, self.inbox = at, rows, stage, inbox
        self.send, self.recv = sems

    def part(self, ref, block, half=None):
        if half is None:
            return ref.at[pl.ds(block * self.rows, self.rows)]
        h = self.rows // 2
        return ref.at[pl.ds(block * self.rows + half * h, h)]

    def leg(self, k):
        at = self.at
        if at.ns != 4:
            src, dst, to = self.part(self.stage, k - 1), self.part(self.inbox, k - 1), at.seq_to(k)[1]
        else:
            b, h, i, n = ((0, 0, 2, 0), (0, 1, 2, 1), (1, 0, 0, 0), (2, 1, 1, 1), (2, 0, 1, 1), (1, 1, 0, 0))[k]
            src, dst, to = self.part(self.stage, b, h), self.part(self.inbox, i, h), at.across()[n]
        return remote(src, dst, self.send.at[k], self.recv.at[k], (at.d, to))

    def push(self, j):
        for k in (j,) if self.at.ns != 4 else ((), (0, 1), (2,), (3,))[j]:
            self.leg(k).start()

    def hop(self):
        if self.at.ns != 4:
            return
        h = self.rows // 2
        for k, b in ((0, 2), (1, 1)):
            self.leg(k).wait_recv()
            mine, came = pl.ds(b * self.rows + k * h, h), pl.ds(2 * self.rows + k * h, h)
            self.stage[mine, :] = (self.stage[mine, :].astype(F32) + self.inbox[came, :].astype(F32)).astype(BF16)
            self.leg(4 + k).start()

    def total(self, acc):
        four = self.at.ns == 4
        for k in range(2, 6) if four else range(1, self.at.ns):
            self.leg(k).wait_recv()
        for b in range(2 if four else self.at.ns - 1):
            acc = acc + self.inbox[b * self.rows : (b + 1) * self.rows, :].astype(F32)
        return acc

    def drain(self):
        for k in range(6) if self.at.ns == 4 else range(1, self.at.ns):
            self.leg(k).wait_send()


class Gather:
    def __init__(self, at, src, dst, sems):
        self.at, self.src, self.dst = at, src, dst
        self.send, self.recv, self.fsend, self.frecv, self.rsend, self.local = sems
        self.rows = src.shape[0]
        nz = at.nz
        self.order = [1, nz - 1] + list(range(2, nz - 1))

    def piece(self, z):
        return self.dst.at[block_of(2 * z + self.at.core, self.rows)]

    def direct(self, j):
        at = self.at
        return remote(self.src, self.piece(at.zz), self.send.at[j], self.recv.at[j], at.z_device(at.z_index(j)))

    def near(self, j):
        at = self.at
        z = at.z_index(j)
        away = z - at.zz
        return ((z > 0) & (z < at.nz - 1)) | (away == 1) | (away == -1)

    def across(self, j):
        piece = self.src if j == 0 else self.piece(self.at.z_from(j))
        return remote(piece, self.piece(self.at.z_from(j)), self.fsend.at[j], self.frecv.at[j], self.at.sib)

    def relay(self, j):
        nz = self.at.nz
        out = []
        for k, (here, end) in enumerate(((1, 0), (nz - 2, nz - 1))):
            origin = (here - j) % nz
            if origin != end:
                piece = self.piece(origin)
                index = (end - origin) % nz
                copy = remote(piece, piece, self.rsend.at[k, j], self.recv.at[index], self.at.z_device(end))
                out.append((self.at.zz == here, copy))
        return out

    def mine(self):
        return pltpu.make_async_copy(self.src, self.dst.at[block_of(self.at.d, self.rows)], self.local.at[0])

    def start(self):
        for j in self.order[2:] + self.order[:2]:
            pl.when(self.near(j))(self.direct(j).start)
        self.across(0).start()
        self.mine().start()

    def hop(self):
        at = self.at

        @pl.when((at.zz == 1) | (at.zz == at.nz - 2))
        def _():
            for j in self.order:
                self.direct(j).wait_recv()
                for here, copy in self.relay(j):
                    pl.when(here)(copy.start)
                self.across(j).start()

    def arrive(self):
        at = self.at

        @pl.when((at.zz != 1) & (at.zz != at.nz - 2))
        def _():
            for j in self.order:
                self.direct(j).wait_recv()
                self.across(j).start()

    def finish(self):
        for j in range(self.at.nz):
            self.across(j).wait_recv()
        self.mine().wait()

    def drain_own(self):
        self.across(0).wait_send()
        for j in range(1, self.at.nz):
            pl.when(self.near(j))(self.direct(j).wait_send)

    def drain_rest(self):
        for j in range(1, self.at.nz):
            self.across(j).wait_send()
            for here, copy in self.relay(j):
                pl.when(here)(copy.wait_send)

    def drain(self):
        self.drain_own()
        self.drain_rest()


def gather_sems(nz):
    return [DMA((nz,)), DMA((nz,)), DMA((nz,)), DMA((nz,)), DMA((2, nz)), DMA((1,))]


class Scatter:
    def __init__(self, at, pieces, inbox, final, out, sems):
        self.at, self.pieces, self.inbox, self.final, self.out = at, pieces, inbox, final, out
        self.send, self.recv, osend, orecv, self.local, self.rsend, self.rrecv = sems
        self.rows = final.shape[0]
        self.share = SeqGather(at, final, lambda r: out.at[r], (osend, orecv))

    def piece(self, z):
        return self.pieces.at[block_of(z, self.rows)]

    def copy(self, j):
        at = self.at
        z = at.z_index(j)
        return remote(self.piece(z), self.inbox.at[j - 1], self.send.at[j], self.recv.at[j], at.z_device(z))

    def far_copy(self, target, via):
        slot = self.inbox.at[self.at.nz - 1]
        return remote(self.piece(target), slot, self.rsend.at[0], self.rrecv.at[0], self.at.z_device(via))

    def far(self):
        nz = self.at.nz
        return ((0, nz - 1, 1, nz - 2), (nz - 1, 0, nz - 2, 2))

    def near(self, away):
        return (away < self.at.nz - 1) & (away > 1 - self.at.nz)

    def free(self, j):
        go = self.near(self.at.z_index(j) - self.at.zz)
        for _, _, via, k in self.far():
            if k == j:
                go = go & (self.at.zz != via)
        return go

    def start(self):
        at = self.at
        for origin, target, via, _ in self.far():
            pl.when(at.zz == origin)(self.far_copy(target, via).start)
        for j in range(1, at.nz):
            pl.when(self.free(j))(self.copy(j).start)
            away = at.z_from(j) - at.zz

            @pl.when((away >= at.nz - 1) | (away <= 1 - at.nz))
            def _():
                self.inbox[j - 1] = jnp.zeros_like(self.inbox[j - 1])

    def relay(self):
        at = self.at
        for _, target, via, j in self.far():

            @pl.when(at.zz == via)
            def _():
                self.far_copy(target, via).wait_recv()
                rows = block_of(target, self.rows)
                both = self.pieces[rows, :].astype(F32) + self.inbox[at.nz - 1].astype(F32)
                self.pieces[rows, :] = both.astype(BF16)
                self.copy(j).start()

    def keep(self):
        return pltpu.make_async_copy(self.final, self.out.at[self.at.s], self.local.at[0])

    def total(self):
        at = self.at
        for j in range(1, at.nz):
            pl.when(self.near(at.z_from(j) - at.zz))(self.copy(j).wait_recv)
        acc = self.pieces[block_of(self.at.zz, self.rows), :].astype(F32)
        for j in range(1, self.at.nz):
            acc = acc + self.inbox[j - 1].astype(F32)
        self.final[...] = acc.astype(BF16)
        self.keep().start()
        self.share.start()

    def drain(self):
        self.keep().wait()
        self.share.finish()
        self.share.drain()
        at = self.at
        for j in range(1, at.nz):
            pl.when(self.near(at.z_index(j) - at.zz))(self.copy(j).wait_send)
        for origin, target, via, _ in self.far():
            pl.when(at.zz == origin)(self.far_copy(target, via).wait_send)


def scatter_sems(ns, nz):
    return [DMA((nz,)), DMA((nz,))] + seq_sems(ns) + [DMA((1,)), DMA((1,)), DMA((1,))]


def block_kernel(
    ns, nd, x, gain1, gain2, gainqk, wqkv_rows, wout_mine, cot, wgate, wup, wdown, cos, sin,
    outputs, gstream, gateall, upall, dnall, qkvall, outall, small,
    normed, projT, qT, kT, krows, vrows, inv, mixT, mrowsT, wout, wqkv, gsum, osend, oown, gsecond,
    vT, resid, cotall, xall, gains, gbuf, wqkv_mine, gu, dn, hrow, hT, gb, gsend, grecv, gown, nmT,
    gur, uur, dnr,
    gaz, gaf, upz, upf, dnz, dnf, grows, qrows, gk, gv, gqT, qkr, qkown, qkz, qkf,
    gor, gostage, gorecv, goown, goz, gof, sm0, sm1, sm2, sm3,
    xs, xr, gs, gr, cs, cr, ms, mr, ns_, nr, ps, pr, ss, sr, loc, wl,
    os_, or_, bs, br, nis, nir, ss2, sr2, gos, gorc, s1, r1, s2, r2, wos, wor, wok, cs2, cr2, *sems,
):
    at = Place(ns, nd)
    s, d, nz, core = at.s, at.d, at.nz, at.core
    T, width = x.shape
    L = ns * T
    R = wqkv_mine.shape[0]
    cw = width // ns
    n = dn.shape[0]
    piece = n // nd
    gl, ql = gain1.shape[1], gainqk.shape[1]
    dn_mine = wdown.at[block_of(s, piece)] if wdown.shape[0] == ns * piece else wdown
    hq, hk = H // ns, KV // ns
    group = hq // hk
    qw, kw = hq * HD, hk * HD
    own = block_of(s, T)
    pw = qw + 2 * kw
    gains[...] = jnp.zeros_like(gains)
    gains[0:1, :gl] = gain1[...]
    gains[1:2, :gl] = gain2[...]
    gains[2:3, :ql] = gainqk[...]
    for i in range(ns):

        @pl.when(s == i)
        def _():
            cuts = ((i * qw, qw), (H * HD + i * kw, kw), ((H + KV) * HD + i * kw, kw))
            wqkv_mine[...] = jnp.concatenate([wqkv_rows[:, a : a + b] for a, b in cuts], axis=1)

    at.greet()

    share_x = SeqGather(at, x, lambda r: xall.at[block_of(r, T)], (xs, xr))
    g_copies = [remote(gains, gbuf.at[d], gs.at[j], gr.at[j], at.dp_to(j)) for j in range(1, nd)]
    hw = width // 2

    def share_half(i, sem):
        c = pl.ds(i * hw, hw)
        return SeqGather(at, cot.at[:, c], lambda r: cotall.at[block_of(r, T), c], sem)

    share_cot = [share_half(0, (cs, cr)), share_half(1, (cs2, cr2))]
    share_nm = SeqGather(at, xall.at[own], lambda r: xall.at[block_of(r, T)], (ns_, nr))
    take_qkv = Gather(at, wqkv_mine, wqkv, sems[0:6])
    wo, mycols = nmT.at[0], block_of(s, cw)

    def out_z(j):
        rows = wo.at[block_of(at.zz, R), mycols]
        return remote(wout_mine.at[:, mycols], rows, sems[6].at[j], sems[7].at[j], at.z_device(at.z_index(j)))

    out_local = pltpu.make_async_copy(wout_mine.at[:, mycols], wo.at[block_of(at.zz, R), mycols], sems[11].at[0])
    share_out = SeqGather(at, wo.at[:, mycols], lambda r: wo.at[:, block_of(r, cw)], (wos, wor))

    def out_across(z):
        rows = wout.at[block_of(2 * z + core, R)]
        return remote(wo.at[pl.ds(z * R, R)], rows, sems[8].at[z], sems[9].at[z], at.sib)

    def out_keep(z):
        return pltpu.make_async_copy(wo.at[pl.ds(z * R, R)], wout.at[block_of(2 * z + core, R)], wok.at[z])

    base = L // 2
    take_gate = Gather(at, gb.at[pl.ds(base, R), pl.ds(0, n)], gu.at[:, pl.ds(0, n)], sems[12:18])
    take_up = Gather(at, gb.at[pl.ds(base, R), pl.ds(n, n)], gu.at[:, pl.ds(n, n)], sems[59:65])
    take_dn = Gather(at, dn_mine, dn, sems[18:24])
    for c in g_copies:
        c.start()
    share_x.start()
    take_qkv.start()
    for j in range(1, nz):
        out_z(j).start()
    out_local.start()
    xall[own, :] = x[...]
    gbuf[d] = gains[...]
    cot_local = pltpu.make_async_copy(cot, cotall.at[own], loc.at[0])
    cot_local.start()
    ff = wgate.shape[1]
    parts = max(1, -(-ff // (2 * n)))
    while nd % parts:
        parts += 1
    span = ff // parts
    stage = []
    for i, w in enumerate((wgate, wup)):
        for k in range(parts):
            row = pl.ds((i * parts + k) * R, R)
            stage.append(
                pltpu.make_async_copy(w.at[:, pl.ds(k * span, span)], gb.at[row, pl.ds(0, span)], wl.at[i, k])
            )
    for c in stage:
        c.start()
    for c in stage:
        c.wait()
    real = wgate.shape[1] // nd // ns
    gap = [jnp.zeros((R, piece - real), BF16)] if piece > real else []
    for i in range(ns):

        @pl.when(s == i)
        def _():
            cuts = []
            for w in range(2):
                for k in range(nd):
                    a = (k * ns + i) * real
                    row = (w * parts + a // span) * R
                    cuts += [gb[row : row + R, a % span : a % span + real]] + gap
            gb[base : base + R, :] = jnp.concatenate(cuts, axis=1)


    for c in g_copies:
        c.wait_recv()
    gain_in = jnp.concatenate([gbuf[k][0:1, :gl] for k in range(nd)], axis=1)
    gain_mid = jnp.concatenate([gbuf[k][1:2, :gl] for k in range(nd)], axis=1)
    gain_qk = jnp.concatenate([gbuf[k][2:3, :ql] for k in range(nd)], axis=1)
    gsum[...] = jnp.zeros_like(gsum)
    gsum[0:1, :] = gain_in
    gsum[1:2, :] = gain_mid
    gsum[2:3, : 2 * HD] = gain_qk
    columns = jnp.transpose(jnp.broadcast_to(gain_qk, (8, 2 * HD)))
    gain_q, gain_k = columns[:HD, 0:1], columns[HD:, 0:1]
    take_qkv.hop()
    take_gate.start()
    take_up.start()
    take_dn.start()
    for j in range(ns):
        rows = block_of(at.gather_rank(j), T)
        if j == 1:
            share_x.hop()
        if j:
            share_x.wait(j)
        xc = xall[rows, :].astype(F32)
        scale = lax.rsqrt(jnp.mean(xc * xc, axis=-1, keepdims=True) + EPSILON)
        normed[rows, :] = (xc * scale * gain_in).astype(BF16)
    for j in range(1, nz):
        out_z(j).wait_recv()
    out_local.wait()
    share_out.start()
    take_qkv.arrive()
    take_qkv.finish()
    for j in range(ns):
        rows = pl.ds(j * T, T)
        proj = mm(normed[rows, :], wqkv[...])
        projT[:, rows] = jnp.transpose(proj[:, : qw + kw])
        val = proj[:, qw + kw :]
        vT[:, rows] = jnp.transpose(val).astype(BF16)
        for i in range(hk):
            vrows[i, rows, :] = val[:, i * HD : (i + 1) * HD].astype(BF16)

    half = HD // 2

    def rope(row, gain, factor):
        u = projT[row, :]
        scale = lax.rsqrt(jnp.mean(u * u, axis=0, keepdims=True) + EPSILON)
        u = u * scale * gain
        a, b = u[:half], u[half:]
        return jnp.concatenate([a * cos[...] - b * sin[...], b * cos[...] + a * sin[...]], axis=0) * factor

    def rope_query(h, carry):
        row = block_of(h, HD)
        qT[row, :] = rope(row, gain_q, HD**-0.5).astype(BF16)
        return carry

    lax.fori_loop(0, hq, rope_query, 0)
    for i in range(hk):
        r = rope(pl.ds(qw + i * HD, HD), gain_k, 1.0)
        kT[i * HD : (i + 1) * HD, :] = r.astype(BF16)
        krows[i, :, :] = jnp.transpose(r).astype(BF16)

    share_x.drain()
    share_out.hop()
    take_gate.hop()
    keep = lax.broadcasted_iota(jnp.int32, (T, T), 0) <= lax.broadcasted_iota(jnp.int32, (T, T), 1)
    block = block_of(s, qw)

    def mixed_out(rb):
        return remote(mixT.at[rb], mrowsT.at[block], ms.at[rb], mr.at[s], (d, rb))

    for rb in range(ns):
        cols = pl.ds(rb * T, T)
        span = rb * T

        def head(h, carry):
            kv = h // group
            row, vrow = block_of(h, HD), block_of(kv, HD)
            q = qT[row, cols]
            p = jnp.where(keep, jnp.exp(mm(krows[kv, cols, :], q)), 0.0)
            tot = jnp.sum(p, axis=0, keepdims=True)
            m = mm(vT[vrow, cols], p.astype(BF16))
            if span:
                p = jnp.exp(mm(krows[kv, 0:span, :], q))
                tot = tot + jnp.sum(p, axis=0, keepdims=True)
                m = m + mm(vT[vrow, 0:span], p.astype(BF16))
            one = 1.0 / tot
            inv[h, :, cols] = one
            mixT[rb, row, :] = (m * one).astype(BF16)
            return carry

        lax.fori_loop(0, hq, head, 0)
        pl.when(s != rb)(mixed_out(rb).start)
        if rb == ns - 1:
            share_out.finish()
            for z in range(nz):
                out_across(z).start()
                out_keep(z).start()

    share_cot[0].start()
    mrowsT[block, :] = mixT[s]
    for j in range(1, ns):
        src = at.seq_from(j)
        remote(mixT.at[0], mrowsT.at[block_of(src, qw)], ms.at[0], mr.at[src], (d, src)).wait_recv()
    for z in range(nz):
        out_across(z).wait_recv()
        out_keep(z).wait()
    residual = x[...].astype(F32) + mm(jnp.transpose(mrowsT[...]), wout[...])
    resid[...] = residual
    scale_mid = lax.rsqrt(jnp.mean(residual * residual, axis=-1, keepdims=True) + EPSILON)
    xall[own, :] = (residual * scale_mid * gain_mid).astype(BF16)
    share_nm.start()
    take_up.hop()
    share_nm.hop()
    share_cot[0].hop()
    share_cot[1].start()
    take_dn.hop()
    take_gate.arrive()
    take_up.arrive()
    ft, nt, wt = n, 1, width

    take_gate.drain_own()
    take_up.drain_own()
    take_gate.finish()
    take_up.finish()
    for j in range(ns):
        if j == ns - 1:
            share_cot[1].hop()
        if j:
            share_nm.wait(j)
        rows = block_of(at.gather_rank(j), T)
        for i in range(2):
            f = pl.ds(i * n, n)
            gb[rows, f] = mm(xall[rows, :], gu[:, f]).astype(BF16)
    share_nm.drain()
    share_out.drain()
    for z in range(nz):
        out_across(z).wait_send()
    for k in range(nd):
        nmT[k % 2, (k // 2) * R : (k // 2 + 1) * R, :] = jnp.transpose(xall[:, k * R : (k + 1) * R])
    take_dn.arrive()
    take_dn.finish()
    share_cot[0].finish()
    share_cot[1].finish()
    cot_local.wait()
    sum_nm = SeqReduce(at, T, gsend, grecv, (ps, pr))
    for j in list(range(1, ns)) + [0]:
        if j == 0:
            sum_nm.hop()
        rows = block_of(at.reduce_rank(j), T)
        stage = pl.ds((j - 1) * T, T)

        def hidden_tile(i, carry):
            f, f2 = block_of(i, ft), block_of(i + nt, ft)
            gate, up = gb[rows, f].astype(F32), gb[rows, f2].astype(F32)
            sig = 1.0 / (1.0 + jnp.exp(-gate))
            act = gate * sig
            back = mm_nt(cotall[rows, :], dn[f, :])
            hid = act * up
            hrow[:, f] = hid.astype(BF16)
            hid = jnp.transpose(hid.astype(BF16))
            for k in range(nd):
                first = (k % 2) * nz * piece + (k // 2) * piece
                hT[first : first + piece, rows] = hid[k * piece : (k + 1) * piece]
            gb[rows, f] = (back * up * sig * (1.0 + gate * (1.0 - sig))).astype(BF16)
            gb[rows, f2] = (back * act).astype(BF16)
            return carry

        lax.fori_loop(0, nt, hidden_tile, 0)

        def back_tile(i, carry):
            w = block_of(i, wt)
            part = mm_nt(gb[rows, :], gu[w, :])
            if j:
                gsend[stage, w] = part.astype(BF16)
            else:
                gown[:, w] = part
            return carry

        lax.fori_loop(0, width // wt, back_tile, 0)
        if j:
            sum_nm.push(j)

        def out_tile(i, carry):
            w = block_of(i, wt)
            part = mm(hrow[...], dn[:, w])
            if j:
                osend[stage, w] = part.astype(BF16)
            else:
                oown[:, w] = part + resid[:, w]
            return carry

        lax.fori_loop(0, width // wt, out_tile, 0)

    share_cot[0].drain()
    share_cot[1].drain()
    take_gate.drain_rest()
    take_up.drain_rest()
    take_dn.drain()
    half_gu, half_dn = nz * R, nz * piece
    dns, dnown = dn.at[pl.ds(0, half_dn)], dn.at[pl.ds(half_dn, half_dn)]
    gus, gateown = (gu.at[pl.ds(i * half_gu, half_gu), pl.ds(0, n)] for i in range(2))
    uus, upown = (gu.at[pl.ds(i * half_gu, half_gu), pl.ds(n, n)] for i in range(2))
    dn_sum = Scatter(at, dnown, dnz, dnf, dnall, sems[24:31])
    gate_sum = Scatter(at, gateown, gaz, gaf, gateall, sems[31:38])
    up_sum = Scatter(at, upown, upz, upf, upall, sems[38:45])
    qkv_sum = Scatter(at, qkown, qkz, qkf, qkvall, sems[45:52])
    out_sum = Scatter(at, goown, goz, gof, outall, sems[52:59])

    def dn_part(c, i):
        return mm(hT[block_of(c, nz * piece), :], cotall[:, block_of(i, 512)])

    tiles = n // 384
    tw = n // tiles

    def other(buf, base):
        def tile(i, carry):
            f = block_of(i, tw)
            buf[:, f] = mm(nmT[1 - core], gb[:, pl.ds(pl.multiple_of(base + i * tw, 128), tw)]).astype(BF16)
            return carry

        lax.fori_loop(0, tiles, tile, 0)

    def summed(buf, got, base):
        def tile(i, carry):
            f = block_of(i, tw)
            part = mm(nmT[core], gb[:, pl.ds(pl.multiple_of(base + i * tw, 128), tw)])
            buf[:, f] = (part + got[:, f].astype(F32)).astype(BF16)
            return carry

        lax.fori_loop(0, tiles, tile, 0)

    dn_copy = remote(dns, dnr, ss.at[0], sr.at[0], at.sib)
    gate_copy = remote(gus, gur, ss.at[1], sr.at[1], at.sib)
    up_copy = remote(uus, uur, ss.at[2], sr.at[2], at.sib)

    def dn_other(i, carry):
        dns[:, block_of(i, 512)] = dn_part(1 - core, i).astype(BF16)
        return carry

    def dn_mine(i, carry):
        dnown[:, block_of(i, 512)] = dn_part(core, i).astype(BF16)
        return carry

    lax.fori_loop(0, width // 512, dn_other, 0)
    dn_copy.start()
    lax.fori_loop(0, width // 512, dn_mine, 0)
    dn_copy.wait_recv()
    dnown[...] = (dnown[...].astype(F32) + dnr[...].astype(F32)).astype(BF16)
    dn_sum.start()
    other(gus, 0)
    gate_copy.start()
    gnm = sum_nm.total(gown[...])
    sum_nm.drain()
    residual = resid[...]
    scale_mid = lax.rsqrt(jnp.mean(residual * residual, axis=-1, keepdims=True) + EPSILON)
    gsecond[...] = jnp.broadcast_to(jnp.sum(gnm * residual * scale_mid, axis=0, keepdims=True), (8, width))
    weighted = gnm * gain_mid
    gown[...] = (
        cotall[own, :].astype(F32)
        + scale_mid * weighted
        - residual * (scale_mid * scale_mid * scale_mid) * jnp.mean(weighted * residual, axis=-1, keepdims=True)
    )
    rback = gown[...].astype(BF16)

    def mixed_back(p):
        return remote(gsend.at[pl.ds(0, T), pl.ds(p * qw, qw)], grows.at[own], bs.at[p], br.at[s], (d, p))

    for p in range(ns):
        gsend[0:T, p * qw : (p + 1) * qw] = mm_nt(rback, wout[p * qw : (p + 1) * qw, :]).astype(BF16)
        pl.when(s != p)(mixed_back(p).start)
    grows[own, :] = gsend[0:T, block_of(s, qw)]

    sum_outputs = SeqReduce(at, T, osend, xall, (os_, or_))
    for j in range(1, ns):
        sum_outputs.push(j)
    other(uus, n)
    up_copy.start()
    gate_copy.wait_recv()
    summed(gateown, gur, 0)
    gate_sum.start()
    up_copy.wait_recv()
    summed(upown, uur, n)
    up_sum.start()
    dn_sum.relay()
    for k in range(nd):
        nmT[k % 2, (k // 2) * R : (k // 2 + 1) * R, :] = mm(mrowsT[k * R : (k + 1) * R, :], rback).astype(BF16)
    go_copy = remote(nmT.at[1 - core], gor, ss2.at[0], sr2.at[0], at.sib)
    go_copy.start()
    for i in range(hk):
        qrows[i, :, :] = jnp.transpose(qT[i * group * HD : (i + 1) * group * HD, :])
    go_copy.wait_recv()
    gate_copy.wait_send()
    up_copy.wait_send()
    sum_gout = SeqReduce(at, nz * R, gostage, gorecv, (gos, gorc))

    def gout_columns(r):
        c = block_of(r, cw)
        return nmT[core, :, c].astype(F32) + gor[:, c].astype(F32)

    for j in range(1, ns):
        gostage[pl.ds((j - 1) * nz * R, nz * R), :] = gout_columns(at.reduce_rank(j)).astype(BF16)
    for j in range(1, ns):
        src = at.seq_from(j)
        remote(gsend.at[pl.ds(0, T), pl.ds(0, qw)], grows.at[block_of(src, T)], bs.at[0], br.at[src], (d, src)).wait_recv()
    for i in range(ns):
        rows = pl.ds(i * T, T)
        hT[pw : pw + qw, rows] = jnp.transpose(grows[rows, :])

    for j in range(1, ns):
        sum_gout.push(j)

    causal = lax.broadcasted_iota(jnp.int32, (T, T), 0) <= lax.broadcasted_iota(jnp.int32, (T, T), 1)
    causal = jnp.concatenate([causal] * group, axis=1)
    gk[...] = jnp.zeros_like(gk)
    gv[...] = jnp.zeros_like(gv)

    def key_head(kv, carry):
        krow = block_of(kv, HD)
        lanes = block_of(kv, group * HD)
        for rb in range(ns):
            cols = pl.ds(rb * T, T)

            def side(ref, base):
                return jnp.concatenate(
                    [ref[pl.ds(pl.multiple_of(base + (kv * group + u) * HD, HD), HD), cols] for u in range(group)],
                    axis=1,
                )

            q, g = side(qT, 0), side(hT, pw)
            one = jnp.concatenate([inv[kv * group + u, :, cols] for u in range(group)], axis=1)
            m = jnp.concatenate(
                [mixT[rb, block_of(kv * group + u, HD), :] for u in range(group)], axis=1
            )
            delta = jnp.sum(g.astype(F32) * m.astype(F32), axis=0, keepdims=True)
            gr, qr = grows[cols, lanes], qrows[kv, cols, :]
            gr = jnp.concatenate([gr[:, u * HD : (u + 1) * HD] for u in range(group)], axis=0)
            qr = jnp.concatenate([qr[:, u * HD : (u + 1) * HD] for u in range(group)], axis=0)
            gq = jnp.zeros((HD, group * T), F32)
            for part, masked in ((pl.ds(0, rb * T), False), (cols, True)):
                if rb == 0 and not masked:
                    continue
                p = jnp.exp(mm(krows[kv, part, :], q)) * one
                if masked:
                    p = jnp.where(causal, p, 0.0)
                gp = mm(vrows[kv, part, :], g)
                ds = (p * (gp - delta)).astype(BF16)
                gv[kv, part, :] += mm(p.astype(BF16), gr)
                gk[kv, part, :] += mm(ds, qr)
                gq = gq + mm(kT[krow, part], ds)
            gq = gq * HD**-0.5
            for u in range(group):
                gqT[block_of(kv * group + u, HD), cols] = gq[:, u * T : (u + 1) * T]
        return carry

    lax.fori_loop(0, hk, key_head, 0)

    sum_outputs.hop()
    columns = jnp.transpose(gsum[:, : 2 * HD])
    gain_q, gain_k = columns[:HD, 2:3], columns[HD:, 2:3]

    def norm_column(row, g, gain):
        a, b = g[:half], g[half:]
        g = jnp.concatenate([a * cos[...] + b * sin[...], b * cos[...] - a * sin[...]], axis=0)
        u = projT[row, :]
        scale = lax.rsqrt(jnp.mean(u * u, axis=0, keepdims=True) + EPSILON)
        us = u * scale
        weighted = g * gain
        inner = jnp.mean(weighted * us, axis=0, keepdims=True)
        hT[row, :] = (scale * (weighted - us * inner)).astype(BF16)
        return jnp.sum(g * us, axis=1, keepdims=True)

    def query_back(h, acc):
        row = block_of(h, HD)
        return acc + norm_column(row, gqT[row, :], gain_q)

    gain_grad_q = lax.fori_loop(0, hq, query_back, jnp.zeros((HD, 1), F32))
    gain_grad_k = jnp.zeros((HD, 1), F32)
    for i in range(hk):
        gain_grad_k = gain_grad_k + norm_column(pl.ds(qw + i * HD, HD), jnp.transpose(gk[i]), gain_k)
        hT[qw + kw + i * HD : qw + kw + (i + 1) * HD, :] = jnp.transpose(gv[i]).astype(BF16)

    sum_gout.hop()
    gate_sum.relay()

    sum_ni = SeqReduce(at, T, gsend, grecv, (nis, nir))
    for p in range(ns):
        pl.when(s != p)(mixed_back(p).wait_send)
    for i in range(ns):
        rows = pl.ds(i * T, T)
        cotall[rows, 0:pw] = jnp.transpose(hT[0:pw, rows])
    for j in list(range(1, ns)) + [0]:
        part = mm_nt(cotall[block_of(at.reduce_rank(j), T), 0:pw], wqkv[...])
        if j:
            gsend[pl.ds((j - 1) * T, T), :] = part.astype(BF16)
            sum_ni.push(j)
        else:
            resid[...] = part
    for k in range(nd):
        part = mm(hT[0:pw, :], normed[:, k * R : (k + 1) * R])
        gb[((k % 2) * nz + k // 2) * R : ((k % 2) * nz + k // 2 + 1) * R, 0:pw] = jnp.transpose(part).astype(BF16)
    qk_copy = remote(gb.at[block_of(1 - core, nz * R), pl.ds(0, pw)], qkr, ss2.at[1], sr2.at[1], at.sib)
    qk_copy.start()
    sum_ni.hop()
    dn_sum.total()
    goown[...] = sum_gout.total(gout_columns(s)).astype(BF16)
    out_sum.start()
    qk_copy.wait_recv()
    qkown[...] = (gb[block_of(core, nz * R), pl.ds(0, pw)].astype(F32) + qkr[...].astype(F32)).astype(BF16)
    qkv_sum.start()
    up_sum.relay()
    out_sum.relay()
    gate_sum.total()
    qkv_sum.relay()

    gni = sum_ni.total(resid[...])
    dn_sum.share.hop()
    stream = x[...].astype(F32)
    scale = lax.rsqrt(jnp.mean(stream * stream, axis=-1, keepdims=True) + EPSILON)
    unit = stream * scale
    weighted = gni * gsum[0:1, :]
    gown[...] = gown[...] + scale * (weighted - unit * jnp.mean(weighted * unit, axis=-1, keepdims=True))
    stream_store = pltpu.make_async_copy(gown, gstream, loc.at[2])
    stream_store.start()
    first = jnp.sum(gni * unit, axis=0, keepdims=True)
    qk = jnp.broadcast_to(jnp.concatenate([gain_grad_q, gain_grad_k], axis=0), (2 * HD, 128))
    sm0[0:1, :] = first
    sm0[1:2, :] = gsecond[0:1, :]
    sm0[2:8, :] = jnp.zeros((6, width), F32)
    sm0[2:3, : 2 * HD] = jnp.transpose(qk)[0:1, :]

    def small_seq(j):
        return remote(sm0, sm1.at[j - 1], s1.at[j], r1.at[j], at.seq_to(j))

    def small_dp(j):
        return remote(sm2.at[at.dp_to(j)[0]], sm3.at[j - 1], s2.at[j], r2.at[j], at.dp_to(j))

    for j in range(1, ns):
        small_seq(j).start()
    gate_sum.share.hop()
    up_sum.total()
    acc = sum_outputs.total(oown[...])
    last = pl.ds((ns - 1) * T, T)
    xall[last, :] = acc.astype(BF16)
    out_store = pltpu.make_async_copy(xall.at[last], outputs, loc.at[1])
    out_store.start()
    for j in range(1, ns):
        small_seq(j).wait_recv()
    acc = sm0[...]
    for j in range(1, ns):
        acc = acc + sm1[j - 1]
    sm2[...] = jnp.zeros_like(sm2)
    for k in range(nd):
        sm2[k, 0:2, :gl] = acc[0:2, k * gl : (k + 1) * gl]
        sm2[k, 2:3, :ql] = acc[2:3, k * ql : (k + 1) * ql]
    for j in range(1, nd):
        small_dp(j).start()
    out_sum.total()
    qkv_sum.total()
    up_sum.share.hop()
    out_sum.share.hop()
    qkv_sum.share.hop()
    for j in range(1, nd):
        small_dp(j).wait_recv()
    acc = sm2[d]
    for j in range(1, nd):
        acc = acc + sm3[j - 1]
    small[...] = acc

    go_copy.wait_send()
    qk_copy.wait_send()
    for j in range(1, ns):
        small_seq(j).wait_send()
    for j in range(1, nd):
        small_dp(j).wait_send()
    for rb in range(ns):
        pl.when(s != rb)(mixed_out(rb).wait_send)
    for t in (sum_outputs, sum_ni, sum_gout):
        t.drain()
    for c in g_copies + [dn_copy]:
        c.wait_send()
    take_qkv.drain()
    for j in range(1, nz):
        out_z(j).wait_send()
    for t in (dn_sum, out_sum, qkv_sum, gate_sum, up_sum):
        t.drain()
    out_store.wait()
    stream_store.wait()


def vmem(n):
    return [pl.BlockSpec(memory_space=pltpu.VMEM)] * n


def block(ns, nd, piece, x, gain1, gain2, gainqk, w_qkv, w_out, cot, w_gate, w_up, w_down):
    T, width = x.shape
    L = ns * T
    R = w_qkv.shape[0]
    n = nd * piece
    n2 = 2 * n
    nz = nd // 2
    hq, hk = H // ns, KV // ns
    qw, kw = hq * HD, hk * HD
    pw = qw + 2 * kw
    cw = width // ns
    cos, sin = rope_columns(L)
    sh, vm = jax.ShapeDtypeStruct, pltpu.VMEM
    outs = (
        sh((T, width), BF16), sh((T, width), F32), sh((ns, R, n), BF16), sh((ns, R, n), BF16),
        sh((ns, piece, width), BF16), sh((ns, R, pw), BF16), sh((ns, R, cw), BF16), sh((8, 128), F32),
    )
    hbm = pl.BlockSpec(memory_space=pl.ANY)
    scratch = [
        vm((L, width), BF16), vm((qw + kw, L), F32), vm((qw, L), BF16), vm((kw, L), BF16),
        vm((hk, L, HD), BF16), vm((hk, L, HD), BF16), vm((hq, 1, L), F32), vm((ns, qw, T), BF16),
        vm((H * HD, T), BF16), vm((H * HD, width), BF16), vm((width, pw), BF16), vm((8, width), F32),
        vm(((ns - 1) * T, width), BF16), vm((T, width), F32), vm((8, width), F32),
        vm((kw, L), BF16), vm((T, width), F32), vm((L, width), BF16), vm((L, width), BF16), vm((8, 128), F32),
        vm((nd, 8, 128), F32), vm((R, pw), BF16), vm((nd * R, n2), BF16), vm((n, width), BF16),
        vm((T, n), BF16), vm((n, L), BF16), vm((L, n2), BF16), vm(((ns - 1) * T, width), BF16),
        vm(((ns - 1) * T, width), BF16), vm((T, width), F32), vm((2, nz * R, L), BF16),
        vm((nz * R, n), BF16), vm((nz * R, n), BF16), vm((nz * piece, width), BF16),
        vm((nz, R, n), BF16), vm((R, n), BF16), vm((nz, R, n), BF16), vm((R, n), BF16),
        vm((nz, piece, width), BF16), vm((piece, width), BF16), vm((L, qw), BF16),
        vm((hk, L, qw // hk), BF16), vm((hk, L, HD), F32), vm((hk, L, HD), F32), vm((qw, L), F32),
        vm((nz * R, pw), BF16), vm((nz * R, pw), BF16), vm((nz, R, pw), BF16), vm((R, pw), BF16),
        vm((nz * R, width), BF16), vm(((ns - 1) * nz * R, cw), BF16), vm(((ns - 1) * nz * R, cw), BF16), vm((nz * R, cw), BF16),
        vm((nz, R, cw), BF16), vm((R, cw), BF16),
        vm((8, width), F32), vm((ns - 1, 8, width), F32), vm((nd, 8, 128), F32), vm((nd - 1, 8, 128), F32),
    ]
    sems = seq_sems(ns) + [DMA((nd,)), DMA((nd,))] + seq_sems(ns) + [DMA((ns,))] * 2 + seq_sems(ns) * 2
    sems += [DMA((3,)), DMA((3,))]
    sems += [DMA((3,)), DMA((2, 8))]
    sems += seq_sems(ns) + [DMA((ns,))] * 2 + seq_sems(ns) + [DMA((2,)), DMA((2,))] + seq_sems(ns) + [DMA((ns,))] * 2 + [DMA((nd,)), DMA((nd,))]
    sems += seq_sems(ns) + [DMA((nz,))] + seq_sems(ns)
    return pl.pallas_call(
        functools.partial(block_kernel, ns, nd),
        out_shape=outs,
        in_specs=vmem(5) + [hbm] * 5 + vmem(2),
        out_specs=[hbm] * 7 + vmem(1),
        scratch_shapes=scratch + sems + gather_sems(nz) * 4 + scatter_sems(ns, nz) * 5 + gather_sems(nz),
        compiler_params=pltpu.CompilerParams(
            collective_id=0, has_side_effects=True, vmem_limit_bytes=VMEM_LIMIT
        ),
        cost_estimate=pl.CostEstimate(flops=38_000_000_000, bytes_accessed=40_000_000, transcendentals=12_000_000),
    )(x, gain1, gain2, gainqk, w_qkv, w_out, cot, w_gate, w_up, w_down, cos, sin)


def finish_kernel(
    ns, nd, piece, gateall, upall, qkvall, outall, dnall, got, stream, sums,
    gate, up, qkv, out, down, outputs, gstream, first, second, qk,
):
    outputs[...] = got[...]
    gstream[...] = stream[...]
    for i, ref in enumerate((first, second, qk)):
        ref[...] = sums[i : i + 1, : ref.shape[1]]
    hq, hk = H // ns, KV // ns
    qw, kw = hq * HD, hk * HD
    pad = gateall.shape[2] // nd
    for ref, got in ((gate, gateall), (up, upall)):
        parts = [got[i].astype(F32) for i in range(ns)]
        ref[...] = jnp.concatenate(
            [parts[i][:, k * pad : k * pad + piece] for k in range(nd) for i in range(ns)], axis=1
        )
    parts = [qkvall[i].astype(F32) for i in range(ns)]
    qkv[...] = jnp.concatenate(
        [p[:, :qw] for p in parts] + [p[:, qw : qw + kw] for p in parts] + [p[:, qw + kw :] for p in parts], axis=1
    )
    out[...] = jnp.concatenate([outall[i].astype(F32) for i in range(ns)], axis=1)
    down[...] = jnp.concatenate([dnall[i].astype(F32)[:piece] for i in range(dnall.shape[0])], axis=0)


def finish(ns, nd, piece, gateall, upall, qkvall, outall, dnall, got, stream, sums):
    R = gateall.shape[1]
    T, width = got.shape
    steps = 4
    rows = R // steps
    ff = ns * nd * piece
    widths = (ff, ff, ns * qkvall.shape[2], ns * outall.shape[2])
    many = ns // steps
    lines = (R, R, 2 * HD // nd)
    ins = [pl.BlockSpec((ns, rows, a.shape[2]), lambda i: (0, i, 0)) for a in (gateall, upall, qkvall, outall)]
    ins.append(pl.BlockSpec((many,) + dnall.shape[1:], lambda i: (i, 0, 0)))
    tokens = pl.BlockSpec((T // steps, width), lambda i: (i, 0))
    ins += [tokens, tokens, pl.BlockSpec((8, 128), lambda i: (0, 0))]
    outs = [pl.BlockSpec((rows, w), lambda i: (i, 0)) for w in widths]
    outs += [pl.BlockSpec((many * piece, width), lambda i: (i, 0)), tokens, tokens]
    outs += [pl.BlockSpec((1, w), lambda i: (0, 0)) for w in lines]
    sh = jax.ShapeDtypeStruct
    return pl.pallas_call(
        functools.partial(finish_kernel, ns, nd, piece),
        grid=(steps,),
        out_shape=[sh((R, w), F32) for w in widths]
        + [sh((ns * piece, width), F32), sh((T, width), BF16), sh((T, width), F32)]
        + [sh((1, w), F32) for w in lines],
        in_specs=ins,
        out_specs=outs,
        compiler_params=pltpu.CompilerParams(vmem_limit_bytes=60 << 20),
    )(gateall, upall, qkvall, outall, dnall, got, stream, sums)


def shards(inputs, cotangent, first_gain, w_qkv, qk_gain, w_out, second_gain, w_gate, w_up, w_down):
    ns, nd = lax.axis_size("seq"), lax.axis_size("dp")
    s, d = lax.axis_index("seq"), lax.axis_index("dp")
    piece = w_down.shape[0] // ns
    pad = -piece % 16
    down_rows = w_down
    if pad:
        down_rows = jnp.pad(lax.dynamic_slice_in_dim(w_down, s * piece, piece, 0), ((0, pad), (0, 0)))
    x = inputs[0]
    outputs, gstream, gateall, upall, dnall, qkvall, outall, small = block(
        ns, nd, piece + pad, x, first_gain[None], second_gain[None], qk_gain[None], w_qkv, w_out, cotangent[0],
        w_gate, w_up, down_rows,
    )
    gate, up, qkv, out, down, outputs, gstream, first, second, qk = finish(
        ns, nd, piece, gateall, upall, qkvall, outall, dnall, outputs, gstream, small
    )
    return (outputs[None], gstream[None], first[0], qkv, qk[0], out, second[0], gate, up, down)


def solution(mesh):
    act = P("dp", "seq", None)
    vec, mat = P("dp"), P("dp", None)
    in_specs = (act, act, vec, mat, vec, mat, vec, mat, mat, mat)
    out_specs = (act, act, vec, mat, vec, mat, vec, mat, mat, mat)
    return jax.shard_map(shards, mesh=mesh, in_specs=in_specs, out_specs=out_specs, check_vma=False)
```
